32 devices in a mesh: dp: 4 (over y, x), tp: 8 (over z, core).
Axes of the slice: x: 2, y: 2, z: 4, core: 2. Of those that a mesh axis runs over, the one named last changes fastest.
Arguments:
- tokens: bfloat16 [8, 2048, 2048], P('dp', 'tp'), may hold values from -6 to 6
- segments: int32 [8, 2048], P('dp'), may hold values from 0 to 3, as said below
- first_gain: float32 [2048], replicated, may hold values from 0.5 to 1.5
- first_shift: float32 [2048], replicated, may hold values from -1.25 to 1.25
- in_weight: bfloat16 [2048, 3, 2048], P('dp', None, 'tp'), may hold values from -0.125 to 0.125
- in_bias: float32 [2, 2048], P(None, 'tp'), may hold values from -1.75 to 1.75
- out_weight: bfloat16 [2048, 2048], P('tp', 'dp'), may hold values from -0.5 to 0.5
- out_bias: float32 [2048], replicated, may hold values from -1.25 to 1.25
- second_gain: float32 [2048], replicated, may hold values from 0.5 to 1.5
- second_shift: float32 [2048], replicated, may hold values from -1.25 to 1.25
- up_weight: bfloat16 [2048, 8192], P('dp', 'tp'), may hold values from -0.125 to 0.125
- up_bias: float32 [8192], P('tp'), may hold values from -1.75 to 1.75
- down_weight: bfloat16 [8192, 2048], P('tp', 'dp'), may hold values from -0.0625 to 0.0625
- down_bias: float32 [2048], replicated, may hold values from -1.25 to 1.25
- cotangent: bfloat16 [8, 2048, 2048], P('dp', 'tp'), may hold values from -8 to 8
Outputs:
- mixed: bfloat16 [8, 2048, 2048], P('dp', 'tp')
- tokens_grad: bfloat16 [8, 2048, 2048], P('dp', 'tp')
- first_gain_grad: float32 [2048], replicated
- first_shift_grad: float32 [2048], replicated
- in_weight_grad: float32 [2048, 3, 2048], P('dp', None, 'tp')
- in_bias_grad: float32 [2, 2048], P(None, 'tp')
- out_weight_grad: float32 [2048, 2048], P('tp', 'dp')
- out_bias_grad: float32 [2048], replicated
- second_gain_grad: float32 [2048], replicated
- second_shift_grad: float32 [2048], replicated
- up_weight_grad: float32 [2048, 8192], P('dp', 'tp')
- up_bias_grad: float32 [8192], P('tp')
- down_weight_grad: float32 [8192, 2048], P('tp', 'dp')
- down_bias_grad: float32 [2048], replicated
The draws below stay inside these ranges and needn't reach their ends.
Inputs may be any that keep to these rules, and one draw needn't show every extreme that they name: `segments`: within a row the numbers start at 0 and never fall. A row is either one sequence of 2048 positions (all 0) or four sequences of 512 positions (0 to 3). Among the 2 rows of one index of dp exactly one is a single sequence.
All inputs are finite; a program needn't handle non-finite values.
Results may differ from the reference program's by a relative error of at most 0.02.
Values may be sent and summed in bfloat16 or wider, within the bound.
A program may use at most 256 MiB of HBM per device.

```python
import jax
import jax.numpy as jnp
from jax import lax

D = 2048
HEADS = 16
HDIM = 128
FF = 8192
SEQ = 2048
MB = 2
ROWS = 8


def draw_segments(key, part):
    key = jax.random.fold_in(key, 11)
    chosen = jax.random.randint(key, (ROWS // MB,), 0, MB)
    row_index = jnp.arange(ROWS)
    whole = row_index % MB == jnp.repeat(chosen, MB)
    quarter = (jnp.arange(SEQ) // (SEQ // 4)).astype(jnp.int32)
    return jnp.where(whole[:, None], 0, quarter[None, :]).astype(jnp.int32)


def with_spikes(values, stream_key, source, target, blocks, factor):
    owner, partner = [(jnp.arange(values.shape[position]) // (values.shape[position] // blocks)).reshape([-1 if axis == position else 1 for axis in range(values.ndim)]) for position in (source, target)]
    chosen = jax.random.permutation(stream_key, blocks)[partner]
    strong = (owner == chosen) | (owner == (partner + blocks // 2) % blocks)
    return jnp.where(strong, factor * values, values)


def shard_levels(stream_key, shape, cuts, low, largest):
    level, own = 1.0, jax.random.fold_in(stream_key, 6)
    for position, shards_of in cuts:
        heights = jnp.exp(jax.random.uniform(jax.random.fold_in(own, position), (shards_of,), jnp.float32, low / len(cuts), largest / len(cuts)))
        level = level * jnp.repeat(heights, shape[position] // shards_of).reshape([-1 if axis == position else 1 for axis in range(len(shape))])
    return level


def centred(own_key, dims, spread, limit, shards=(), held_as=jnp.bfloat16):
    values = spread * jax.random.normal(own_key, dims, jnp.float32)
    if shards:
        values = values * shard_levels(own_key, dims, shards, -0.22, 0.18)
    return jnp.clip(values, -limit, limit).astype(held_as)


def gaussian_with(own_key, extent, width, reach, pieces, heavy, held_as=jnp.bfloat16):
    values = width * jax.random.normal(own_key, extent, jnp.float32)
    if pieces:
        values = values * shard_levels(own_key, extent, pieces, -0.22, 0.18)
    return jnp.clip(with_spikes(values, jax.random.fold_in(own_key, 3), *heavy), -reach, reach).astype(held_as)


def setup_inputs(seed: int = 0) -> dict:
    key_of = jax.random.split(jax.random.key(seed), 16)
    tokens = centred(key_of[0], (ROWS, SEQ, D), 1.0, 6.0, ((0, 4), (1, 8)))
    segments = draw_segments(jax.random.fold_in(key_of[15], 71), 0)
    first_gain = jnp.clip(1.0 + 0.1 * jax.random.normal(key_of[2], (D,), jnp.float32), 0.5, 1.5)
    first_shift = centred(key_of[3], (D,), 0.2, 1.25, (), jnp.float32)
    in_weight = centred(key_of[4], (D, 3, D), D ** -0.5, 0.125, ((0, 4), (2, 8)))
    in_bias = centred(key_of[5], (2, D), 0.3, 1.75, ((1, 8),), jnp.float32)
    out_weight = centred(key_of[6], (D, D), (D // 16) ** -0.5, 0.5, ((0, 8), (1, 4)))
    out_bias = centred(key_of[7], (D,), 0.2, 1.25, (), jnp.float32)
    second_gain = jnp.clip(1.0 + 0.1 * jax.random.normal(key_of[8], (D,), jnp.float32), 0.5, 1.5)
    second_shift = centred(key_of[9], (D,), 0.2, 1.25, (), jnp.float32)
    up_weight = centred(key_of[10], (D, FF), D ** -0.5, 0.125, ((0, 4), (1, 8)))
    up_bias = centred(key_of[11], (FF,), 0.3, 1.75, ((0, 8),), jnp.float32)
    down_weight = centred(key_of[12], (FF, D), FF ** -0.5, 0.0625, ((0, 8), (1, 4)))
    down_bias = centred(key_of[13], (D,), 0.2, 1.25, (), jnp.float32)
    cotangent = gaussian_with(key_of[14], (ROWS, SEQ, D), 1.0, 8.0, ((0, 4), (1, 8)), (0, 2, 4, 2.0))
    return {"tokens": tokens, "segments": segments, "first_gain": first_gain, "first_shift": first_shift, "in_weight": in_weight, "in_bias": in_bias, "out_weight": out_weight, "out_bias": out_bias, "second_gain": second_gain, "second_shift": second_shift, "up_weight": up_weight, "up_bias": up_bias, "down_weight": down_weight, "down_bias": down_bias, "cotangent": cotangent}


@jax.custom_vjp
def low(v):
    return lax.optimization_barrier(v.astype(jnp.bfloat16)).astype(jnp.float32)

@jax.custom_vjp
def low_back(v):
    return v

def low_keep(v):
    return (low(v), None)

def low_pass(kept, grad):
    return (grad,)

def back_keep(v):
    return (v, None)

def back_low(kept, grad):
    return (low(grad),)
low.defvjp(low_keep, low_pass)
low_back.defvjp(back_keep, back_low)
HIGHEST = lax.Precision.HIGHEST
EPSILON = 1e-05
MASKED = -1e+30

def layer_norm(values, gain, shift):
    center = values - lax.optimization_barrier(jnp.mean(values, axis=-1, keepdims=True))
    inverse = lax.rsqrt(lax.optimization_barrier(jnp.mean(center * center, axis=-1, keepdims=True)) + EPSILON)
    return center * inverse * gain + shift

def to_heads(matrix):
    return matrix.reshape(SEQ, HEADS, HDIM).transpose(1, 0, 2)

def attend_block(query, keys, values, seg_query, seg_keys, offset):
    block = query.shape[1]
    scores = low_back(HDIM ** (-0.5) * jnp.einsum('hqd,hkd->hqk', query, keys, precision=HIGHEST))
    rows_at = offset + jnp.arange(block)
    cols_at = jnp.arange(keys.shape[1])
    allowed = (seg_query[:, None] == seg_keys[None, :]) & (cols_at[None, :] <= rows_at[:, None])
    scores = jnp.where(allowed[None], scores, MASKED)
    top = lax.optimization_barrier(jnp.max(scores, axis=-1, keepdims=True))
    expo = jnp.exp(scores - top)
    probs = expo / lax.optimization_barrier(jnp.sum(expo, axis=-1, keepdims=True))
    return jnp.einsum('hqk,hkd->hqd', low(probs), values, precision=HIGHEST)

def forward(rows, params, seg):
    first_gain, first_shift, in_weight, in_bias, out_weight, out_bias, second_gain, second_shift, up_weight, up_bias, down_weight, down_bias = params
    normed1 = low(layer_norm(rows, first_gain, first_shift))
    proj = jnp.dot(normed1, in_weight.reshape(D, 3 * D), precision=HIGHEST).reshape(SEQ, 3, D)
    query = to_heads(low(low_back(proj[:, 0] + in_bias[0])))
    keys = to_heads(low(low_back(proj[:, 1])))
    values = to_heads(low(low_back(proj[:, 2] + in_bias[1])))
    block = min(512, SEQ)
    count = SEQ // block
    query_blocks = query.reshape(HEADS, count, block, HDIM).transpose(1, 0, 2, 3)
    seg_blocks = seg.reshape(count, block)
    offsets = (jnp.arange(count) * block).astype(jnp.int32)
    checked = jax.checkpoint(attend_block)
    outputs = lax.map(lambda item: checked(item[0], keys, values, item[1], seg, item[2]), (query_blocks, seg_blocks, offsets))
    attended = low(low_back(outputs.transpose(0, 2, 1, 3).reshape(SEQ, D)))
    resid = rows + low_back(jnp.dot(attended, out_weight, precision=HIGHEST)) + out_bias
    normed2 = low(layer_norm(resid, second_gain, second_shift))
    upward = low_back(jnp.dot(normed2, up_weight, precision=HIGHEST) + up_bias)
    active = low(jax.nn.gelu(upward))
    return resid + low_back(jnp.dot(active, down_weight, precision=HIGHEST)) + down_bias

def reference(tokens, segments, first_gain, first_shift, in_weight, in_bias, out_weight, out_bias, second_gain, second_shift, up_weight, up_bias, down_weight, down_bias, cotangent):
    params = tuple((p.astype(jnp.float32) for p in (first_gain, first_shift, in_weight, in_bias, out_weight, out_bias, second_gain, second_shift, up_weight, up_bias, down_weight, down_bias)))

    def one_row(totals, item):
        rows, seg, cot = item
        result, pull = jax.vjp(lambda r, p: forward(r, p, seg), rows.astype(jnp.float32), params)
        grad_rows, grad_params = pull(cot.astype(jnp.float32))
        totals = jax.tree.map(lambda a, b: a + b, totals, grad_params)
        return (totals, (result.astype(jnp.bfloat16), grad_rows.astype(jnp.bfloat16)))
    zeros = jax.tree.map(jnp.zeros_like, params)
    totals, (mixed, tokens_grad) = lax.scan(one_row, zeros, (tokens, segments, cotangent))
    return (mixed, tokens_grad, totals[0], totals[1], totals[2], totals[3], totals[4], totals[5], totals[6], totals[7], totals[8], totals[9], totals[10], totals[11])
```

```python
import functools

import jax
import jax.numpy as jnp
from jax import lax
from jax.experimental import pallas as pl
from jax.experimental.pallas import tpu as pltpu
from jax.sharding import Mesh, PartitionSpec as P

HDIM = 128
EPSILON = 1e-05
MASKED = -1e30
LOG2E = 1.4426950408889634
F32 = jnp.float32
BF16 = jnp.bfloat16
VMEM_LIMIT = 48 * 1024 * 1024
DP = ("e", "b", "a")
TP = ("g", "h", "c")
SLOTS = (0, 2, 1, 3)


def dot(x, y, contract=((1,), (0,))):
    return lax.dot_general(x, y, (contract, ((), ())), preferred_element_type=F32)


def stats(rows):
    mean = jnp.mean(rows, axis=-1, keepdims=True)
    center = rows - mean
    inverse = lax.rsqrt(jnp.mean(center * center, axis=-1, keepdims=True) + EPSILON)
    return center * inverse, inverse


def norm_back(grad_normed, scaled, inverse, gain):
    weighted = grad_normed * gain
    return inverse * (
        weighted
        - jnp.mean(weighted, axis=-1, keepdims=True)
        - scaled * jnp.mean(weighted * scaled, axis=-1, keepdims=True)
    )


def flip(x, axis):
    return lax.ppermute(x, axis, [(0, 1), (1, 0)])


def after(x, *others):
    return lax.optimization_barrier((x,) + others)[0]


def gather4(own):
    core = flip(own, "c")
    far = flip(own, "h")
    return jnp.concatenate([own, far, core, flip(far, "c")], 0)


def scatter4(product):
    away = product(1).astype(BF16)
    kept = product(0) + flip(away, "c").astype(F32)
    local = kept.shape[0] // 2
    return kept[:local] + flip(kept[local:].astype(BF16), "h").astype(F32)


def turn(x, groups, by, axes=("e", "g")):
    extra, count = groups
    pairs = []
    for e in range(extra):
        for g in range(count):
            pairs.append((e * count + g, (e + by[0]) % extra * count + (g + by[1]) % count))
    return lax.ppermute(x, axes, pairs)


def square_gather(own):
    half = own.shape[0] // 2
    by_a = flip(own, "a")
    by_b = flip(own, "b")
    return own, by_a, by_b, flip(by_a[:half], "b"), flip(by_b[half:], "a")


def square_scatter(piece):
    diag = piece(1, 1)
    half = diag.shape[0] // 2
    first = flip(diag[:half], "a")
    second = flip(diag[half:], "b")
    to_a, to_b, own = piece(0, 1), piece(1, 0), piece(0, 0)
    a_top = flip(to_a[:half], "a")
    b_low = flip(to_b[half:], "b")
    a_low = flip((to_a[half:].astype(F32) + second.astype(F32)).astype(BF16), "a")
    b_top = flip((to_b[:half].astype(F32) + first.astype(F32)).astype(BF16), "b")
    top = own[:half].astype(F32) + a_top.astype(F32) + b_top.astype(F32)
    low = own[half:].astype(F32) + a_low.astype(F32) + b_low.astype(F32)
    return jnp.concatenate([top, low], 0)


def sum_axis(x, axis):
    if lax.axis_size(axis) == 1:
        return x
    if lax.axis_size(axis) == 2:
        return x + flip(x, axis)
    return jnp.sum(lax.all_gather(x, axis), 0)


def row_blocks(place, count, size):
    found = []
    for j in range(count):
        other = jnp.bitwise_xor(place, j)
        slot = (other >> 1) + 2 * (other & 1)
        found.append(pl.multiple_of(slot * size, size))
    return found


def causal(size):
    keys = lax.broadcasted_iota(jnp.int32, (size, size), 0)
    queries = lax.broadcasted_iota(jnp.int32, (size, size), 1)
    return keys <= queries


def first_key(block, size, segment):
    return 0 if segment is None else block * size // segment * segment


def forward_kernel(size, segment, scale, place, *refs):
    if segment is None:
        q_ref, k_ref, v_ref, kp_ref, vp_ref, out_ref, lse_ref, k_own, v_own = refs
    else:
        q_ref, k_ref, v_ref, out_ref, lse_ref, k_own, v_own = refs
        kp_ref = vp_ref = None
    length = q_ref.shape[0]
    count = length // size
    at = row_blocks(place[1], count, size)
    for j in range(count):
        k_own[j * size : (j + 1) * size] = k_ref[pl.ds(at[j], size), :]
        v_own[j * size : (j + 1) * size] = v_ref[pl.ds(at[j], size), :]

    def run(before):
        for i in range(count):
            q = q_ref[pl.ds(at[i], size), :]
            start, end = first_key(i, size, segment), i * size
            parts = [
                (kp_ref[n * length : (n + 1) * length], vp_ref[n * length : (n + 1) * length], None)
                for n in range(before)
            ]
            if end > start:
                parts.append((k_own[start:end], v_own[start:end], None))
            parts.append((k_own[end : end + size], v_own[end : end + size], causal(size)))
            scores = []
            for k, _, mask in parts:
                s = dot(k, q, ((1,), (1,)))
                scores.append(s if mask is None else jnp.where(mask, s, MASKED))
            top = functools.reduce(
                jnp.maximum, [jnp.max(s, axis=0, keepdims=True) for s in scores]
            )
            total = jnp.zeros((1, size), F32)
            out = jnp.zeros((HDIM, size), F32)
            for s, (_, v, _) in zip(scores, parts):
                p = jnp.exp2((s - top) * scale)
                total = total + jnp.sum(p, axis=0, keepdims=True)
                out = out + dot(v, p.astype(BF16), ((0,), (0,)))
            out_ref[pl.ds(at[i], size), :] = (out / total).T.astype(BF16)
            lse_ref[0, :, i * size : (i + 1) * size] = top * scale + jnp.log(total) * LOG2E

    if segment is not None:
        run(0)
    else:
        for n in range(kp_ref.shape[0] // length + 1):
            pl.when(place[0] == n)(functools.partial(run, n))


def backward_kernel(size, segment, scale, place, *refs):
    if segment is None:
        q_ref, k_ref, v_ref, out_ref, do_ref, lse_ref, kp_ref, vp_ref = refs[:8]
        dproj_ref, dp_ref, k_own, v_own, dk_own, dv_own, dk_pre, dv_pre = refs[8:]
    else:
        q_ref, k_ref, v_ref, out_ref, do_ref, lse_ref = refs[:6]
        dproj_ref, k_own, v_own, dk_own, dv_own = refs[6:]
        kp_ref = vp_ref = None
    length = q_ref.shape[0]
    count = length // size
    head = pl.program_id(0)
    width = pl.num_programs(0) * HDIM
    factor = HDIM**-0.5
    at = row_blocks(place[1], count, size)
    column = [pl.multiple_of(n * width + head * HDIM, HDIM) for n in range(3)]
    for j in range(count):
        k_own[j * size : (j + 1) * size] = k_ref[pl.ds(at[j], size), :]
        v_own[j * size : (j + 1) * size] = v_ref[pl.ds(at[j], size), :]
    dk_own[...] = jnp.zeros_like(dk_own)
    dv_own[...] = jnp.zeros_like(dv_own)
    if segment is None:
        dk_pre[...] = jnp.zeros_like(dk_pre)
        dv_pre[...] = jnp.zeros_like(dv_pre)

    def run(before):
        for i in range(count):
            q = q_ref[pl.ds(at[i], size), :]
            do = do_ref[pl.ds(at[i], size), :]
            product = do.astype(F32) * out_ref[pl.ds(at[i], size), :].astype(F32)
            delta = lax.dot_general(
                jnp.ones((8, HDIM), F32),
                product,
                (((1,), (1,)), ((), ())),
                precision=lax.Precision.HIGHEST,
                preferred_element_type=F32,
            )[:1]
            lse = lse_ref[0, :, i * size : (i + 1) * size]
            start, end = first_key(i, size, segment), i * size
            parts = [
                (kp_ref, vp_ref, dk_pre, dv_pre, n * length, (n + 1) * length, None)
                for n in range(before)
            ]
            if end > start:
                parts.append((k_own, v_own, dk_own, dv_own, start, end, None))
            parts.append((k_own, v_own, dk_own, dv_own, end, end + size, causal(size)))
            dq = jnp.zeros((HDIM, size), F32)
            for k_at, v_at, dk, dv, low, high, mask in parts:
                k, v = k_at[low:high], v_at[low:high]
                s = dot(k, q, ((1,), (1,))) * scale - lse
                p = jnp.exp2(s if mask is None else jnp.where(mask, s, MASKED))
                dscores = (p * (dot(v, do, ((1,), (1,))) - delta)).astype(BF16)
                dv[low:high] += dot(p.astype(BF16), do)
                dk[low:high] += dot(dscores, q)
                dq = dq + dot(k, dscores, ((0,), (0,)))
            dproj_ref[pl.ds(at[i], size), pl.ds(column[0], HDIM)] = (dq * factor).T.astype(BF16)

    if segment is not None:
        run(0)
    else:
        for n in range(kp_ref.shape[0] // length + 1):
            pl.when(place[0] == n)(functools.partial(run, n))
        dp_ref[:, pl.ds(column[0], HDIM)] = (dk_pre[...] * factor).astype(BF16)
        dp_ref[:, pl.ds(column[1], HDIM)] = dv_pre[...].astype(BF16)
    for j in range(count):
        rows = slice(j * size, (j + 1) * size)
        dproj_ref[pl.ds(at[j], size), pl.ds(column[1], HDIM)] = (dk_own[rows] * factor).astype(BF16)
        dproj_ref[pl.ds(at[j], size), pl.ds(column[2], HDIM)] = dv_own[rows].astype(BF16)


def head_spec(length, first):
    return pl.BlockSpec((length, HDIM), lambda h: (0, first + h))


def attention_cost(length, heads, prefix, matmuls):
    pairs = heads * length * (prefix + length // 2)
    return pl.CostEstimate(
        flops=2 * matmuls * pairs * HDIM * 2, bytes_accessed=length * heads * 2048, transcendentals=pairs
    )


def attend(place, proj, size, segment=None, prefix=None):
    length = proj.shape[0]
    heads = proj.shape[1] // (3 * HDIM)
    scale = HDIM**-0.5 * LOG2E
    operands = [place, proj, proj, proj]
    specs = [pl.BlockSpec(memory_space=pltpu.SMEM)] + [head_spec(length, n * heads) for n in range(3)]
    if segment is None:
        operands += [prefix, prefix]
        specs += [head_spec(prefix.shape[0], n * heads) for n in range(2)]
    return pl.pallas_call(
        functools.partial(forward_kernel, size, segment, scale),
        grid=(heads,),
        in_specs=specs,
        out_specs=[head_spec(length, 0), pl.BlockSpec((1, 1, length), lambda h: (h, 0, 0))],
        out_shape=[
            jax.ShapeDtypeStruct((length, heads * HDIM), BF16),
            jax.ShapeDtypeStruct((heads, 1, length), F32),
        ],
        scratch_shapes=[pltpu.VMEM((length, HDIM), BF16)] * 2,
        compiler_params=pltpu.CompilerParams(vmem_limit_bytes=VMEM_LIMIT),
        cost_estimate=attention_cost(length, heads, 0 if prefix is None else prefix.shape[0], 2),
    )(*operands)


def attend_back(place, proj, out, grad_out, lse, size, segment=None, prefix=None):
    length = proj.shape[0]
    heads = proj.shape[1] // (3 * HDIM)
    scale = HDIM**-0.5 * LOG2E
    operands = [place, proj, proj, proj, out, grad_out, lse]
    specs = [pl.BlockSpec(memory_space=pltpu.SMEM)] + [head_spec(length, n * heads) for n in range(3)]
    specs += [head_spec(length, 0)] * 2 + [pl.BlockSpec((1, 1, length), lambda h: (h, 0, 0))]
    out_specs = [pl.BlockSpec(proj.shape, lambda h: (0, 0))]
    out_shape = [jax.ShapeDtypeStruct(proj.shape, BF16)]
    scratch = [pltpu.VMEM((length, HDIM), BF16)] * 2 + [pltpu.VMEM((length, HDIM), F32)] * 2
    if segment is None:
        operands += [prefix, prefix]
        specs += [head_spec(prefix.shape[0], n * heads) for n in range(2)]
        out_specs.append(pl.BlockSpec(prefix.shape, lambda h: (0, 0)))
        out_shape.append(jax.ShapeDtypeStruct(prefix.shape, BF16))
        scratch += [pltpu.VMEM((prefix.shape[0], HDIM), F32)] * 2
    return pl.pallas_call(
        functools.partial(backward_kernel, size, segment, scale),
        grid=(heads,),
        in_specs=specs,
        out_specs=out_specs,
        out_shape=out_shape,
        scratch_shapes=scratch,
        compiler_params=pltpu.CompilerParams(vmem_limit_bytes=VMEM_LIMIT),
        cost_estimate=attention_cost(length, heads, 0 if prefix is None else prefix.shape[0], 5),
    )(*operands)


def local(
    tokens,
    segments,
    first_gain,
    first_shift,
    in_weight,
    in_bias,
    out_weight,
    out_bias,
    second_gain,
    second_shift,
    up_weight,
    up_bias,
    down_weight,
    down_bias,
    cotangent,
):
    extra, groups = lax.axis_size("e"), lax.axis_size("g")
    split = (extra, groups)
    size, width = tokens.shape[1:]
    cols, hidden, depth = in_weight.shape[2], up_weight.shape[1], in_weight.shape[0]
    quarter = segments.shape[1] // 4
    at_e, at_b, at_a, at_g = (lax.axis_index(n) for n in ("e", "b", "a", "g"))
    place = jnp.stack([at_g, 2 * lax.axis_index("h") + lax.axis_index("c")]).astype(jnp.int32)
    sources = [(e, g) for g in range(groups) for e in range(extra)]

    single = jnp.where(segments[0, -1] == 0, 0, 1)
    order = (single, 1 - single)

    def pick(x):
        return [lax.dynamic_index_in_dim(x, r, 0, keepdims=False) for r in order]

    def unpick(first, second):
        return jnp.where(single == 0, jnp.stack([first, second]), jnp.stack([second, first]))

    rows = [r.astype(F32) for r in pick(tokens)]
    cots = pick(cotangent)

    def dp_place(e_off, i, j):
        return ((at_e + e_off) % extra) * 4 + (at_b ^ i) * 2 + (at_a ^ j)

    def gather_weight(weight, full_shape, put, wait=()):
        half = weight.shape[0] // 2
        full = jnp.zeros(full_shape, BF16)
        held = after(weight, *wait) if wait else weight
        arrived = []
        for e_off, g_off in sources:
            piece = held if (e_off, g_off) == (0, 0) else turn(held, split, (e_off, g_off))
            own, by_a, by_b, top, low = square_gather(piece)
            arrived += [by_a, by_b]
            full = put(full, own, dp_place(-e_off, 0, 0), g_off, 0)
            full = put(full, by_a, dp_place(-e_off, 0, 1), g_off, 0)
            full = put(full, by_b, dp_place(-e_off, 1, 0), g_off, 0)
            full = put(full, top, dp_place(-e_off, 1, 1), g_off, 0)
            full = put(full, low, dp_place(-e_off, 1, 1), g_off, half)
        return full, arrived

    def put_in(full, piece, d, g, skip):
        for n in range(3):
            full = lax.dynamic_update_slice(
                full,
                piece[:, n * cols : (n + 1) * cols],
                (d * depth + skip, (n * groups + g) * cols),
            )
        return full

    def put_rows(full, piece, d, g, skip):
        return lax.dynamic_update_slice(full, piece, (d * depth + skip, g * hidden))

    def put_columns(full, piece, d, g, skip):
        return lax.dynamic_update_slice(
            full, piece, (g * (full.shape[0] // groups) + skip, d * depth)
        )

    in_all, came_in = gather_weight(
        in_weight.reshape(depth, 3 * cols), (width, 3 * groups * cols), put_in
    )
    out_all, came_out = gather_weight(out_weight, (groups * cols, width), put_columns, came_in[:2])
    up_all, came_up = gather_weight(up_weight, (width, groups * hidden), put_rows, came_in)
    down_all, _ = gather_weight(down_weight, (groups * hidden, width), put_columns, came_up[:2])
    kv_all = in_all[:, groups * cols :]

    biases = jnp.concatenate([in_bias.reshape(-1), up_bias])
    shares = [biases if g == 0 else turn(biases, split, (0, g)) for g in range(groups)]
    bias_q = jnp.concatenate([s[:cols] for s in shares])
    bias_v = jnp.concatenate([s[cols : 2 * cols] for s in shares])
    bias_k = jnp.zeros_like(bias_q)
    bias_up = jnp.concatenate([s[2 * cols :] for s in shares])
    bias_proj = jnp.concatenate([bias_q, bias_k, bias_v])
    bias_kv = jnp.concatenate([bias_k, bias_v])

    scaled1, inverse1, full1 = [], [], []
    for r in range(2):
        scaled, inverse = stats(rows[r])
        scaled1.append(scaled)
        inverse1.append(inverse)
        full1.append((scaled * first_gain + first_shift).astype(BF16))
    low1 = full1
    full1 = [gather4(x) for x in low1]
    prefix1 = [
        lax.ppermute(low1[0], "g", [(g, g + k) for g in range(groups - k)])
        for k in range(1, groups)
    ]
    prefix1 = jnp.concatenate([gather4(x) for x in prefix1], 0)
    proj = [(dot(x, in_all) + bias_proj).astype(BF16) for x in full1]
    proj_prefix = (dot(prefix1, kv_all) + bias_kv).astype(BF16)
    attended, lse = [None, None], [None, None]
    attended[1], lse[1] = attend(place, proj[1], size, segment=quarter)
    attended[0], lse[0] = attend(place, proj[0], size, prefix=proj_prefix)

    def halves(x):
        middle = x.shape[0] // 2
        return lambda i: x[i * middle : (i + 1) * middle]

    def product_of(x, weight, contract):
        part = halves(x)
        return lambda i: dot(part(i), weight, contract)

    resid, scaled2, inverse2, full2 = [None] * 2, [None] * 2, [None] * 2, [None] * 2
    for r in (1, 0):
        summed = scatter4(product_of(attended[r], out_all, ((1,), (0,))))
        resid[r] = rows[r] + summed + out_bias
        scaled2[r], inverse2[r] = stats(resid[r])
        full2[r] = gather4((scaled2[r] * second_gain + second_shift).astype(BF16))

    active, slope, full_cot, dup = [None] * 2, [None] * 2, [None] * 2, [None] * 2
    for r in (1, 0):
        full_cot[r] = gather4(after(cots[r], full1[r]))
        upward = dot(full2[r], up_all) + bias_up
        tanh = jnp.tanh(0.7978845608028654 * (upward + 0.044715 * upward * upward * upward))
        active[r] = (0.5 * upward * (1.0 + tanh)).astype(BF16)
        slope[r] = (
            0.5 * (1.0 + tanh)
            + 0.5
            * upward
            * (1.0 - tanh * tanh)
            * 0.7978845608028654
            * (1.0 + 3 * 0.044715 * upward * upward)
        )
    dres, sums2 = [None] * 2, []
    for r in (0, 1):
        dup[r] = (dot(full_cot[r], down_all, ((1,), (1,))) * slope[r]).astype(BF16)
        dnormed2 = scatter4(product_of(dup[r], up_all, ((1,), (1,))))
        cot = cots[r].astype(F32)
        dres[r] = cot + norm_back(dnormed2, scaled2[r], inverse2[r], second_gain)
        sums2.append(
            jnp.stack(
                [
                    jnp.sum(dres[r], 0),
                    jnp.sum(dnormed2 * scaled2[r], 0),
                    jnp.sum(dnormed2, 0),
                    jnp.sum(cot, 0),
                ]
            )
        )
    full_dres = [gather4(x.astype(BF16)) for x in dres]
    mixed = [None] * 2
    for r in (1, 0):
        summed = scatter4(product_of(active[r], down_all, ((1,), (0,))))
        mixed[r] = (resid[r] + summed + down_bias).astype(BF16)

    def scatter_weight(grad, shape, take):
        middle = {}
        for e_off, g_off in sources[::-1]:
            summed = square_scatter(
                lambda i, j: take(grad, dp_place(-e_off, i, j), g_off)
            )
            if (e_off, g_off) != (0, 0):
                summed = turn(
                    summed.astype(BF16), split, ((-e_off) % extra, (-g_off) % groups)
                ).astype(F32)
            middle[e_off, g_off] = summed
        return functools.reduce(jnp.add, [middle[s] for s in sources])

    def take_rows(grad, d, g):
        return lax.dynamic_slice(grad, (d * depth, g * hidden), (depth, hidden))

    def take_columns(grad, d, g):
        count = grad.shape[0] // groups
        return lax.dynamic_slice(grad, (g * count, d * depth), (count, depth))

    def take_in(grad, d, g):
        return jnp.concatenate(
            [
                lax.dynamic_slice(grad, (d * depth, (n * groups + g) * cols), (depth, cols))
                for n in range(3)
            ],
            1,
        )

    def weight_grad(lefts, rights):
        left, right = jnp.concatenate(lefts, 0), jnp.concatenate(rights, 0)
        return dot(left, right, ((0,), (0,))).astype(BF16)

    grad_down = scatter_weight(weight_grad(active, full_cot), down_weight.shape, take_columns)
    grad_up = scatter_weight(weight_grad(full2, dup), up_weight.shape, take_rows)
    grad_up_bias = jnp.sum(dup[0], 0, dtype=F32) + jnp.sum(dup[1], 0, dtype=F32)

    dattended = [dot(x, out_all, ((1,), (1,))).astype(BF16) for x in full_dres]
    dproj = [None, None]
    dproj[0], dprefix = attend_back(
        place, proj[0], attended[0], dattended[0], lse[0], size, prefix=proj_prefix
    )
    dproj[1] = attend_back(
        place, proj[1], attended[1], dattended[1], lse[1], size, segment=quarter
    )[0]
    grad_out = scatter_weight(weight_grad(attended, full_dres), out_weight.shape, take_columns)

    dnormed1 = [None, None]
    length = 4 * size
    returned = []
    for k in range(1, groups):
        part = scatter4(
            product_of(dprefix[(k - 1) * length : k * length], kv_all, ((1,), (1,)))
        ).astype(BF16)
        returned.append(
            lax.ppermute(part, "g", [(g + k, g) for g in range(groups - k)]).astype(F32)
        )
    for r in (1, 0):
        dnormed1[r] = scatter4(product_of(dproj[r], in_all, ((1,), (1,))))
    dnormed1[0] = functools.reduce(jnp.add, [dnormed1[0]] + returned)

    grad_q = weight_grad(full1, [x[:, : groups * cols] for x in dproj])
    grad_kv = weight_grad(full1 + [prefix1], [x[:, groups * cols :] for x in dproj] + [dprefix])
    grad_in = scatter_weight(
        jnp.concatenate([grad_q, grad_kv], 1), in_weight.shape, take_in
    ).reshape(in_weight.shape)
    tokens_grad, sums1 = [], []
    for r in range(2):
        tokens_grad.append(
            (dres[r] + norm_back(dnormed1[r], scaled1[r], inverse1[r], first_gain)).astype(BF16)
        )
        sums1.append(jnp.stack([jnp.sum(dnormed1[r] * scaled1[r], 0), jnp.sum(dnormed1[r], 0)]))

    grad_q_bias = jnp.sum(dproj[0][:, : groups * cols], 0, dtype=F32) + jnp.sum(
        dproj[1][:, : groups * cols], 0, dtype=F32
    )
    grad_v_bias = (
        jnp.sum(dproj[0][:, 2 * groups * cols :], 0, dtype=F32)
        + jnp.sum(dproj[1][:, 2 * groups * cols :], 0, dtype=F32)
        + jnp.sum(dprefix[:, groups * cols :], 0, dtype=F32)
    )

    def to_owner(x):
        share = x.reshape(groups, -1)
        return functools.reduce(
            jnp.add,
            [share[0]] + [turn(share[g], split, (0, (-g) % groups)) for g in range(1, groups)],
        )

    def sum_over(x, axes):
        for axis in axes:
            x = sum_axis(x, axis)
        return x

    early = sum_over(sums2[0] + sums2[1], ("c", "h", "g") + DP)
    grad_up_bias = sum_over(to_owner(grad_up_bias), DP)
    late = sum_over(sums1[0] + sums1[1], ("c", "h", "g") + DP)
    grad_in_bias = sum_over(jnp.stack([to_owner(grad_q_bias), to_owner(grad_v_bias)]), DP)
    return (
        unpick(*mixed),
        unpick(*tokens_grad),
        late[0],
        late[1],
        grad_in,
        grad_in_bias,
        grad_out,
        early[0],
        early[1],
        early[2],
        grad_up,
        grad_up_bias,
        grad_down,
        early[3],
    )


def solution(mesh):
    dp, tp = mesh.shape["dp"], mesh.shape["tp"]
    split = Mesh(mesh.devices.reshape(dp // 4, 2, 2, tp // 4, 2, 2), DP + TP)
    in_specs = (
        P(DP, TP, None),
        P(DP, None),
        P(),
        P(),
        P(DP, None, TP),
        P(None, TP),
        P(TP, DP),
        P(),
        P(),
        P(),
        P(DP, TP),
        P(TP),
        P(TP, DP),
        P(),
        P(DP, TP, None),
    )
    out_specs = (
        P(DP, TP, None),
        P(DP, TP, None),
        P(),
        P(),
        P(DP, None, TP),
        P(None, TP),
        P(TP, DP),
        P(),
        P(),
        P(),
        P(DP, TP),
        P(TP),
        P(TP, DP),
        P(),
    )
    return jax.shard_map(local, mesh=split, in_specs=in_specs, out_specs=out_specs, check_vma=False)
```

```python
import functools

import jax
import jax.numpy as jnp
from jax import lax
from jax.experimental import pallas as pl
from jax.experimental.pallas import tpu as pltpu
from jax.sharding import Mesh, PartitionSpec as P

HDIM = 128
EPSILON = 1e-05
MASKED = -1e30
LOG2E = 1.4426950408889634
F32 = jnp.float32
BF16 = jnp.bfloat16
VMEM_LIMIT = 48 * 1024 * 1024
KERNEL_VMEM = 63 * 1024 * 1024
DP = ("e", "b", "a")
TP = ("g", "h", "c")
SLOTS = (0, 2, 1, 3)


def dot(x, y, contract=((1,), (0,))):
    return lax.dot_general(x, y, (contract, ((), ())), preferred_element_type=F32)


def stats(rows):
    mean = jnp.mean(rows, axis=-1, keepdims=True)
    center = rows - mean
    inverse = lax.rsqrt(jnp.mean(center * center, axis=-1, keepdims=True) + EPSILON)
    return center * inverse, inverse


def norm_back(grad_normed, scaled, inverse, gain):
    weighted = grad_normed * gain
    return inverse * (
        weighted
        - jnp.mean(weighted, axis=-1, keepdims=True)
        - scaled * jnp.mean(weighted * scaled, axis=-1, keepdims=True)
    )


def flip(x, axis):
    return lax.ppermute(x, axis, [(0, 1), (1, 0)])


def scatter4(product):
    away = product(1).astype(BF16)
    kept = product(0) + flip(away, "c").astype(F32)
    local = kept.shape[0] // 2
    return kept[:local] + flip(kept[local:].astype(BF16), "h").astype(F32)


def turn(x, groups, by, axes=("e", "g")):
    extra, count = groups
    pairs = []
    for e in range(extra):
        for g in range(count):
            pairs.append((e * count + g, (e + by[0]) % extra * count + (g + by[1]) % count))
    return lax.ppermute(x, axes, pairs)


def sum_axis(x, axis):
    if lax.axis_size(axis) == 1:
        return x
    if lax.axis_size(axis) == 2:
        return x + flip(x, axis)
    return jnp.sum(lax.all_gather(x, axis), 0)


def row_blocks(place, count, size):
    found = []
    for j in range(count):
        other = jnp.bitwise_xor(place, j)
        slot = (other >> 1) + 2 * (other & 1)
        found.append(pl.multiple_of(slot * size, size))
    return found


def causal(size):
    keys = lax.broadcasted_iota(jnp.int32, (size, size), 0)
    queries = lax.broadcasted_iota(jnp.int32, (size, size), 1)
    return keys <= queries


def first_key(block, size, segment):
    return 0 if segment is None else block * size // segment * segment


class Copies:
    def __init__(self, send, recv, near):
        self.send, self.recv, self.near = send, recv, near
        self.remotes, self.locals = 0, 0
        self.open_sends, self.open_locals = [], []

    def remote(self, source, target, device, tracked=True):
        copy = pltpu.make_async_remote_copy(
            src_ref=source,
            dst_ref=target,
            send_sem=self.send.at[self.remotes],
            recv_sem=self.recv.at[self.remotes],
            device_id=device,
            device_id_type=pl.DeviceIdType.MESH,
        )
        self.remotes += 1
        if tracked:
            copy.start()
            self.open_sends.append(copy)
        return copy

    def local(self, source, target, tracked=True):
        copy = pltpu.make_async_copy(source, target, self.near.at[self.locals])
        self.locals += 1
        copy.start()
        if tracked:
            self.open_locals.append(copy)
        return copy

    def sent(self, copy):
        copy.wait_send()
        self.open_sends = [c for c in self.open_sends if c is not copy]

    def finish(self):
        for copy in self.open_sends:
            copy.wait_send()
        for copy in self.open_locals:
            copy.wait()


class Places:
    def __init__(self, extra, groups):
        self.extra, self.groups = extra, groups
        self.e, self.b, self.a, self.g, self.h, self.c = (lax.axis_index(n) for n in DP + TP)
        self.to_a, self.to_b = {"a": 1 - self.a}, {"b": 1 - self.b}
        self.to_h, self.to_c = {"h": 1 - self.h}, {"c": 1 - self.c}
        self.offsets = [(e, g) for g in range(groups) for e in range(extra)]

    def further(self, offset):
        return {
            "e": lax.rem(self.e + offset[0] + self.extra, self.extra),
            "g": lax.rem(self.g + offset[1] + self.groups, self.groups),
        }

    def share(self, offset, i, j):
        e = lax.rem(self.e - offset[0] + self.extra, self.extra)
        b = self.b if i == 0 else 1 - self.b
        a = self.a if j == 0 else 1 - self.a
        return e * 4 + b * 2 + a

    def barrier(self):
        semaphore = pltpu.get_barrier_semaphore()
        partners = [self.to_a, self.to_b, self.to_h, self.to_c]
        partners += [self.further(o) for o in self.offsets[1:]]
        for partner in partners:
            pl.semaphore_signal(
                semaphore, inc=1, device_id=partner, device_id_type=pl.DeviceIdType.MESH
            )
        pl.semaphore_wait(semaphore, len(partners))


class WeightGather:
    def __init__(self, copies, places, shard, full, at):
        self.copies, self.places, self.shard, self.full, self.at = copies, places, shard, full, at
        self.rows = shard.shape[0]
        self.steps = {}

    def piece(self, n, i, j, low=0, count=None):
        place = self.at(n, self.places.share(self.places.offsets[n], i, j))
        return self.full.at[
            pl.ds(place[0] + low, self.rows if count is None else count), place[1]
        ]

    def own(self):
        self.here = self.copies.local(self.shard, self.piece(0, 0, 0), tracked=False)
        self._first(0, self.shard)

    def turn(self):
        for n, offset in enumerate(self.places.offsets):
            if n:
                e, g = offset
                share = self.places.share((0, 0), 0, 0)
                place = self.at(n, share)
                target = self.full.at[pl.ds(place[0], self.rows), place[1]]
                self.steps["t", n] = self.copies.remote(
                    self.shard, target, self.places.further(offset)
                )

    def _first(self, n, source):
        piece = self.piece(n, 0, 0)
        self.steps["a", n] = self.copies.remote(source, piece, self.places.to_a)
        self.steps["b", n] = self.copies.remote(source, piece, self.places.to_b)

    def turned(self):
        for n in range(1, len(self.places.offsets)):
            self.steps["t", n].wait_recv()
            self._first(n, self.piece(n, 0, 0))

    def second(self, far):
        half = self.rows // 2
        for n in range(1, len(self.places.offsets)) if far else (0,):
            self.steps["a", n].wait_recv()
            top = self.piece(n, 0, 1, 0, half)
            self.steps["ab", n] = self.copies.remote(top, top, self.places.to_b)
            self.steps["b", n].wait_recv()
            low = self.piece(n, 1, 0, half, half)
            self.steps["ba", n] = self.copies.remote(low, low, self.places.to_a)

    def finish(self, far):
        if not far:
            self.here.wait()
        for n in range(1, len(self.places.offsets)) if far else (0,):
            self.steps["ab", n].wait_recv()
            self.steps["ba", n].wait_recv()


def in_tiles(rows, size, body):
    lax.fori_loop(0, rows // size, lambda n, _: (body(pl.multiple_of(n * size, size)), 0)[1], 0)


def layer_forward(extra, groups, quarter, *refs):
    (
        rows_ref, in_ref, out_ref, up_ref, down_ref, wide_ref, bias_ref, cots_ref,
        in_all, out_all, up_all, down_all, bias_all, full1, prefix1, proj_out, prefix_out, att_out,
        lse_out, resid_out, full2, full_cot,
        in_here, out_here, norm_here, prefix_here, proj, prefix_proj, att, lse, c_send, c_recv, h_send,
        h_recv, resid, normed2, k_own, v_own, send_sem, recv_sem, near_sem,
    ) = refs
    size, width = rows_ref.shape[1:]
    length = 4 * size
    cols = in_ref.shape[1] // 3
    hidden, depth = up_ref.shape[1], up_ref.shape[0]
    heads = groups * cols // HDIM
    per = cols // HDIM
    scale = HDIM**-0.5 * LOG2E
    places = Places(extra, groups)
    copies = Copies(send_sem, recv_sem, near_sem)
    bias_here = bias_all
    place = 2 * places.h + places.c
    at = row_blocks(place, 4, size)
    chunk = min(64, size)

    def in_at(wide):
        return lambda n, share: (share * depth, pl.ds((n // extra) * wide, wide))

    def column_at(rows):
        def where(n, share):
            return (n // extra) * rows, pl.ds(pl.multiple_of(share * depth, depth), depth)

        return where

    w_in = WeightGather(copies, places, in_ref, in_here, in_at(3 * cols))
    w_out = WeightGather(copies, places, out_ref, out_here, column_at(cols))
    w_up = WeightGather(copies, places, up_ref, up_all, in_at(hidden))
    w_down = WeightGather(copies, places, down_ref, down_all, column_at(hidden))

    def spread_to(source, full, row):
        return Spread(copies, places, source, full, row, size)

    def normalized(values, gain, shift):
        mean = jnp.mean(values, axis=-1, keepdims=True)
        center = values - mean
        inverse = lax.rsqrt(jnp.mean(center * center, axis=-1, keepdims=True) + EPSILON)
        return (center * inverse * wide_ref[gain : gain + 1] + wide_ref[shift : shift + 1]).astype(BF16)

    def first_norm(r):
        def body(at_row):
            values = rows_ref[r, pl.ds(at_row, chunk), :].astype(F32)
            norm_here[pl.ds(r * length + at_row, chunk), :] = normalized(values, 0, 1)

        in_tiles(size, chunk, body)

    def project(source, row, target, row_to, kind):
        wide = (3 - kind) * cols

        def body(n, _):
            g, m = n // 4, lax.rem(n, 4)
            x = source[pl.ds(pl.multiple_of(row + m * size, size), size), :]
            w = in_here[:, pl.ds(pl.multiple_of((g * 3 + kind) * cols, HDIM), wide)]
            bias = bias_here[g, :1, kind * cols : 3 * cols]
            to = pl.ds(pl.multiple_of(g * wide, HDIM), wide)
            target[pl.ds(pl.multiple_of(row_to + m * size, size), size), to] = (dot(x, w) + bias).astype(BF16)
            return 0

        lax.fori_loop(0, 4 * groups, body, 0)

    def attention(r, segment):
        def head(n, _):
            g, i = n // per, lax.rem(n, per)
            base = g * 3 * cols + i * HDIM
            q_at, k_at, v_at = (pl.ds(pl.multiple_of(base + m * cols, HDIM), HDIM) for m in range(3))
            pre = g * 2 * cols + i * HDIM
            kp_at, vp_at = (pl.ds(pl.multiple_of(pre + m * cols, HDIM), HDIM) for m in range(2))
            out_at = pl.ds(pl.multiple_of(n * HDIM, HDIM), HDIM)
            for j in range(4):
                there = pl.ds(r * length + at[j], size)
                k_own[j * size : (j + 1) * size] = proj[there, k_at]
                v_own[j * size : (j + 1) * size] = proj[there, v_at]

            def run(before):
                for j in range(4):
                    there = pl.ds(r * length + at[j], size)
                    q = proj[there, q_at]
                    start, end = first_key(j, size, segment), j * size
                    parts = [
                        (
                            prefix_proj[m * length : (m + 1) * length, kp_at],
                            prefix_proj[m * length : (m + 1) * length, vp_at],
                            None,
                        )
                        for m in range(before)
                    ]
                    if end > start:
                        parts.append((k_own[start:end], v_own[start:end], None))
                    parts.append((k_own[end : end + size], v_own[end : end + size], causal(size)))
                    scores = []
                    for k, _, mask in parts:
                        s = dot(k, q, ((1,), (1,)))
                        scores.append(s if mask is None else jnp.where(mask, s, MASKED))
                    top = functools.reduce(
                        jnp.maximum, [jnp.max(s, axis=0, keepdims=True) for s in scores]
                    )
                    total = jnp.zeros((1, size), F32)
                    out = jnp.zeros((HDIM, size), F32)
                    for s, (_, v, _) in zip(scores, parts):
                        p = jnp.exp2((s - top) * scale)
                        total = total + jnp.sum(p, axis=0, keepdims=True)
                        out = out + dot(v, p.astype(BF16), ((0,), (0,)))
                    att[there, out_at] = (out / total).T.astype(BF16)
                    lse[r * heads + n, :, j * size : (j + 1) * size] = top * scale + jnp.log(total) * LOG2E

            if segment is not None:
                run(0)
            else:
                for m in range(groups):
                    pl.when(places.g == m)(functools.partial(run, m))
            return 0

        lax.fori_loop(0, heads, head, 0)

    to_core, to_far = [None, None], [None, None]

    def out_product(r):
        def away(t):
            c_send[r, pl.ds(t, size), :] = dot(
                att[pl.ds(r * length + 2 * size + t, size), :], out_here[...]
            ).astype(BF16)

        in_tiles(2 * size, size, away)
        to_core[r] = copies.remote(c_send.at[r], c_recv.at[r], places.to_c)

    def out_sum(r):
        to_core[r].wait_recv()

        def far(t):
            h_send[r, pl.ds(t, size), :] = (
                dot(att[pl.ds(r * length + size + t, size), :], out_here[...])
                + c_recv[r, pl.ds(size + t, size), :].astype(F32)
            ).astype(BF16)

        in_tiles(size, size, far)
        to_far[r] = copies.remote(h_send.at[r], h_recv.at[r], places.to_h)

        def own(t):
            resid[r, pl.ds(t, size), :] = (
                dot(att[pl.ds(r * length + t, size), :], out_here[...])
                + c_recv[r, pl.ds(t, size), :].astype(F32)
                + rows_ref[r, pl.ds(t, size), :].astype(F32)
                + wide_ref[2:3]
            )

        in_tiles(size, size, own)

    def second_norm(r):
        to_far[r].wait_recv()

        def body(t):
            values = resid[r, pl.ds(t, chunk), :] + h_recv[r, pl.ds(t, chunk), :].astype(F32)
            resid[r, pl.ds(t, chunk), :] = values
            normed2[r, pl.ds(t, chunk), :] = normalized(values, 3, 4)

        in_tiles(size, chunk, body)
        copies.local(resid.at[r], resid_out.at[r])
        copies.local(normed2.at[r], full2.at[pl.ds(r * length, size), :])
        return spread_to(normed2.at[r], full2, r * length)

    def clear(t):
        prefix_here[pl.ds(t, size), :] = jnp.zeros((size, width), BF16)

    places.barrier()
    w_in.own()
    w_in.turn()
    bias_steps = [
        copies.remote(bias_ref, bias_here.at[n // extra], places.further(o))
        for n, o in enumerate(places.offsets)
        if n and o[0] == 0
    ]
    bias_here[0] = bias_ref[...]
    first_norm(0)
    spread = [spread_to(norm_here.at[pl.ds(0, size), :], norm_here, 0), None]
    before = []
    for k in range(1, groups):
        copy = copies.remote(
            norm_here.at[pl.ds(0, size), :],
            prefix_here.at[pl.ds((k - 1) * length, size), :],
            places.further((0, k)),
            tracked=False,
        )
        pl.when(places.g + k < groups)(copy.start)
        before.append(copy)
    first_norm(1)
    spread[1] = spread_to(norm_here.at[pl.ds(length, size), :], norm_here, length)
    w_in.second(False)
    w_out.own()
    w_out.turn()
    spread[0].forward()
    w_in.turned()
    w_out.second(False)
    spread[1].forward()
    w_in.second(True)
    w_up.own()
    w_up.turn()
    spread_cot = []
    for r in range(2):
        copies.local(cots_ref.at[r], full_cot.at[pl.ds(r * length, size), :])
        spread_cot.append(spread_to(cots_ref.at[r], full_cot, r * length))

    later = []
    for k in range(1, groups):
        row = (k - 1) * length
        slot = [prefix_here.at[pl.ds(row + n * size, size), :] for n in range(4)]
        far = copies.remote(slot[0], slot[1], places.to_h, tracked=False)
        core = copies.remote(slot[0], slot[2], places.to_c, tracked=False)
        last = copies.remote(slot[1], slot[3], places.to_c, tracked=False)
        later.append((far, core, last))

        @pl.when(places.g >= k)
        def _():
            before[k - 1].wait_recv()
            far.start()
            core.start()

        @pl.when(places.g < k)
        def _():
            in_tiles(length, size, lambda t: clear(row + t))

    w_in.finish(False)
    w_in.finish(True)
    copies.local(in_here, in_all)
    for copy in bias_steps:
        copy.wait_recv()
    spread[1].finish()
    project(norm_here, length, proj, length, 0)
    w_out.turned()
    attention(1, quarter)
    w_out.second(True)
    w_up.second(False)
    for k in range(1, groups):
        far, core, last = later[k - 1]

        @pl.when(places.g >= k)
        def _():
            far.wait_recv()
            last.start()

    spread[0].finish()
    copies.local(norm_here, full1)
    project(norm_here, 0, proj, 0, 0)
    w_out.finish(False)
    w_out.finish(True)
    copies.local(out_here, out_all)
    out_product(1)
    w_down.own()
    for k in range(1, groups):
        far, core, last = later[k - 1]

        @pl.when(places.g >= k)
        def _():
            core.wait_recv()
            last.wait_recv()

    for k in range(1, groups):
        project(prefix_here, (k - 1) * length, prefix_proj, (k - 1) * length, 1)
    copies.local(prefix_here, prefix1)
    copies.local(prefix_proj, prefix_out)
    copies.local(proj, proj_out)
    out_sum(1)
    w_up.turned()
    w_down.turn()
    spread_cot[0].forward()
    spread_cot[1].forward()
    attention(0, None)
    copies.local(att, att_out)
    copies.local(lse, lse_out)
    out_product(0)
    w_down.second(False)
    spread2 = [None, second_norm(1)]
    out_sum(0)
    w_up.second(True)
    spread2[0] = second_norm(0)
    spread2[1].forward()
    w_down.turned()
    spread2[0].forward()
    w_up.finish(False)
    w_up.finish(True)
    w_down.second(True)
    w_down.finish(False)
    spread2[1].finish()
    spread2[0].finish()
    spread_cot[0].finish()
    spread_cot[1].finish()
    w_down.finish(True)

    for k in range(1, groups):
        far, core, last = later[k - 1]
        pl.when(places.g + k < groups)(before[k - 1].wait_send)

        @pl.when(places.g >= k)
        def _():
            far.wait_send()
            core.wait_send()
            last.wait_send()

    copies.finish()


def run_forward(split, quarter, rows, in_w, out_w, up_w, down_w, wide, bias, cots):
    extra, groups = split
    size, width = rows.shape[1:]
    length = 4 * size
    cols, hidden = in_w.shape[1] // 3, up_w.shape[1]
    all_cols = groups * cols
    heads = all_cols // HDIM
    shape = jax.ShapeDtypeStruct
    anywhere = pl.BlockSpec(memory_space=pl.ANY)
    inside = pl.BlockSpec(memory_space=pltpu.VMEM)
    count = extra * groups * 20 + 4 * groups + 24
    out_shape = [
        shape((width, 3 * all_cols), BF16),
        shape((all_cols, width), BF16),
        shape((width, groups * hidden), BF16),
        shape((groups * hidden, width), BF16),
        shape((groups,) + bias.shape, F32),
        shape((2 * length, width), BF16),
        shape(((groups - 1) * length, width), BF16),
        shape((2 * length, 3 * all_cols), BF16),
        shape(((groups - 1) * length, 2 * all_cols), BF16),
        shape((2 * length, all_cols), BF16),
        shape((2 * heads, 1, length), F32),
        shape((2, size, width), F32),
        shape((2 * length, width), BF16),
        shape((2 * length, width), BF16),
    ]
    return pl.pallas_call(
        functools.partial(layer_forward, extra, groups, quarter),
        in_specs=[inside] + [anywhere] * 4 + [inside] * 2 + [anywhere],
        out_specs=[inside if n == 4 else anywhere for n in range(len(out_shape))],
        out_shape=out_shape,
        scratch_shapes=[
            pltpu.VMEM((width, 3 * all_cols), BF16),
            pltpu.VMEM((all_cols, width), BF16),
            pltpu.VMEM((2 * length, width), BF16),
            pltpu.VMEM(((groups - 1) * length, width), BF16),
            pltpu.VMEM((2 * length, 3 * all_cols), BF16),
            pltpu.VMEM(((groups - 1) * length, 2 * all_cols), BF16),
            pltpu.VMEM((2 * length, all_cols), BF16),
            pltpu.VMEM((2 * heads, 1, length), F32),
            pltpu.VMEM((2, 2 * size, width), BF16),
            pltpu.VMEM((2, 2 * size, width), BF16),
            pltpu.VMEM((2, size, width), BF16),
            pltpu.VMEM((2, size, width), BF16),
            pltpu.VMEM((2, size, width), F32),
            pltpu.VMEM((2, size, width), BF16),
            pltpu.VMEM((length, HDIM), BF16),
            pltpu.VMEM((length, HDIM), BF16),
            pltpu.SemaphoreType.DMA((count,)),
            pltpu.SemaphoreType.DMA((count,)),
            pltpu.SemaphoreType.DMA((24,)),
        ],
        compiler_params=kernel_params(0),
        cost_estimate=pl.CostEstimate(flops=10**11, bytes_accessed=10**8, transcendentals=10**7),
    )(rows, in_w, out_w, up_w, down_w, wide, bias, cots)


class GradScatter:
    def __init__(self, copies, places, parts, land, turned, work, own, fetched, out):
        self.copies, self.places, self.parts = copies, places, parts
        self.land, self.turned, self.work, self.own = land, turned, work, own
        self.fetched, self.out = fetched, out
        self.half, self.cols = land.shape[2:]
        self.steps = {}

    def piece(self, n, i, j, part):
        places = self.places
        offset = places.offsets[n]
        index = offset[1] * places.extra * 4 + places.share(offset, i, j)
        return self.parts.at[index, pl.ds(part * self.half, self.half), :]

    def _send(self, n, key, source, partner):
        self.steps[n, key] = self.copies.remote(source, self.land.at[n, key], partner)

    def start(self, n):
        to_a, to_b = self.places.to_a, self.places.to_b
        self._send(n, 0, self.piece(n, 1, 1, 0), to_a)
        self._send(n, 1, self.piece(n, 1, 1, 1), to_b)
        self._send(n, 2, self.piece(n, 0, 1, 0), to_a)
        self._send(n, 3, self.piece(n, 1, 0, 1), to_b)

    def _fetch(self, sources):
        got = [self.fetched.at[m, : self.half, : self.cols] for m in range(len(sources))]
        loads = [self.copies.local(s, t, tracked=False) for s, t in zip(sources, got)]
        for load in loads:
            load.wait()
        return functools.reduce(jnp.add, [t[...].astype(F32) for t in got])

    def middle(self, n):
        self.steps[n, 0].wait_recv()
        self.work[n, 0] = self._fetch([self.land.at[n, 0], self.piece(n, 1, 0, 0)]).astype(BF16)
        self._send(n, 5, self.work.at[n, 0], self.places.to_b)
        self.steps[n, 1].wait_recv()
        self.work[n, 1] = self._fetch([self.land.at[n, 1], self.piece(n, 0, 1, 1)]).astype(BF16)
        self._send(n, 4, self.work.at[n, 1], self.places.to_a)

    def last(self, n):
        for part, keys in ((0, (2, 5)), (1, (3, 4))):
            for key in keys:
                self.steps[n, key].wait_recv()
            summed = self._fetch([self.piece(n, 0, 0, part)] + [self.land.at[n, k] for k in keys])
            rows = slice(part * self.half, (part + 1) * self.half)
            if n == 0:
                self.out[rows, :] = summed
            else:
                self.own[n - 1, rows, :] = summed.astype(BF16)
        if n:
            e, g = self.places.offsets[n]
            self.steps[n, "t"] = self.copies.remote(
                self.own.at[n - 1], self.turned.at[n - 1], self.places.further((-e, -g))
            )

    def total(self):
        for n in range(1, len(self.places.offsets)):
            self.steps[n, "t"].wait_recv()
            for part in range(2):
                rows = slice(part * self.half, (part + 1) * self.half)
                self.out[rows, :] += self._fetch(
                    [self.turned.at[n - 1, pl.ds(part * self.half, self.half), :]]
                )

    @staticmethod
    def landing(sources, rows, cols):
        return [
            jax.ShapeDtypeStruct((sources, 6, rows // 2, cols), BF16),
            jax.ShapeDtypeStruct((max(sources - 1, 1), rows, cols), BF16),
        ]

    @staticmethod
    def working(sources, rows, cols):
        return [
            pltpu.VMEM((sources, 2, rows // 2, cols), BF16),
            pltpu.VMEM((max(sources - 1, 1), rows, cols), BF16),
        ]


class Fold:
    def __init__(self, copies, places, c_send, c_recv, h_send, free, size):
        self.copies, self.places, self.size = copies, places, size
        self.c_send, self.c_recv, self.h_send, self.free = c_send, c_recv, h_send, free
        self.core = self.far = None

    def away(self, block):
        if self.core is not None:
            self.copies.sent(self.core)
        for t in range(2):
            self.c_send[t * self.size : (t + 1) * self.size, :] = block(2 + t).astype(BF16)
        if self.core is not None:
            pl.semaphore_wait(self.free, 1)
        self.core = self.copies.remote(self.c_send, self.c_recv, self.places.to_c)

    def kept(self, block, target, h_recv, more):
        size = self.size
        far = block(1)
        self.core.wait_recv()
        if self.far is not None:
            self.copies.sent(self.far)
        self.h_send[...] = (far + self.c_recv[size:, :].astype(F32)).astype(BF16)
        self.far = self.copies.remote(self.h_send, h_recv, self.places.to_h)
        target[...] = (block(0) + self.c_recv[:size, :].astype(F32)).astype(target.dtype)
        if more:
            pl.semaphore_signal(
                self.free, inc=1, device_id=self.places.to_c, device_id_type=pl.DeviceIdType.MESH
            )
        return self.far


class Stream:
    def __init__(self, copies, slots, blocks):
        self.copies, self.slots, self.blocks = copies, slots, blocks
        self.loads = {}
        self._load(0)

    def _load(self, n):
        if n < len(self.blocks):
            targets = [s[n % 2] for s in self.slots]
            self.loads[n] = [
                self.copies.local(s, t, tracked=False) for s, t in zip(self.blocks[n], targets)
            ]

    def take(self, n):
        for load in self.loads[n]:
            load.wait()
        self._load(n + 1)
        return n % 2


class Spread:
    def __init__(self, copies, places, source, full, row, size):
        self.copies, self.places, self.full, self.row, self.size = copies, places, full, row, size
        self.far = copies.remote(source, self.slot(1), places.to_h)
        self.core = copies.remote(source, self.slot(2), places.to_c)

    def slot(self, n):
        return self.full.at[pl.ds(self.row + n * self.size, self.size), :]

    def forward(self):
        self.far.wait_recv()
        self.last = self.copies.remote(self.slot(1), self.slot(3), self.places.to_c)

    def finish(self):
        self.core.wait_recv()
        self.last.wait_recv()


def middle_kernel(extra, groups, *refs):
    (
        dup, act, full2, full_cot, up_all, cots, resid, wide,
        dres, full_dres, grad_down, up_parts, sums, down_parts, land, turned,
        big, narrow, tiles, c_send, c_recv, h_send, h_recv, low, stage_down, stage_up, work, own,
        fetched, send_sem, recv_sem, near_sem, free,
    ) = refs
    size, width = cots.shape[1:]
    length = 4 * size
    hidden, depth = grad_down.shape
    shares = extra * 4
    chunk = min(64, size)
    places = Places(extra, groups)
    copies = Copies(send_sem, recv_sem, near_sem)
    sources = len(places.offsets)
    down = GradScatter(
        copies, places, down_parts, land, turned, work, own, fetched, grad_down
    )
    fold = Fold(copies, places, c_send, c_recv, h_send, free, size)
    folded = []

    def load_big(source):
        return copies.local(source, big.at[: source.shape[0]], tracked=False)

    loading = load_big(up_all)
    order = [(r, slot) for r in range(2) for slot in (2, 3, 1, 0)]
    tile_slots = [tiles.at[0], tiles.at[1]]
    narrow_slots = [narrow.at[0], narrow.at[1]]
    stream = Stream(
        copies, [tile_slots], [[dup.at[pl.ds(r * length + s * size, size), :]] for r, s in order]
    )
    places.barrier()
    sums[...] = jnp.zeros_like(sums)
    loading.wait()

    def block_of(r):
        def block(slot):
            at = stream.take(order.index((r, slot)))
            return dot(tiles[at], big[:width], ((1,), (1,)))

        return block

    for r in range(2):
        fold.away(block_of(r))
        folded.append(fold.kept(block_of(r), dres.at[r], h_recv.at[r], r == 0))

    def norm_back_rows(r):
        folded[r].wait_recv()

        def body(t):
            rows = pl.ds(t, chunk)
            grad = dres[r, rows, :] + h_recv[r, rows, :].astype(F32)
            scaled, inverse = stats(resid[r, rows, :])
            cot = cots[r, rows, :].astype(F32)
            value = cot + norm_back(grad, scaled, inverse, wide[3:4])
            dres[r, rows, :] = value
            low[r, rows, :] = value.astype(BF16)
            for n, term in enumerate((value, grad * scaled, grad, cot)):
                sums[n : n + 1, :] += jnp.sum(term, axis=0, keepdims=True)

        in_tiles(size, chunk, body)
        copies.local(low.at[r], full_dres.at[pl.ds(r * length, size), :])
        return Spread(copies, places, low.at[r], full_dres, r * length, size)

    def columns(source):
        return [
            [source.at[:, pl.ds(d * depth, depth)]] for g in range(groups) for d in range(shares)
        ]

    turn_order = list(range(groups))[::-1]
    loading = load_big(act)
    stream_cot = Stream(copies, [narrow_slots], columns(full_cot))
    loading.wait()
    put = {}
    count = 0
    spread = [None, None]

    def down_grad(g):
        nonlocal count
        for d in range(shares):
            at = stream_cot.take(count)
            slot = count % 2
            if count - 2 in put:
                put.pop(count - 2).wait()

            def body(t):
                left = big[: 2 * length, pl.ds(pl.multiple_of(g * hidden + t, HDIM), hidden // 2)]
                stage_down[slot, pl.ds(t, hidden // 2), :] = dot(
                    left, narrow[at], ((0,), (0,))
                ).astype(BF16)

            in_tiles(hidden, hidden // 2, body)
            put[count] = copies.local(
                stage_down.at[slot], down_parts.at[g * shares + d], tracked=False
            )
            count += 1

    def of_group(g):
        return [n for n in range(sources) if places.offsets[n][1] == g][::-1]

    def flush():
        for n in range(max(count - 2, 0), count):
            if n in put:
                put.pop(n).wait()

    for step, g in enumerate(turn_order):
        down_grad(g)
        flush()
        for n in of_group(g):
            down.start(n)
        if step == 0:
            spread[0] = norm_back_rows(0)
    spread[1] = norm_back_rows(1)
    loading = load_big(dup)
    stream_two = Stream(copies, [narrow_slots], columns(full2))
    for n in of_group(turn_order[0]):
        down.middle(n)
    spread[0].forward()
    loading.wait()
    put_up = {}
    done = 0
    for step, g in enumerate(turn_order):
        for d in range(shares):
            at = stream_two.take(done)
            slot = done % 2
            if done >= 2:
                put_up.pop(done - 2).wait()
            stage_up[slot] = dot(
                narrow[at], big[: 2 * length, g * hidden : (g + 1) * hidden], ((0,), (0,))
            ).astype(BF16)
            put_up[done] = copies.local(
                stage_up.at[slot], up_parts.at[g * shares + d], tracked=False
            )
            done += 1
        if step == 0:
            for n in of_group(turn_order[0]):
                if n:
                    down.last(n)
            spread[1].forward()
            for g_next in turn_order[1:]:
                for n in of_group(g_next):
                    down.middle(n)
    for copy in put_up.values():
        copy.wait()
    spread[0].finish()
    spread[1].finish()
    for g in turn_order:
        for n in of_group(g):
            if (n, "t") not in down.steps:
                down.last(n)
    down.total()
    copies.finish()


def attention_back_rows(places, row, length, size, heads, per, segment, refs, column):
    (
        proj, prefix_proj, att, datt, lse, dproj, dprefix,
        k_own, v_own, dk_own, dv_own, dk_pre, dv_pre,
    ) = refs
    scale = HDIM**-0.5 * LOG2E
    factor = HDIM**-0.5
    at = row_blocks(2 * places.h + places.c, 4, size)
    base = row * length

    def head(n, _):
        q_at, k_at, v_at = (pl.ds(column(n, 3, m), HDIM) for m in range(3))
        kp_at, vp_at = (pl.ds(column(n, 2, m), HDIM) for m in range(2))
        out_at = pl.ds(pl.multiple_of(n * HDIM, HDIM), HDIM)
        for j in range(4):
            there = pl.ds(base + at[j], size)
            k_own[j * size : (j + 1) * size] = proj[there, k_at]
            v_own[j * size : (j + 1) * size] = proj[there, v_at]
        dk_own[...] = jnp.zeros_like(dk_own)
        dv_own[...] = jnp.zeros_like(dv_own)
        if segment is None:
            dk_pre[...] = jnp.zeros_like(dk_pre)
            dv_pre[...] = jnp.zeros_like(dv_pre)

        def run(before):
            for j in range(4):
                there = pl.ds(base + at[j], size)
                q = proj[there, q_at]
                do = datt[there, out_at]
                product = do.astype(F32) * att[there, out_at].astype(F32)
                delta = lax.dot_general(
                    jnp.ones((8, HDIM), F32),
                    product,
                    (((1,), (1,)), ((), ())),
                    precision=lax.Precision.HIGHEST,
                    preferred_element_type=F32,
                )[:1]
                log_total = lse[row * heads + n, :, j * size : (j + 1) * size]
                start, end = first_key(j, size, segment), j * size
                parts = []
                step = min(512, length)
                for m in range(0, before * length, step):
                    rows = slice(m, m + step)
                    parts.append(
                        (prefix_proj[rows, kp_at], prefix_proj[rows, vp_at], dk_pre, dv_pre, rows, None)
                    )
                if end > start:
                    rows = slice(start, end)
                    parts.append((k_own[rows], v_own[rows], dk_own, dv_own, rows, None))
                rows = slice(end, end + size)
                parts.append((k_own[rows], v_own[rows], dk_own, dv_own, rows, causal(size)))
                dq = jnp.zeros((HDIM, size), F32)
                for k, v, dk, dv, rows, mask in parts:
                    s = dot(k, q, ((1,), (1,))) * scale - log_total
                    p = jnp.exp2(s if mask is None else jnp.where(mask, s, MASKED))
                    dscores = (p * (dot(v, do, ((1,), (1,))) - delta)).astype(BF16)
                    dv[rows] += dot(p.astype(BF16), do)
                    dk[rows] += dot(dscores, q)
                    dq = dq + dot(k, dscores, ((0,), (0,)))
                dproj[there, q_at] = (dq * factor).T.astype(BF16)

        if segment is not None:
            run(0)
        else:
            for m in range(places.groups):
                pl.when(places.g == m)(functools.partial(run, m))
            dprefix[:, q_at] = jnp.zeros_like(dk_pre, dtype=BF16)
            dprefix[:, k_at] = (dk_pre[...] * factor).astype(BF16)
            dprefix[:, v_at] = dv_pre[...].astype(BF16)
        for j in range(4):
            rows = slice(j * size, (j + 1) * size)
            there = pl.ds(base + at[j], size)
            dproj[there, k_at] = (dk_own[rows] * factor).astype(BF16)
            dproj[there, v_at] = dv_own[rows].astype(BF16)
        return 0

    lax.fori_loop(0, heads, head, 0)


def last_kernel(extra, groups, quarter, *refs):
    (
        proj_in, prefix_in, att_in, full_dres, out_all, in_all, full1, prefix1, up_parts, lse,
        grad_in, grad_out, grad_up, dnormed1, h_recv, returned, dproj_sums,
        in_parts, out_parts, land_in, turned_in, land_out, turned_out, land_up, turned_up,
        proj, prefix_proj, att, datt, dprefix, w_in, w_out, spare,
        k_own, v_own, dk_own, dv_own, dk_pre, dv_pre,
        c_send, c_recv, h_send, back, stage_in, stage_out,
        work_in, own_in, work_out, own_out, work_up, own_up, fetched, send_sem, recv_sem, near_sem, free,
    ) = refs
    size, width = dnormed1.shape[1:]
    length = 4 * size
    cols = grad_in.shape[1] // 3
    depth = grad_in.shape[0]
    wide = 3 * cols
    heads = groups * cols // HDIM
    per = cols // HDIM
    shares = extra * 4
    places = Places(extra, groups)
    copies = Copies(send_sem, recv_sem, near_sem)
    sources = len(places.offsets)
    far_first = list(range(sources))[::-1]
    up = GradScatter(
        copies, places, up_parts, land_up, turned_up, work_up, own_up, fetched, grad_up
    )
    out = GradScatter(
        copies, places, out_parts, land_out, turned_out, work_out, own_out, fetched, grad_out
    )
    into = GradScatter(
        copies, places, in_parts, land_in, turned_in, work_in, own_in, fetched, grad_in
    )
    dproj = proj
    folds = Fold(copies, places, c_send, c_recv, h_send, free, size)
    folded = {}

    def column(n, parts, m):
        return pl.multiple_of((n // per * parts + m) * cols + lax.rem(n, per) * HDIM, HDIM)

    here = [
        copies.local(s, t, tracked=False)
        for s, t in (
            (out_all, w_out), (proj_in, proj), (prefix_in, prefix_proj), (att_in, att), (in_all, w_in),
        )
    ]
    order = [(r, slot) for r in range(2) for slot in range(4)]
    tiles = [c_send.at[pl.ds(n * size, size), :] for n in range(2)]
    stream = Stream(
        copies, [tiles], [[full_dres.at[pl.ds(r * length + s * size, size), :]] for r, s in order]
    )
    places.barrier()
    for n in far_first:
        up.start(n)
    for copy in here:
        copy.wait()

    def attended_grad(r):
        for slot in range(4):
            at = stream.take(r * 4 + slot)
            datt[r * length + slot * size : r * length + (slot + 1) * size, :] = dot(
                tiles[at][...], w_out[...], ((1,), (1,))
            ).astype(BF16)

    def attention_back(r, segment):
        attention_back_rows(
            places, r, length, size, heads, per, segment,
            (
                proj, prefix_proj, att, datt, lse, dproj, dprefix,
                k_own, v_own, dk_own, dv_own, dk_pre, dv_pre,
            ),
            column,
        )

    def block_of(source, row):
        def block(slot):
            rows = source[row + slot * size : row + (slot + 1) * size, :]
            return dot(rows, w_in[...], ((1,), (1,)))

        return block

    def fold(number, source, row, target, more=True):
        folds.away(block_of(source, row))
        folded[number] = folds.kept(block_of(source, row), target, h_recv.at[number], more)

    attended_grad(0)
    attended_grad(1)
    attention_back(0, None)
    for n in far_first:
        up.middle(n)
    for k in range(1, groups):
        fold(1 + k, dprefix, (k - 1) * length, back.at[k - 1])
    attention_back(1, quarter)
    for n in far_first:
        up.last(n)

    home = []
    for k in range(1, groups):
        folded[1 + k].wait_recv()
        back[k - 1] = (back[k - 1].astype(F32) + h_recv[1 + k].astype(F32)).astype(BF16)
        copy = copies.remote(
            back.at[k - 1], returned.at[k - 1], places.further((0, -k)), tracked=False
        )
        pl.when(places.g >= k)(copy.start)
        home.append(copy)

    slots = [datt.at[:, pl.ds(0, depth)], spare]
    prefix_rows = prefix1.shape[0]
    slots_pre = [prefix_proj.at[:, pl.ds(n * depth, depth)] for n in range(2)]

    class Columns:
        def __init__(self, sources_and_slots, count):
            self.pairs, self.count, self.loads = sources_and_slots, count, {}
            self._load(0)

        def _load(self, n):
            if n < self.count:
                d = n % shares
                self.loads[n] = [
                    copies.local(s.at[:, pl.ds(d * depth, depth)], slot[n % 2], tracked=False)
                    for s, slot in self.pairs
                ]

        def take(self, n):
            for load in self.loads[n]:
                load.wait()
            self._load(n + 1)
            return n % 2

    put = []

    def store(stage, target):
        put.append(copies.local(stage, target, tracked=False))

    def drain(left):
        while len(put) > left:
            put.pop(0).wait()

    stream_in = Columns([(full1, slots), (prefix1, slots_pre)], groups * shares)
    count = 0
    for g in range(groups)[::-1]:
        for d in range(shares):
            at = stream_in.take(count)
            drain(1)
            which = pl.ds(g * wide, wide)
            value = dot(slots[at][...], dproj[:, which], ((0,), (0,)))
            if prefix_rows:
                value = value + dot(slots_pre[at][...], dprefix[:, which], ((0,), (0,)))
            stage_in[count % 2] = value.astype(BF16)
            store(stage_in.at[count % 2], in_parts.at[g * shares + d])
            count += 1
        drain(0)
        for n in far_first:
            if places.offsets[n][1] == g:
                into.start(n)
    stream_out = Columns([(full_dres, slots)], shares)
    for d in range(shares):
        at = stream_out.take(d)
        for g in range(groups):
            drain(1)
            slot = (d * groups + g) % 2
            stage_out[slot] = dot(
                att[:, g * cols : (g + 1) * cols], slots[at][...], ((0,), (0,))
            ).astype(BF16)
            store(stage_out.at[slot], out_parts.at[g * shares + d])
    drain(0)
    for n in far_first:
        out.start(n)
    fold(0, dproj, 0, dnormed1.at[0])
    for n in far_first:
        if places.offsets[n][1] == groups - 1:
            into.middle(n)
    fold(1, dproj, length, dnormed1.at[1], False)
    for n in far_first:
        if places.offsets[n][1] != groups - 1:
            into.middle(n)
    for n in far_first:
        if n and places.offsets[n][1] == groups - 1:
            into.last(n)
    for n in far_first:
        out.middle(n)
    dproj_sums[...] = jnp.zeros_like(dproj_sums)

    def add_rows(t):
        dproj_sums[0:1, :] += jnp.sum(dproj[pl.ds(t, size), :].astype(F32), axis=0, keepdims=True)

    in_tiles(2 * length, size, add_rows)

    def add_prefix(t):
        dproj_sums[1:2, :] += jnp.sum(dprefix[pl.ds(t, size), :].astype(F32), axis=0, keepdims=True)

    in_tiles(prefix_rows, size, add_prefix)
    up.total()
    for n in far_first:
        if (n, "t") not in into.steps:
            into.last(n)
    for n in far_first:
        out.last(n)
    for r in range(2):
        folded[r].wait_recv()
    out.total()
    into.total()
    for k in range(1, groups):
        pl.when(places.g + k < groups)(home[k - 1].wait_recv)
        pl.when(places.g >= k)(home[k - 1].wait_send)
    copies.finish()


def kernel_params(number):
    return pltpu.CompilerParams(
        collective_id=number, has_side_effects=True, vmem_limit_bytes=KERNEL_VMEM
    )


def run_middle(split, dup, act, full2, full_cot, up_all, cots, resid, wide, hidden, depth):
    extra, groups = split
    sources = extra * groups
    size, width = cots.shape[1:]
    length = 4 * size
    shape = jax.ShapeDtypeStruct
    anywhere = pl.BlockSpec(memory_space=pl.ANY)
    inside = pl.BlockSpec(memory_space=pltpu.VMEM)
    shares = sources * 4
    return pl.pallas_call(
        functools.partial(middle_kernel, extra, groups),
        in_specs=[anywhere] * 5 + [inside] * 3,
        out_specs=[inside, anywhere, inside, anywhere, inside] + [anywhere] * 3,
        out_shape=[
            shape((2, size, width), F32),
            shape((2 * length, width), BF16),
            shape((hidden, depth), F32),
            shape((shares, depth, hidden), BF16),
            shape((4, width), F32),
            shape((shares, hidden, depth), BF16),
        ]
        + GradScatter.landing(sources, hidden, depth),
        scratch_shapes=[
            pltpu.VMEM((max(width, 2 * length), groups * hidden), BF16),
            pltpu.VMEM((2, 2 * length, depth), BF16),
            pltpu.VMEM((2, size, groups * hidden), BF16),
            pltpu.VMEM((2 * size, width), BF16),
            pltpu.VMEM((2 * size, width), BF16),
            pltpu.VMEM((size, width), BF16),
            pltpu.VMEM((2, size, width), BF16),
            pltpu.VMEM((2, size, width), BF16),
            pltpu.VMEM((2, hidden, depth), BF16),
            pltpu.VMEM((2, depth, hidden), BF16),
        ]
        + GradScatter.working(sources, hidden, depth)
        + [
            pltpu.VMEM((3, hidden // 2, depth), BF16),
            pltpu.SemaphoreType.DMA((sources * 8 + 16,)),
            pltpu.SemaphoreType.DMA((sources * 8 + 16,)),
            pltpu.SemaphoreType.DMA((sources * 16 + 6 * shares + 24,)),
            pltpu.SemaphoreType.REGULAR,
        ],
        compiler_params=kernel_params(1),
        cost_estimate=pl.CostEstimate(flops=10**11, bytes_accessed=10**8, transcendentals=10**6),
    )(dup, act, full2, full_cot, up_all, cots, resid, wide)


def run_last(split, quarter, proj, prefix_proj, att, full_dres, out_all, in_all, full1, prefix1, up_parts, lse):
    extra, groups = split
    sources = extra * groups
    shares = sources * 4
    length, width = full1.shape[0] // 2, full1.shape[1]
    size = length // 4
    cols = att.shape[1] // groups
    depth, hidden = up_parts.shape[1:]
    wide, all_wide = 3 * cols, 3 * cols * groups
    prefix_rows = prefix1.shape[0]
    shape = jax.ShapeDtypeStruct
    anywhere = pl.BlockSpec(memory_space=pl.ANY)
    inside = pl.BlockSpec(memory_space=pltpu.VMEM)
    heads_rows = [pltpu.VMEM((length, HDIM), BF16)] * 2 + [pltpu.VMEM((length, HDIM), F32)] * 2
    return pl.pallas_call(
        functools.partial(last_kernel, extra, groups, quarter),
        in_specs=[anywhere] * 9 + [inside],
        out_specs=[inside] * 7 + [anywhere] * 8,
        out_shape=[
            shape((depth, wide), F32),
            shape((cols, depth), F32),
            shape((depth, hidden), F32),
            shape((2, size, width), BF16),
            shape((1 + groups, size, width), BF16),
            shape((max(groups - 1, 1), size, width), BF16),
            shape((2, all_wide), F32),
            shape((shares, depth, wide), BF16),
            shape((shares, cols, depth), BF16),
        ]
        + GradScatter.landing(sources, depth, wide)
        + GradScatter.landing(sources, cols, depth)
        + GradScatter.landing(sources, depth, hidden),
        scratch_shapes=[
            pltpu.VMEM(proj.shape, BF16),
            pltpu.VMEM(prefix_proj.shape, BF16),
            pltpu.VMEM(att.shape, BF16),
            pltpu.VMEM(att.shape, BF16),
            pltpu.VMEM((prefix_rows, all_wide), BF16),
            pltpu.VMEM(in_all.shape, BF16),
            pltpu.VMEM(out_all.shape, BF16),
            pltpu.VMEM((2 * length, depth), BF16),
        ]
        + heads_rows
        + [pltpu.VMEM((prefix_rows, HDIM), F32)] * 2
        + [
            pltpu.VMEM((2 * size, width), BF16),
            pltpu.VMEM((2 * size, width), BF16),
            pltpu.VMEM((size, width), BF16),
            pltpu.VMEM((max(groups - 1, 1), size, width), BF16),
            pltpu.VMEM((2, depth, wide), BF16),
            pltpu.VMEM((2, cols, depth), BF16),
        ]
        + GradScatter.working(sources, depth, wide)
        + GradScatter.working(sources, cols, depth)
        + GradScatter.working(sources, depth, hidden)
        + [
            pltpu.VMEM((3, depth // 2, max(wide, hidden, depth)), BF16),
            pltpu.SemaphoreType.DMA((sources * 24 + 4 * groups + 16,)),
            pltpu.SemaphoreType.DMA((sources * 24 + 4 * groups + 16,)),
            pltpu.SemaphoreType.DMA((sources * 48 + 10 * shares + 32,)),
            pltpu.SemaphoreType.REGULAR,
        ],
        compiler_params=kernel_params(2),
        cost_estimate=pl.CostEstimate(flops=10**11, bytes_accessed=10**8, transcendentals=10**7),
    )(proj, prefix_proj, att, full_dres, out_all, in_all, full1, prefix1, up_parts, lse)


def local(
    tokens,
    segments,
    first_gain,
    first_shift,
    in_weight,
    in_bias,
    out_weight,
    out_bias,
    second_gain,
    second_shift,
    up_weight,
    up_bias,
    down_weight,
    down_bias,
    cotangent,
):
    extra, groups = lax.axis_size("e"), lax.axis_size("g")
    split = (extra, groups)
    size, width = tokens.shape[1:]
    cols, hidden, depth = in_weight.shape[2], up_weight.shape[1], in_weight.shape[0]
    quarter = segments.shape[1] // 4

    single = jnp.where(segments[0, -1] == 0, 0, 1)
    order = (single, 1 - single)

    def pick(x):
        return [lax.dynamic_index_in_dim(x, r, 0, keepdims=False) for r in order]

    def unpick(first, second):
        return jnp.where(single == 0, jnp.stack([first, second]), jnp.stack([second, first]))

    rows = [r.astype(F32) for r in pick(tokens)]
    cots = pick(cotangent)

    no_bias = jnp.zeros_like(in_bias[0])
    biases = jnp.concatenate([in_bias[0], no_bias, in_bias[1], up_bias])
    biases = jnp.broadcast_to(biases, (8, biases.shape[0]))
    wide = jnp.stack([first_gain, first_shift, out_bias, second_gain, second_shift])
    (
        in_all, out_all, up_all, down_all, biases, full1, prefix1, proj, proj_prefix, attended, lse,
        resid, full2, full_cot,
    ) = run_forward(
        split,
        quarter,
        jnp.stack(pick(tokens)),
        in_weight.reshape(depth, 3 * cols),
        out_weight,
        up_weight,
        down_weight,
        wide,
        biases,
        jnp.stack(cots),
    )
    bias_up = biases[:, 0, 3 * cols :].reshape(-1)
    length = 4 * size
    both = (slice(0, length), slice(length, 2 * length))

    def halves(x):
        middle = x.shape[0] // 2
        return lambda i: x[i * middle : (i + 1) * middle]

    def product_of(x, weight, contract):
        part = halves(x)
        return lambda i: dot(part(i), weight, contract)

    scaled1, inverse1 = zip(*[stats(x) for x in rows])

    active, dup = [None] * 2, [None] * 2
    for r in (1, 0):
        upward = dot(full2[both[r]], up_all) + bias_up
        tanh = jnp.tanh(0.7978845608028654 * (upward + 0.044715 * upward * upward * upward))
        active[r] = (0.5 * upward * (1.0 + tanh)).astype(BF16)
        slope = (
            0.5 * (1.0 + tanh)
            + 0.5
            * upward
            * (1.0 - tanh * tanh)
            * 0.7978845608028654
            * (1.0 + 3 * 0.044715 * upward * upward)
        )
        dup[r] = (dot(full_cot[both[r]], down_all, ((1,), (1,))) * slope).astype(BF16)
    grad_up_bias = jnp.sum(dup[0], 0, dtype=F32) + jnp.sum(dup[1], 0, dtype=F32)
    dup, act = jnp.concatenate(dup, 0), jnp.concatenate(active, 0)
    dres, full_dres, grad_down, up_parts, sums2 = run_middle(
        split, dup, act, full2, full_cot, up_all, jnp.stack(cots), resid, wide, hidden, depth
    )[:5]
    mixed = [None] * 2
    for r in (1, 0):
        summed = scatter4(product_of(active[r], down_all, ((1,), (0,))))
        mixed[r] = (resid[r] + summed + down_bias).astype(BF16)

    grad_in, grad_out, grad_up, kept, halves_far, returned, dproj_sums = run_last(
        split, quarter, proj, proj_prefix, attended, full_dres, out_all, in_all, full1, prefix1, up_parts, lse
    )[:7]
    dnormed1 = [kept[r].astype(F32) + halves_far[r].astype(F32) for r in range(2)]
    at_g = lax.axis_index("g")
    for k in range(1, groups):
        dnormed1[0] += jnp.where(at_g + k < groups, returned[k - 1].astype(F32), 0.0)
    grad_in = grad_in.reshape(in_weight.shape)
    tokens_grad, sums1 = [], []
    for r in range(2):
        tokens_grad.append(
            (dres[r] + norm_back(dnormed1[r], scaled1[r], inverse1[r], first_gain)).astype(BF16)
        )
        sums1.append(jnp.stack([jnp.sum(dnormed1[r] * scaled1[r], 0), jnp.sum(dnormed1[r], 0)]))

    sums = dproj_sums.reshape(2, groups, 3, cols)
    grad_q_bias = sums[0, :, 0]
    grad_v_bias = sums[0, :, 2] + sums[1, :, 2]

    def to_owner(x):
        share = x.reshape(groups, -1)
        return functools.reduce(
            jnp.add,
            [share[0]] + [turn(share[g], split, (0, (-g) % groups)) for g in range(1, groups)],
        )

    def sum_over(x, axes):
        for axis in axes:
            x = sum_axis(x, axis)
        return x

    early = sum_over(sums2, ("c", "h", "g") + DP)
    grad_up_bias = sum_over(to_owner(grad_up_bias), DP)
    late = sum_over(sums1[0] + sums1[1], ("c", "h", "g") + DP)
    grad_in_bias = sum_over(jnp.stack([to_owner(grad_q_bias), to_owner(grad_v_bias)]), DP)
    return (
        unpick(*mixed),
        unpick(*tokens_grad),
        late[0],
        late[1],
        grad_in,
        grad_in_bias,
        grad_out,
        early[0],
        early[1],
        early[2],
        grad_up,
        grad_up_bias,
        grad_down,
        early[3],
    )


def solution(mesh):
    dp, tp = mesh.shape["dp"], mesh.shape["tp"]
    split = Mesh(mesh.devices.reshape(dp // 4, 2, 2, tp // 4, 2, 2), DP + TP)
    in_specs = (
        P(DP, TP, None),
        P(DP, None),
        P(),
        P(),
        P(DP, None, TP),
        P(None, TP),
        P(TP, DP),
        P(),
        P(),
        P(),
        P(DP, TP),
        P(TP),
        P(TP, DP),
        P(),
        P(DP, TP, None),
    )
    out_specs = (
        P(DP, TP, None),
        P(DP, TP, None),
        P(),
        P(),
        P(DP, None, TP),
        P(None, TP),
        P(TP, DP),
        P(),
        P(),
        P(),
        P(DP, TP),
        P(TP),
        P(TP, DP),
        P(),
    )
    return jax.shard_map(local, mesh=split, in_specs=in_specs, out_specs=out_specs, check_vma=False)
```

```python
import functools

import jax
import jax.numpy as jnp
from jax import lax
from jax.experimental import pallas as pl
from jax.experimental.pallas import tpu as pltpu
from jax.sharding import Mesh, PartitionSpec as P

HDIM = 128
EPSILON = 1e-05
MASKED = -1e30
LOG2E = 1.4426950408889634
F32 = jnp.float32
BF16 = jnp.bfloat16
VMEM_LIMIT = 48 * 1024 * 1024
KERNEL_VMEM = 63 * 1024 * 1024
DP = ("e", "b", "a")
TP = ("g", "h", "c")
SLOTS = (0, 2, 1, 3)


def dot(x, y, contract=((1,), (0,))):
    return lax.dot_general(x, y, (contract, ((), ())), preferred_element_type=F32)


def stats(rows):
    mean = jnp.mean(rows, axis=-1, keepdims=True)
    center = rows - mean
    inverse = lax.rsqrt(jnp.mean(center * center, axis=-1, keepdims=True) + EPSILON)
    return center * inverse, inverse


def norm_back(grad_normed, scaled, inverse, gain):
    weighted = grad_normed * gain
    return inverse * (
        weighted
        - jnp.mean(weighted, axis=-1, keepdims=True)
        - scaled * jnp.mean(weighted * scaled, axis=-1, keepdims=True)
    )


def flip(x, axis):
    return lax.ppermute(x, axis, [(0, 1), (1, 0)])


def turn(x, groups, by, axes=("e", "g")):
    extra, count = groups
    pairs = []
    for e in range(extra):
        for g in range(count):
            pairs.append((e * count + g, (e + by[0]) % extra * count + (g + by[1]) % count))
    return lax.ppermute(x, axes, pairs)


def sum_axis(x, axis):
    if lax.axis_size(axis) == 1:
        return x
    if lax.axis_size(axis) == 2:
        return x + flip(x, axis)
    return jnp.sum(lax.all_gather(x, axis), 0)


def row_blocks(place, count, size):
    found = []
    for j in range(count):
        other = jnp.bitwise_xor(place, j)
        slot = (other >> 1) + 2 * (other & 1)
        found.append(pl.multiple_of(slot * size, size))
    return found


def causal(size):
    keys = lax.broadcasted_iota(jnp.int32, (size, size), 0)
    queries = lax.broadcasted_iota(jnp.int32, (size, size), 1)
    return keys <= queries


def first_key(block, size, segment):
    return 0 if segment is None else block * size // segment * segment


class Copies:
    def __init__(self, send, recv, near):
        self.send, self.recv, self.near = send, recv, near
        self.remotes, self.locals = 0, 0
        self.open_sends, self.open_locals = [], []

    def remote(self, source, target, device, tracked=True):
        copy = pltpu.make_async_remote_copy(
            src_ref=source,
            dst_ref=target,
            send_sem=self.send.at[self.remotes],
            recv_sem=self.recv.at[self.remotes],
            device_id=device,
            device_id_type=pl.DeviceIdType.MESH,
        )
        self.remotes += 1
        if tracked:
            copy.start()
            self.open_sends.append(copy)
        return copy

    def local(self, source, target, tracked=True):
        copy = pltpu.make_async_copy(source, target, self.near.at[self.locals])
        self.locals += 1
        copy.start()
        if tracked:
            self.open_locals.append(copy)
        return copy

    def sent(self, copy):
        copy.wait_send()
        self.open_sends = [c for c in self.open_sends if c is not copy]

    def finish(self):
        for copy in self.open_sends:
            copy.wait_send()
        for copy in self.open_locals:
            copy.wait()


class Places:
    def __init__(self, extra, groups):
        self.extra, self.groups = extra, groups
        self.e, self.b, self.a, self.g, self.h, self.c = (lax.axis_index(n) for n in DP + TP)
        self.to_a, self.to_b = {"a": 1 - self.a}, {"b": 1 - self.b}
        self.to_h, self.to_c = {"h": 1 - self.h}, {"c": 1 - self.c}
        self.offsets = [(e, g) for g in range(groups) for e in range(extra)]

    def further(self, offset):
        return {
            "e": lax.rem(self.e + offset[0] + self.extra, self.extra),
            "g": lax.rem(self.g + offset[1] + self.groups, self.groups),
        }

    def share(self, offset, i, j):
        e = lax.rem(self.e - offset[0] + self.extra, self.extra)
        b = self.b if i == 0 else 1 - self.b
        a = self.a if j == 0 else 1 - self.a
        return e * 4 + b * 2 + a

    def barrier(self):
        semaphore = pltpu.get_barrier_semaphore()
        partners = [self.to_a, self.to_b, self.to_h, self.to_c]
        partners += [self.further(o) for o in self.offsets[1:]]
        for partner in partners:
            pl.semaphore_signal(
                semaphore, inc=1, device_id=partner, device_id_type=pl.DeviceIdType.MESH
            )
        pl.semaphore_wait(semaphore, len(partners))


class WeightGather:
    def __init__(self, copies, places, shard, full, at):
        self.copies, self.places, self.shard, self.full, self.at = copies, places, shard, full, at
        self.rows = shard.shape[0]
        self.steps = {}

    def piece(self, n, i, j, low=0, count=None):
        place = self.at(n, self.places.share(self.places.offsets[n], i, j))
        return self.full.at[
            pl.ds(place[0] + low, self.rows if count is None else count), place[1]
        ]

    def own(self):
        self.here = self.copies.local(self.shard, self.piece(0, 0, 0), tracked=False)
        self._first(0, self.shard)

    def turn(self):
        for n, offset in enumerate(self.places.offsets):
            if n:
                e, g = offset
                share = self.places.share((0, 0), 0, 0)
                place = self.at(n, share)
                target = self.full.at[pl.ds(place[0], self.rows), place[1]]
                self.steps["t", n] = self.copies.remote(
                    self.shard, target, self.places.further(offset)
                )

    def _first(self, n, source):
        piece = self.piece(n, 0, 0)
        self.steps["a", n] = self.copies.remote(source, piece, self.places.to_a)
        self.steps["b", n] = self.copies.remote(source, piece, self.places.to_b)

    def turned(self):
        for n in range(1, len(self.places.offsets)):
            self.steps["t", n].wait_recv()
            self._first(n, self.piece(n, 0, 0))

    def second(self, far):
        half = self.rows // 2
        for n in range(1, len(self.places.offsets)) if far else (0,):
            self.steps["a", n].wait_recv()
            top = self.piece(n, 0, 1, 0, half)
            self.steps["ab", n] = self.copies.remote(top, top, self.places.to_b)
            self.steps["b", n].wait_recv()
            low = self.piece(n, 1, 0, half, half)
            self.steps["ba", n] = self.copies.remote(low, low, self.places.to_a)

    def finish(self, far):
        if not far:
            self.here.wait()
        for n in range(1, len(self.places.offsets)) if far else (0,):
            self.steps["ab", n].wait_recv()
            self.steps["ba", n].wait_recv()


def in_tiles(rows, size, body):
    lax.fori_loop(0, rows // size, lambda n, _: (body(pl.multiple_of(n * size, size)), 0)[1], 0)


def layer_forward(extra, groups, quarter, *refs):
    (
        rows_ref, in_ref, out_ref, up_ref, down_ref, wide_ref, bias_ref, cots_ref,
        in_all, out_all, up_all, down_all, bias_all, full1, prefix1, proj_out, prefix_out, att_out,
        lse_out, resid_out, full2, full_cot,
        in_here, out_here, norm_here, prefix_here, proj, prefix_proj, att, lse, c_send, c_recv, h_send,
        h_recv, resid, normed2, k_own, v_own, send_sem, recv_sem, near_sem,
    ) = refs
    size, width = rows_ref.shape[1:]
    length = 4 * size
    cols = in_ref.shape[1] // 3
    hidden, depth = up_ref.shape[1], up_ref.shape[0]
    heads = groups * cols // HDIM
    per = cols // HDIM
    scale = HDIM**-0.5 * LOG2E
    places = Places(extra, groups)
    copies = Copies(send_sem, recv_sem, near_sem)
    bias_here = bias_all
    place = 2 * places.h + places.c
    at = row_blocks(place, 4, size)
    chunk = min(64, size)

    def in_at(wide):
        return lambda n, share: (share * depth, pl.ds((n // extra) * wide, wide))

    def column_at(rows):
        def where(n, share):
            return (n // extra) * rows, pl.ds(pl.multiple_of(share * depth, depth), depth)

        return where

    w_in = WeightGather(copies, places, in_ref, in_here, in_at(3 * cols))
    w_out = WeightGather(copies, places, out_ref, out_here, column_at(cols))
    w_up = WeightGather(copies, places, up_ref, up_all, in_at(hidden))
    w_down = WeightGather(copies, places, down_ref, down_all, column_at(hidden))

    def spread_to(source, full, row):
        return Spread(copies, places, source, full, row, size)

    def normalized(values, gain, shift):
        mean = jnp.mean(values, axis=-1, keepdims=True)
        center = values - mean
        inverse = lax.rsqrt(jnp.mean(center * center, axis=-1, keepdims=True) + EPSILON)
        return (center * inverse * wide_ref[gain : gain + 1] + wide_ref[shift : shift + 1]).astype(BF16)

    def first_norm(r):
        def body(at_row):
            values = rows_ref[r, pl.ds(at_row, chunk), :].astype(F32)
            norm_here[pl.ds(r * length + at_row, chunk), :] = normalized(values, 0, 1)

        in_tiles(size, chunk, body)

    def project(source, row, target, row_to, kind):
        wide = (3 - kind) * cols

        def body(n, _):
            g, m = n // 4, lax.rem(n, 4)
            x = source[pl.ds(pl.multiple_of(row + m * size, size), size), :]
            w = in_here[:, pl.ds(pl.multiple_of((g * 3 + kind) * cols, HDIM), wide)]
            bias = bias_here[g, :1, kind * cols : 3 * cols]
            to = pl.ds(pl.multiple_of(g * wide, HDIM), wide)
            target[pl.ds(pl.multiple_of(row_to + m * size, size), size), to] = (dot(x, w) + bias).astype(BF16)
            return 0

        lax.fori_loop(0, 4 * groups, body, 0)

    def attention(r, segment):
        def head(n, _):
            g, i = n // per, lax.rem(n, per)
            base = g * 3 * cols + i * HDIM
            q_at, k_at, v_at = (pl.ds(pl.multiple_of(base + m * cols, HDIM), HDIM) for m in range(3))
            pre = g * 2 * cols + i * HDIM
            kp_at, vp_at = (pl.ds(pl.multiple_of(pre + m * cols, HDIM), HDIM) for m in range(2))
            out_at = pl.ds(pl.multiple_of(n * HDIM, HDIM), HDIM)
            for j in range(4):
                there = pl.ds(r * length + at[j], size)
                k_own[j * size : (j + 1) * size] = proj[there, k_at]
                v_own[j * size : (j + 1) * size] = proj[there, v_at]

            def run(before):
                for j in range(4):
                    there = pl.ds(r * length + at[j], size)
                    q = proj[there, q_at]
                    start, end = first_key(j, size, segment), j * size
                    parts = [
                        (
                            prefix_proj[m * length : (m + 1) * length, kp_at],
                            prefix_proj[m * length : (m + 1) * length, vp_at],
                            None,
                        )
                        for m in range(before)
                    ]
                    if end > start:
                        parts.append((k_own[start:end], v_own[start:end], None))
                    parts.append((k_own[end : end + size], v_own[end : end + size], causal(size)))
                    scores = []
                    for k, _, mask in parts:
                        s = dot(k, q, ((1,), (1,)))
                        scores.append(s if mask is None else jnp.where(mask, s, MASKED))
                    top = functools.reduce(
                        jnp.maximum, [jnp.max(s, axis=0, keepdims=True) for s in scores]
                    )
                    total = jnp.zeros((1, size), F32)
                    out = jnp.zeros((HDIM, size), F32)
                    for s, (_, v, _) in zip(scores, parts):
                        p = jnp.exp2((s - top) * scale)
                        total = total + jnp.sum(p, axis=0, keepdims=True)
                        out = out + dot(v, p.astype(BF16), ((0,), (0,)))
                    att[there, out_at] = (out / total).T.astype(BF16)
                    lse[r * heads + n, :, j * size : (j + 1) * size] = top * scale + jnp.log(total) * LOG2E

            if segment is not None:
                run(0)
            else:
                for m in range(groups):
                    pl.when(places.g == m)(functools.partial(run, m))
            return 0

        lax.fori_loop(0, heads, head, 0)

    to_core, to_far = [None, None], [None, None]

    def out_product(r):
        def away(t):
            c_send[r, pl.ds(t, size), :] = dot(
                att[pl.ds(r * length + 2 * size + t, size), :], out_here[...]
            ).astype(BF16)

        in_tiles(2 * size, size, away)
        to_core[r] = copies.remote(c_send.at[r], c_recv.at[r], places.to_c)

    def out_sum(r):
        to_core[r].wait_recv()

        def far(t):
            h_send[r, pl.ds(t, size), :] = (
                dot(att[pl.ds(r * length + size + t, size), :], out_here[...])
                + c_recv[r, pl.ds(size + t, size), :].astype(F32)
            ).astype(BF16)

        in_tiles(size, size, far)
        to_far[r] = copies.remote(h_send.at[r], h_recv.at[r], places.to_h)

        def own(t):
            resid[r, pl.ds(t, size), :] = (
                dot(att[pl.ds(r * length + t, size), :], out_here[...])
                + c_recv[r, pl.ds(t, size), :].astype(F32)
                + rows_ref[r, pl.ds(t, size), :].astype(F32)
                + wide_ref[2:3]
            )

        in_tiles(size, size, own)

    def second_norm(r):
        to_far[r].wait_recv()

        def body(t):
            values = resid[r, pl.ds(t, chunk), :] + h_recv[r, pl.ds(t, chunk), :].astype(F32)
            resid[r, pl.ds(t, chunk), :] = values
            normed2[r, pl.ds(t, chunk), :] = normalized(values, 3, 4)

        in_tiles(size, chunk, body)
        copies.local(resid.at[r], resid_out.at[r])
        copies.local(normed2.at[r], full2.at[pl.ds(r * length, size), :])
        return spread_to(normed2.at[r], full2, r * length)

    def clear(t):
        prefix_here[pl.ds(t, size), :] = jnp.zeros((size, width), BF16)

    places.barrier()
    w_in.own()
    w_in.turn()
    bias_steps = [
        copies.remote(bias_ref, bias_here.at[n // extra], places.further(o))
        for n, o in enumerate(places.offsets)
        if n and o[0] == 0
    ]
    bias_here[0] = bias_ref[...]
    first_norm(0)
    spread = [spread_to(norm_here.at[pl.ds(0, size), :], norm_here, 0), None]
    first_norm(1)
    spread[1] = spread_to(norm_here.at[pl.ds(length, size), :], norm_here, length)
    w_in.second(False)
    w_out.own()
    w_out.turn()
    spread[0].forward()
    w_out.second(False)
    w_in.turned()

    before, later = [], []
    for k in range(1, groups):
        row = (k - 1) * length
        slot = [prefix_here.at[pl.ds(row + n * size, size), :] for n in range(4)]
        copy = copies.remote(
            norm_here.at[pl.ds(0, size), :], slot[0], places.further((0, k)), tracked=False
        )
        pl.when(places.g + k < groups)(copy.start)
        before.append(copy)
        far = copies.remote(slot[0], slot[1], places.to_h, tracked=False)
        core = copies.remote(slot[0], slot[2], places.to_c, tracked=False)
        last = copies.remote(slot[1], slot[3], places.to_c, tracked=False)
        later.append((far, core, last))

    def for_prefix(action):
        for k in range(1, groups):
            pl.when(places.g >= k)(functools.partial(action, k - 1))

    def prefix_came(k):
        before[k].wait_recv()
        later[k][0].start()
        later[k][1].start()

    def prefix_forward(k):
        later[k][0].wait_recv()
        later[k][2].start()

    def prefix_finish(k):
        later[k][1].wait_recv()
        later[k][2].wait_recv()

    for k in range(1, groups):

        @pl.when(places.g < k)
        def _():
            in_tiles(length, size, lambda t: clear((k - 1) * length + t))

    spread[1].forward()
    w_in.second(True)
    w_in.finish(False)
    w_in.finish(True)
    w_up.own()
    w_out.turned()
    copies.local(in_here, in_all)
    for copy in bias_steps:
        copy.wait_recv()
    spread_cot = []
    for r in range(2):
        copies.local(cots_ref.at[r], full_cot.at[pl.ds(r * length, size), :])
        spread_cot.append(spread_to(cots_ref.at[r], full_cot, r * length))
    spread[1].finish()
    project(norm_here, length, proj, length, 0)
    w_out.second(True)
    attention(1, quarter)
    spread[0].finish()
    copies.local(norm_here, full1)
    w_up.second(False)
    w_out.finish(False)
    w_out.finish(True)
    copies.local(out_here, out_all)
    out_product(1)
    w_down.own()
    for_prefix(prefix_came)
    w_up.turn()
    project(norm_here, 0, proj, 0, 0)
    copies.local(proj, proj_out)
    out_sum(1)
    for_prefix(prefix_forward)
    w_down.second(False)
    spread_cot[0].forward()
    spread_cot[1].forward()
    for_prefix(prefix_finish)
    for k in range(1, groups):
        project(prefix_here, (k - 1) * length, prefix_proj, (k - 1) * length, 1)
    copies.local(prefix_here, prefix1)
    copies.local(prefix_proj, prefix_out)
    spread2 = [None, second_norm(1)]
    w_down.turn()
    attention(0, None)
    copies.local(att, att_out)
    copies.local(lse, lse_out)
    out_product(0)
    w_up.turned()
    out_sum(0)
    spread2[1].forward()
    w_up.second(True)
    spread2[0] = second_norm(0)
    w_down.turned()
    spread2[0].forward()
    w_up.finish(False)
    w_up.finish(True)
    w_down.second(True)
    w_down.finish(False)
    spread2[1].finish()
    spread2[0].finish()
    spread_cot[0].finish()
    spread_cot[1].finish()
    w_down.finish(True)

    for k in range(1, groups):
        far, core, last = later[k - 1]
        pl.when(places.g + k < groups)(before[k - 1].wait_send)

        @pl.when(places.g >= k)
        def _():
            far.wait_send()
            core.wait_send()
            last.wait_send()

    copies.finish()


def run_forward(split, quarter, rows, in_w, out_w, up_w, down_w, wide, bias, cots):
    extra, groups = split
    size, width = rows.shape[1:]
    length = 4 * size
    cols, hidden = in_w.shape[1] // 3, up_w.shape[1]
    all_cols = groups * cols
    heads = all_cols // HDIM
    shape = jax.ShapeDtypeStruct
    anywhere = pl.BlockSpec(memory_space=pl.ANY)
    inside = pl.BlockSpec(memory_space=pltpu.VMEM)
    count = extra * groups * 20 + 4 * groups + 24
    out_shape = [
        shape((width, 3 * all_cols), BF16),
        shape((all_cols, width), BF16),
        shape((width, groups * hidden), BF16),
        shape((groups * hidden, width), BF16),
        shape((groups,) + bias.shape, F32),
        shape((2 * length, width), BF16),
        shape(((groups - 1) * length, width), BF16),
        shape((2 * length, 3 * all_cols), BF16),
        shape(((groups - 1) * length, 2 * all_cols), BF16),
        shape((2 * length, all_cols), BF16),
        shape((2 * heads, 1, length), F32),
        shape((2, size, width), F32),
        shape((2 * length, width), BF16),
        shape((2 * length, width), BF16),
    ]
    return pl.pallas_call(
        functools.partial(layer_forward, extra, groups, quarter),
        in_specs=[inside] + [anywhere] * 4 + [inside] * 2 + [anywhere],
        out_specs=[inside if n == 4 else anywhere for n in range(len(out_shape))],
        out_shape=out_shape,
        scratch_shapes=[
            pltpu.VMEM((width, 3 * all_cols), BF16),
            pltpu.VMEM((all_cols, width), BF16),
            pltpu.VMEM((2 * length, width), BF16),
            pltpu.VMEM(((groups - 1) * length, width), BF16),
            pltpu.VMEM((2 * length, 3 * all_cols), BF16),
            pltpu.VMEM(((groups - 1) * length, 2 * all_cols), BF16),
            pltpu.VMEM((2 * length, all_cols), BF16),
            pltpu.VMEM((2 * heads, 1, length), F32),
            pltpu.VMEM((2, 2 * size, width), BF16),
            pltpu.VMEM((2, 2 * size, width), BF16),
            pltpu.VMEM((2, size, width), BF16),
            pltpu.VMEM((2, size, width), BF16),
            pltpu.VMEM((2, size, width), F32),
            pltpu.VMEM((2, size, width), BF16),
            pltpu.VMEM((length, HDIM), BF16),
            pltpu.VMEM((length, HDIM), BF16),
            pltpu.SemaphoreType.DMA((count,)),
            pltpu.SemaphoreType.DMA((count,)),
            pltpu.SemaphoreType.DMA((24,)),
        ],
        compiler_params=kernel_params(0),
        cost_estimate=pl.CostEstimate(flops=10**11, bytes_accessed=10**8, transcendentals=10**7),
    )(rows, in_w, out_w, up_w, down_w, wide, bias, cots)


class GradScatter:
    def __init__(self, copies, places, parts, land, turned, work, own, fetched, out):
        self.copies, self.places, self.parts = copies, places, parts
        self.land, self.turned, self.work, self.own = land, turned, work, own
        self.fetched, self.out = fetched, out
        self.half, self.cols = land.shape[2:]
        self.steps = {}

    def piece(self, n, i, j, part):
        places = self.places
        offset = places.offsets[n]
        index = offset[1] * places.extra * 4 + places.share(offset, i, j)
        return self.parts.at[index, pl.ds(part * self.half, self.half), :]

    def _send(self, n, key, source, partner):
        self.steps[n, key] = self.copies.remote(source, self.land.at[n, key], partner)

    def start(self, n):
        to_a, to_b = self.places.to_a, self.places.to_b
        self._send(n, 0, self.piece(n, 1, 1, 0), to_a)
        self._send(n, 1, self.piece(n, 1, 1, 1), to_b)
        self._send(n, 2, self.piece(n, 0, 1, 0), to_a)
        self._send(n, 3, self.piece(n, 1, 0, 1), to_b)

    def _fetch(self, sources):
        got = [self.fetched.at[m, : self.half, : self.cols] for m in range(len(sources))]
        loads = [self.copies.local(s, t, tracked=False) for s, t in zip(sources, got)]
        for load in loads:
            load.wait()
        return functools.reduce(jnp.add, [t[...].astype(F32) for t in got])

    def middle(self, n):
        self.steps[n, 0].wait_recv()
        self.work[n, 0] = self._fetch([self.land.at[n, 0], self.piece(n, 1, 0, 0)]).astype(BF16)
        self._send(n, 5, self.work.at[n, 0], self.places.to_b)
        self.steps[n, 1].wait_recv()
        self.work[n, 1] = self._fetch([self.land.at[n, 1], self.piece(n, 0, 1, 1)]).astype(BF16)
        self._send(n, 4, self.work.at[n, 1], self.places.to_a)

    def last(self, n):
        for part, keys in ((0, (2, 5)), (1, (3, 4))):
            for key in keys:
                self.steps[n, key].wait_recv()
            summed = self._fetch([self.piece(n, 0, 0, part)] + [self.land.at[n, k] for k in keys])
            rows = slice(part * self.half, (part + 1) * self.half)
            if n == 0:
                self.out[rows, :] = summed
            else:
                self.own[n - 1, rows, :] = summed.astype(BF16)
        if n:
            e, g = self.places.offsets[n]
            self.steps[n, "t"] = self.copies.remote(
                self.own.at[n - 1], self.turned.at[n - 1], self.places.further((-e, -g))
            )

    def total(self):
        for n in range(1, len(self.places.offsets)):
            self.steps[n, "t"].wait_recv()
            for part in range(2):
                rows = slice(part * self.half, (part + 1) * self.half)
                self.out[rows, :] += self._fetch(
                    [self.turned.at[n - 1, pl.ds(part * self.half, self.half), :]]
                )

    @staticmethod
    def landing(sources, rows, cols):
        return [
            jax.ShapeDtypeStruct((sources, 6, rows // 2, cols), BF16),
            jax.ShapeDtypeStruct((max(sources - 1, 1), rows, cols), BF16),
        ]

    @staticmethod
    def working(sources, rows, cols):
        return [
            pltpu.VMEM((sources, 2, rows // 2, cols), BF16),
            pltpu.VMEM((max(sources - 1, 1), rows, cols), BF16),
        ]


class Fold:
    def __init__(self, copies, places, c_send, c_recv, h_send, free, size):
        self.copies, self.places, self.size = copies, places, size
        self.c_send, self.c_recv, self.h_send, self.free = c_send, c_recv, h_send, free
        self.core = self.far = None

    def away(self, block):
        if self.core is not None:
            self.copies.sent(self.core)
        for t in range(2):
            self.c_send[t * self.size : (t + 1) * self.size, :] = block(2 + t).astype(BF16)
        if self.core is not None:
            pl.semaphore_wait(self.free, 1)
        self.core = self.copies.remote(self.c_send, self.c_recv, self.places.to_c)

    def kept(self, block, target, h_recv, more):
        size = self.size
        far = block(1)
        self.core.wait_recv()
        if self.far is not None:
            self.copies.sent(self.far)
        self.h_send[...] = (far + self.c_recv[size:, :].astype(F32)).astype(BF16)
        self.far = self.copies.remote(self.h_send, h_recv, self.places.to_h)
        target[...] = (block(0) + self.c_recv[:size, :].astype(F32)).astype(target.dtype)
        if more:
            pl.semaphore_signal(
                self.free, inc=1, device_id=self.places.to_c, device_id_type=pl.DeviceIdType.MESH
            )
        return self.far


class Stream:
    def __init__(self, copies, slots, blocks):
        self.copies, self.slots, self.blocks = copies, slots, blocks
        self.loads = {}
        self._load(0)

    def _load(self, n):
        if n < len(self.blocks):
            targets = [s[n % 2] for s in self.slots]
            self.loads[n] = [
                self.copies.local(s, t, tracked=False) for s, t in zip(self.blocks[n], targets)
            ]

    def take(self, n):
        for load in self.loads[n]:
            load.wait()
        self._load(n + 1)
        return n % 2


class Spread:
    def __init__(self, copies, places, source, full, row, size):
        self.copies, self.places, self.full, self.row, self.size = copies, places, full, row, size
        self.far = copies.remote(source, self.slot(1), places.to_h)
        self.core = copies.remote(source, self.slot(2), places.to_c)

    def slot(self, n):
        return self.full.at[pl.ds(self.row + n * self.size, self.size), :]

    def forward(self):
        self.far.wait_recv()
        self.last = self.copies.remote(self.slot(1), self.slot(3), self.places.to_c)

    def finish(self):
        self.core.wait_recv()
        self.last.wait_recv()


def middle_kernel(extra, groups, *refs):
    (
        full2, full_cot, up_all, down_all, resid, wide, bias_up,
        mixed, full_dres, grad_down, up_parts, sums, up_sums, act, dup, down_parts, land, turned,
        big, down, narrow, tiles, cots, c_send, c_recv, h_send, h_recv, low, stage_down, work, own,
        fetched, send_sem, recv_sem, near_sem, free,
    ) = refs
    size, width = mixed.shape[1:]
    length = 4 * size
    hidden, depth = grad_down.shape
    shares = extra * 4
    chunk = min(64, size)
    strip = min(512, hidden)
    places = Places(extra, groups)
    copies = Copies(send_sem, recv_sem, near_sem)
    sources = len(places.offsets)
    scatter = GradScatter(
        copies, places, down_parts, land, turned, work, own, fetched, grad_down
    )
    fold = Fold(copies, places, c_send, c_recv, h_send, free, size)
    folded = {}

    def load(source, target):
        return copies.local(source, target, tracked=False)

    def load_big(source):
        return load(source, big.at[: source.shape[0]])

    loading = [load_big(up_all), load(down_all, down)]
    tile_slots = [tiles.at[0], tiles.at[1]]
    cot_slots = [cots.at[0], cots.at[1]]
    narrow_slots = [narrow.at[0], narrow.at[1]]
    order = [(r, slot) for r in range(2) for slot in (2, 3, 1, 0)]
    where = [pl.ds(r * length + s * size, size) for r, s in order]
    stream = Stream(
        copies, [tile_slots, cot_slots], [[full2.at[w, :], full_cot.at[w, :]] for w in where]
    )
    places.barrier()
    sums[...] = jnp.zeros_like(sums)
    up_sums[...] = jnp.zeros_like(up_sums)
    for copy in loading:
        copy.wait()

    stored = {}
    for n, (r, slot) in enumerate(order):
        at = stream.take(n)
        if n >= 2:
            for copy in stored.pop(n - 2):
                copy.wait()
        act_at, dup_at = c_send.at[pl.ds(at * size, size), :], low.at[at]

        def body(g, _):
            columns = pl.ds(pl.multiple_of(g * strip, HDIM), strip)
            value = dot(tiles[at], big[:width, columns]) + bias_up[:1, columns]
            square = value * value
            tanh = jnp.tanh(0.7978845608028654 * value * (1.0 + 0.044715 * square))
            half = 0.5 * (1.0 + tanh)
            act_at[:, columns] = (value * half).astype(BF16)
            slope = half + 0.5 * value * (1.0 - tanh * tanh) * 0.7978845608028654 * (
                1.0 + 3 * 0.044715 * square
            )
            back = (dot(cots[at], down[columns, :], ((1,), (1,))) * slope).astype(BF16)
            dup_at[:, columns] = back
            up_sums[:, columns] += jnp.sum(back.astype(F32), axis=0, keepdims=True)
            return 0

        lax.fori_loop(0, groups * hidden // strip, body, 0)
        stored[n] = [
            load(act_at, act.at[where[n], :]),
            load(dup_at, dup.at[where[n], :]),
        ]
    for n in list(stored):
        for copy in stored.pop(n):
            copy.wait()

    own_cots = [load(full_cot.at[pl.ds(r * length, size), :], cots.at[r]) for r in range(2)]
    stream_dup = Stream(copies, [tile_slots], [[dup.at[w, :]] for w in where])

    def dup_block(r):
        def block(slot):
            at = stream_dup.take(order.index((r, slot)))
            return dot(tiles[at], big[:width], ((1,), (1,)))

        return block

    for r in range(2):
        fold.away(dup_block(r))
        folded[r] = fold.kept(dup_block(r), low.at[r], h_recv.at[r], True)

    def norm_back_rows(r):
        folded[r].wait_recv()

        def body(t):
            rows = pl.ds(t, chunk)
            grad = low[r, rows, :].astype(F32) + h_recv[r, rows, :].astype(F32)
            scaled, inverse = stats(resid[r, rows, :])
            cot = cots[r, rows, :].astype(F32)
            value = cot + norm_back(grad, scaled, inverse, wide[3:4])
            low[r, rows, :] = value.astype(BF16)
            for n, term in enumerate((value, grad * scaled, grad, cot)):
                sums[n : n + 1, :] += jnp.sum(term, axis=0, keepdims=True)

        in_tiles(size, chunk, body)
        copies.local(low.at[r], full_dres.at[pl.ds(r * length, size), :])
        return Spread(copies, places, low.at[r], full_dres, r * length, size)

    def columns_of(source):
        return [
            [source.at[:, pl.ds(d * depth, depth)]] for g in range(groups) for d in range(shares)
        ]

    turn_order = list(range(groups))[::-1]
    loading = load_big(act)
    stream_cot = Stream(copies, [narrow_slots], columns_of(full_cot))
    loading.wait()
    for copy in own_cots:
        copy.wait()
    put = {}
    count = 0
    spread = [None, None]

    def down_grad(g):
        nonlocal count
        for d in range(shares):
            at = stream_cot.take(count)
            slot = count % 2
            if count - 2 in put:
                put.pop(count - 2).wait()

            def body(t):
                left = big[: 2 * length, pl.ds(pl.multiple_of(g * hidden + t, HDIM), hidden // 2)]
                stage_down[slot, pl.ds(t, hidden // 2), :] = dot(
                    left, narrow[at], ((0,), (0,))
                ).astype(BF16)

            in_tiles(hidden, hidden // 2, body)
            put[count] = load(stage_down.at[slot], down_parts.at[g * shares + d])
            count += 1

    def of_group(g):
        return [n for n in range(sources) if places.offsets[n][1] == g][::-1]

    for step, g in enumerate(turn_order):
        down_grad(g)
        for n in list(put):
            put.pop(n).wait()
        for n in of_group(g):
            scatter.start(n)
        if step == 0:
            spread[0] = norm_back_rows(0)
    spread[1] = norm_back_rows(1)
    for n in of_group(turn_order[0]):
        scatter.middle(n)

    def act_block(r):
        def block(slot):
            return dot(big[r * length + slot * size : r * length + (slot + 1) * size, :], down[...])

        return block

    for r in range(2):
        fold.away(act_block(r))
        folded[2 + r] = fold.kept(act_block(r), mixed.at[r], h_recv.at[2 + r], r == 0)
        spread[r].forward()
        if r == 0:
            for g in turn_order[1:]:
                for n in of_group(g):
                    scatter.middle(n)
    for n in of_group(turn_order[0]):
        if n:
            scatter.last(n)

    loading = load_big(dup)
    stream_two = Stream(copies, [narrow_slots], columns_of(full2))
    stage_up = [down.at[pl.ds(n * depth, depth), pl.ds(0, hidden)] for n in range(2)]
    loading.wait()
    put_up = {}
    done = 0
    for g in turn_order:
        for d in range(shares):
            at = stream_two.take(done)
            if done >= 2:
                put_up.pop(done - 2).wait()
            stage_up[done % 2][...] = dot(
                narrow[at], big[: 2 * length, g * hidden : (g + 1) * hidden], ((0,), (0,))
            ).astype(BF16)
            put_up[done] = load(stage_up[done % 2], up_parts.at[g * shares + d])
            done += 1
    for r in range(2):
        folded[2 + r].wait_recv()

        def add(t):
            rows = pl.ds(t, chunk)
            mixed[r, rows, :] = (
                resid[r, rows, :]
                + mixed[r, rows, :].astype(F32)
                + h_recv[2 + r, rows, :].astype(F32)
                + wide[5:6]
            ).astype(BF16)

        in_tiles(size, chunk, add)
    for copy in put_up.values():
        copy.wait()
    spread[0].finish()
    spread[1].finish()
    for g in turn_order:
        for n in of_group(g):
            if (n, "t") not in scatter.steps:
                scatter.last(n)
    scatter.total()
    copies.finish()


def attention_back_rows(places, row, length, size, heads, per, segment, refs, column):
    (
        proj, prefix_proj, att, datt, lse, dproj, dprefix,
        k_own, v_own, dk_own, dv_own, dk_pre, dv_pre,
    ) = refs
    scale = HDIM**-0.5 * LOG2E
    factor = HDIM**-0.5
    at = row_blocks(2 * places.h + places.c, 4, size)
    base = row * length

    def head(n, _):
        q_at, k_at, v_at = (pl.ds(column(n, 3, m), HDIM) for m in range(3))
        kp_at, vp_at = (pl.ds(column(n, 2, m), HDIM) for m in range(2))
        out_at = pl.ds(pl.multiple_of(n * HDIM, HDIM), HDIM)
        for j in range(4):
            there = pl.ds(base + at[j], size)
            k_own[j * size : (j + 1) * size] = proj[there, k_at]
            v_own[j * size : (j + 1) * size] = proj[there, v_at]
        dk_own[...] = jnp.zeros_like(dk_own)
        dv_own[...] = jnp.zeros_like(dv_own)
        if segment is None:
            dk_pre[...] = jnp.zeros_like(dk_pre)
            dv_pre[...] = jnp.zeros_like(dv_pre)

        def run(before):
            for j in range(4):
                there = pl.ds(base + at[j], size)
                q = proj[there, q_at]
                do = datt[there, out_at]
                product = do.astype(F32) * att[there, out_at].astype(F32)
                delta = lax.dot_general(
                    jnp.ones((8, HDIM), F32),
                    product,
                    (((1,), (1,)), ((), ())),
                    precision=lax.Precision.HIGHEST,
                    preferred_element_type=F32,
                )[:1]
                log_total = lse[row * heads + n, :, j * size : (j + 1) * size]
                start, end = first_key(j, size, segment), j * size
                parts = []
                step = min(512, length)
                for m in range(0, before * length, step):
                    rows = slice(m, m + step)
                    parts.append(
                        (prefix_proj[rows, kp_at], prefix_proj[rows, vp_at], dk_pre, dv_pre, rows, None)
                    )
                if end > start:
                    rows = slice(start, end)
                    parts.append((k_own[rows], v_own[rows], dk_own, dv_own, rows, None))
                rows = slice(end, end + size)
                parts.append((k_own[rows], v_own[rows], dk_own, dv_own, rows, causal(size)))
                dq = jnp.zeros((HDIM, size), F32)
                for k, v, dk, dv, rows, mask in parts:
                    s = dot(k, q, ((1,), (1,))) * scale - log_total
                    p = jnp.exp2(s if mask is None else jnp.where(mask, s, MASKED))
                    dscores = (p * (dot(v, do, ((1,), (1,))) - delta)).astype(BF16)
                    dv[rows] += dot(p.astype(BF16), do)
                    dk[rows] += dot(dscores, q)
                    dq = dq + dot(k, dscores, ((0,), (0,)))
                dproj[there, q_at] = (dq * factor).T.astype(BF16)

        if segment is not None:
            run(0)
        else:
            for m in range(places.groups):
                pl.when(places.g == m)(functools.partial(run, m))
            dprefix[:, q_at] = jnp.zeros_like(dk_pre, dtype=BF16)
            dprefix[:, k_at] = (dk_pre[...] * factor).astype(BF16)
            dprefix[:, v_at] = dv_pre[...].astype(BF16)
        for j in range(4):
            rows = slice(j * size, (j + 1) * size)
            there = pl.ds(base + at[j], size)
            dproj[there, k_at] = (dk_own[rows] * factor).astype(BF16)
            dproj[there, v_at] = dv_own[rows].astype(BF16)
        return 0

    lax.fori_loop(0, heads, head, 0)


def last_kernel(extra, groups, quarter, *refs):
    (
        proj_in, prefix_in, att_in, full_dres, out_all, in_all, full1, prefix1, up_parts, lse,
        grad_in, grad_out, grad_up, dnormed1, h_recv, returned, dproj_sums,
        in_parts, out_parts, land_in, turned_in, land_out, turned_out, land_up, turned_up,
        proj, prefix_proj, att, datt, dprefix, w_in, w_out, spare,
        k_own, v_own, dk_own, dv_own, dk_pre, dv_pre,
        c_send, c_recv, h_send, back, stage_in, stage_out,
        work_in, own_in, work_out, own_out, work_up, own_up, fetched, send_sem, recv_sem, near_sem, free,
    ) = refs
    size, width = dnormed1.shape[1:]
    length = 4 * size
    cols = grad_in.shape[1] // 3
    depth = grad_in.shape[0]
    wide = 3 * cols
    heads = groups * cols // HDIM
    per = cols // HDIM
    shares = extra * 4
    places = Places(extra, groups)
    copies = Copies(send_sem, recv_sem, near_sem)
    sources = len(places.offsets)
    far_first = list(range(sources))[::-1]
    up = GradScatter(
        copies, places, up_parts, land_up, turned_up, work_up, own_up, fetched, grad_up
    )
    out = GradScatter(
        copies, places, out_parts, land_out, turned_out, work_out, own_out, fetched, grad_out
    )
    into = GradScatter(
        copies, places, in_parts, land_in, turned_in, work_in, own_in, fetched, grad_in
    )
    dproj = proj
    folds = Fold(copies, places, c_send, c_recv, h_send, free, size)
    folded = {}

    def column(n, parts, m):
        return pl.multiple_of((n // per * parts + m) * cols + lax.rem(n, per) * HDIM, HDIM)

    here = [
        copies.local(s, t, tracked=False)
        for s, t in (
            (out_all, w_out), (proj_in, proj), (prefix_in, prefix_proj), (att_in, att), (in_all, w_in),
        )
    ]
    order = [(r, slot) for r in range(2) for slot in range(4)]
    tiles = [c_send.at[pl.ds(n * size, size), :] for n in range(2)]
    stream = Stream(
        copies, [tiles], [[full_dres.at[pl.ds(r * length + s * size, size), :]] for r, s in order]
    )
    places.barrier()
    for n in far_first:
        up.start(n)
    for copy in here:
        copy.wait()

    def attended_grad(r):
        for slot in range(4):
            at = stream.take(r * 4 + slot)
            datt[r * length + slot * size : r * length + (slot + 1) * size, :] = dot(
                tiles[at][...], w_out[...], ((1,), (1,))
            ).astype(BF16)

    def attention_back(r, segment):
        attention_back_rows(
            places, r, length, size, heads, per, segment,
            (
                proj, prefix_proj, att, datt, lse, dproj, dprefix,
                k_own, v_own, dk_own, dv_own, dk_pre, dv_pre,
            ),
            column,
        )

    def block_of(source, row):
        def block(slot):
            rows = source[row + slot * size : row + (slot + 1) * size, :]
            return dot(rows, w_in[...], ((1,), (1,)))

        return block

    def fold(number, source, row, target, more=True):
        folds.away(block_of(source, row))
        folded[number] = folds.kept(block_of(source, row), target, h_recv.at[number], more)

    attended_grad(0)
    attended_grad(1)
    attention_back(0, None)
    for n in far_first:
        up.middle(n)
    for k in range(1, groups):
        fold(1 + k, dprefix, (k - 1) * length, back.at[k - 1])
    attention_back(1, quarter)
    for n in far_first:
        up.last(n)

    home = []
    for k in range(1, groups):
        folded[1 + k].wait_recv()
        back[k - 1] = (back[k - 1].astype(F32) + h_recv[1 + k].astype(F32)).astype(BF16)
        copy = copies.remote(
            back.at[k - 1], returned.at[k - 1], places.further((0, -k)), tracked=False
        )
        pl.when(places.g >= k)(copy.start)
        home.append(copy)

    slots = [datt.at[:, pl.ds(0, depth)], spare]
    prefix_rows = prefix1.shape[0]
    slots_pre = [prefix_proj.at[:, pl.ds(n * depth, depth)] for n in range(2)]

    class Columns:
        def __init__(self, sources_and_slots, count):
            self.pairs, self.count, self.loads = sources_and_slots, count, {}
            self._load(0)

        def _load(self, n):
            if n < self.count:
                d = n % shares
                self.loads[n] = [
                    copies.local(s.at[:, pl.ds(d * depth, depth)], slot[n % 2], tracked=False)
                    for s, slot in self.pairs
                ]

        def take(self, n):
            for load in self.loads[n]:
                load.wait()
            self._load(n + 1)
            return n % 2

    put = []

    def store(stage, target):
        put.append(copies.local(stage, target, tracked=False))

    def drain(left):
        while len(put) > left:
            put.pop(0).wait()

    stream_in = Columns([(full1, slots), (prefix1, slots_pre)], groups * shares)
    count = 0
    for g in range(groups)[::-1]:
        for d in range(shares):
            at = stream_in.take(count)
            drain(1)
            which = pl.ds(g * wide, wide)
            value = dot(slots[at][...], dproj[:, which], ((0,), (0,)))
            if prefix_rows:
                value = value + dot(slots_pre[at][...], dprefix[:, which], ((0,), (0,)))
            stage_in[count % 2] = value.astype(BF16)
            store(stage_in.at[count % 2], in_parts.at[g * shares + d])
            count += 1
        drain(0)
        for n in far_first:
            if places.offsets[n][1] == g:
                into.start(n)
    stream_out = Columns([(full_dres, slots)], shares)
    for d in range(shares):
        at = stream_out.take(d)
        for g in range(groups):
            drain(1)
            slot = (d * groups + g) % 2
            stage_out[slot] = dot(
                att[:, g * cols : (g + 1) * cols], slots[at][...], ((0,), (0,))
            ).astype(BF16)
            store(stage_out.at[slot], out_parts.at[g * shares + d])
    drain(0)
    for n in far_first:
        out.start(n)
    fold(0, dproj, 0, dnormed1.at[0])
    for n in far_first:
        if places.offsets[n][1] == groups - 1:
            into.middle(n)
    fold(1, dproj, length, dnormed1.at[1], False)
    for n in far_first:
        if places.offsets[n][1] != groups - 1:
            into.middle(n)
    for n in far_first:
        if n and places.offsets[n][1] == groups - 1:
            into.last(n)
    for n in far_first:
        out.middle(n)
    dproj_sums[...] = jnp.zeros_like(dproj_sums)

    def add_rows(t):
        dproj_sums[0:1, :] += jnp.sum(dproj[pl.ds(t, size), :].astype(F32), axis=0, keepdims=True)

    in_tiles(2 * length, size, add_rows)

    def add_prefix(t):
        dproj_sums[1:2, :] += jnp.sum(dprefix[pl.ds(t, size), :].astype(F32), axis=0, keepdims=True)

    in_tiles(prefix_rows, size, add_prefix)
    up.total()
    for n in far_first:
        if (n, "t") not in into.steps:
            into.last(n)
    for n in far_first:
        out.last(n)
    for r in range(2):
        folded[r].wait_recv()
    out.total()
    into.total()
    for k in range(1, groups):
        pl.when(places.g + k < groups)(home[k - 1].wait_recv)
        pl.when(places.g >= k)(home[k - 1].wait_send)
    copies.finish()


def kernel_params(number):
    return pltpu.CompilerParams(
        collective_id=number, has_side_effects=True, vmem_limit_bytes=KERNEL_VMEM
    )


def run_middle(split, full2, full_cot, up_all, down_all, resid, wide, bias_up, hidden, depth):
    extra, groups = split
    sources = extra * groups
    size, width = resid.shape[1:]
    length = 4 * size
    all_hidden = groups * hidden
    shape = jax.ShapeDtypeStruct
    anywhere = pl.BlockSpec(memory_space=pl.ANY)
    inside = pl.BlockSpec(memory_space=pltpu.VMEM)
    shares = sources * 4
    return pl.pallas_call(
        functools.partial(middle_kernel, extra, groups),
        in_specs=[anywhere] * 4 + [inside] * 3,
        out_specs=[inside, anywhere, inside, anywhere, inside, inside] + [anywhere] * 5,
        out_shape=[
            shape((2, size, width), BF16),
            shape((2 * length, width), BF16),
            shape((hidden, depth), F32),
            shape((shares, depth, hidden), BF16),
            shape((4, width), F32),
            shape((1, all_hidden), F32),
            shape((2 * length, all_hidden), BF16),
            shape((2 * length, all_hidden), BF16),
            shape((shares, hidden, depth), BF16),
        ]
        + GradScatter.landing(sources, hidden, depth),
        scratch_shapes=[
            pltpu.VMEM((max(width, 2 * length), all_hidden), BF16),
            pltpu.VMEM((all_hidden, width), BF16),
            pltpu.VMEM((2, 2 * length, depth), BF16),
            pltpu.VMEM((2, size, width), BF16),
            pltpu.VMEM((2, size, width), BF16),
            pltpu.VMEM((2 * size, width), BF16),
            pltpu.VMEM((2 * size, width), BF16),
            pltpu.VMEM((size, width), BF16),
            pltpu.VMEM((4, size, width), BF16),
            pltpu.VMEM((2, size, width), BF16),
            pltpu.VMEM((2, hidden, depth), BF16),
        ]
        + GradScatter.working(sources, hidden, depth)
        + [
            pltpu.VMEM((3, hidden // 2, depth), BF16),
            pltpu.SemaphoreType.DMA((sources * 8 + 16,)),
            pltpu.SemaphoreType.DMA((sources * 8 + 16,)),
            pltpu.SemaphoreType.DMA((sources * 16 + 6 * shares + 80,)),
            pltpu.SemaphoreType.REGULAR,
        ],
        compiler_params=kernel_params(1),
        cost_estimate=pl.CostEstimate(flops=10**11, bytes_accessed=10**8, transcendentals=10**6),
    )(full2, full_cot, up_all, down_all, resid, wide, bias_up)


def run_last(split, quarter, proj, prefix_proj, att, full_dres, out_all, in_all, full1, prefix1, up_parts, lse):
    extra, groups = split
    sources = extra * groups
    shares = sources * 4
    length, width = full1.shape[0] // 2, full1.shape[1]
    size = length // 4
    cols = att.shape[1] // groups
    depth, hidden = up_parts.shape[1:]
    wide, all_wide = 3 * cols, 3 * cols * groups
    prefix_rows = prefix1.shape[0]
    shape = jax.ShapeDtypeStruct
    anywhere = pl.BlockSpec(memory_space=pl.ANY)
    inside = pl.BlockSpec(memory_space=pltpu.VMEM)
    heads_rows = [pltpu.VMEM((length, HDIM), BF16)] * 2 + [pltpu.VMEM((length, HDIM), F32)] * 2
    return pl.pallas_call(
        functools.partial(last_kernel, extra, groups, quarter),
        in_specs=[anywhere] * 9 + [inside],
        out_specs=[inside] * 7 + [anywhere] * 8,
        out_shape=[
            shape((depth, wide), F32),
            shape((cols, depth), F32),
            shape((depth, hidden), F32),
            shape((2, size, width), BF16),
            shape((1 + groups, size, width), BF16),
            shape((max(groups - 1, 1), size, width), BF16),
            shape((2, all_wide), F32),
            shape((shares, depth, wide), BF16),
            shape((shares, cols, depth), BF16),
        ]
        + GradScatter.landing(sources, depth, wide)
        + GradScatter.landing(sources, cols, depth)
        + GradScatter.landing(sources, depth, hidden),
        scratch_shapes=[
            pltpu.VMEM(proj.shape, BF16),
            pltpu.VMEM(prefix_proj.shape, BF16),
            pltpu.VMEM(att.shape, BF16),
            pltpu.VMEM(att.shape, BF16),
            pltpu.VMEM((prefix_rows, all_wide), BF16),
            pltpu.VMEM(in_all.shape, BF16),
            pltpu.VMEM(out_all.shape, BF16),
            pltpu.VMEM((2 * length, depth), BF16),
        ]
        + heads_rows
        + [pltpu.VMEM((prefix_rows, HDIM), F32)] * 2
        + [
            pltpu.VMEM((2 * size, width), BF16),
            pltpu.VMEM((2 * size, width), BF16),
            pltpu.VMEM((size, width), BF16),
            pltpu.VMEM((max(groups - 1, 1), size, width), BF16),
            pltpu.VMEM((2, depth, wide), BF16),
            pltpu.VMEM((2, cols, depth), BF16),
        ]
        + GradScatter.working(sources, depth, wide)
        + GradScatter.working(sources, cols, depth)
        + GradScatter.working(sources, depth, hidden)
        + [
            pltpu.VMEM((3, depth // 2, max(wide, hidden, depth)), BF16),
            pltpu.SemaphoreType.DMA((sources * 24 + 4 * groups + 16,)),
            pltpu.SemaphoreType.DMA((sources * 24 + 4 * groups + 16,)),
            pltpu.SemaphoreType.DMA((sources * 48 + 10 * shares + 32,)),
            pltpu.SemaphoreType.REGULAR,
        ],
        compiler_params=kernel_params(2),
        cost_estimate=pl.CostEstimate(flops=10**11, bytes_accessed=10**8, transcendentals=10**7),
    )(proj, prefix_proj, att, full_dres, out_all, in_all, full1, prefix1, up_parts, lse)


def local(
    tokens,
    segments,
    first_gain,
    first_shift,
    in_weight,
    in_bias,
    out_weight,
    out_bias,
    second_gain,
    second_shift,
    up_weight,
    up_bias,
    down_weight,
    down_bias,
    cotangent,
):
    extra, groups = lax.axis_size("e"), lax.axis_size("g")
    split = (extra, groups)
    size, width = tokens.shape[1:]
    cols, hidden, depth = in_weight.shape[2], up_weight.shape[1], in_weight.shape[0]
    quarter = segments.shape[1] // 4

    single = jnp.where(segments[0, -1] == 0, 0, 1)
    order = (single, 1 - single)

    def pick(x):
        return [lax.dynamic_index_in_dim(x, r, 0, keepdims=False) for r in order]

    def unpick(first, second):
        return jnp.where(single == 0, jnp.stack([first, second]), jnp.stack([second, first]))

    rows = [r.astype(F32) for r in pick(tokens)]
    cots = pick(cotangent)

    no_bias = jnp.zeros_like(in_bias[0])
    biases = jnp.concatenate([in_bias[0], no_bias, in_bias[1], up_bias])
    biases = jnp.broadcast_to(biases, (8, biases.shape[0]))
    wide = jnp.stack([first_gain, first_shift, out_bias, second_gain, second_shift, down_bias])
    (
        in_all, out_all, up_all, down_all, biases, full1, prefix1, proj, proj_prefix, attended, lse,
        resid, full2, full_cot,
    ) = run_forward(
        split,
        quarter,
        jnp.stack(pick(tokens)),
        in_weight.reshape(depth, 3 * cols),
        out_weight,
        up_weight,
        down_weight,
        wide,
        biases,
        jnp.stack(cots),
    )
    bias_up = biases[:, 0, 3 * cols :].reshape(1, -1)
    length = 4 * size
    scaled1, inverse1 = zip(*[stats(x) for x in rows])

    mixed, full_dres, grad_down, up_parts, sums2, grad_up_bias = run_middle(
        split, full2, full_cot, up_all, down_all, resid, wide, bias_up, hidden, depth
    )[:6]
    dres = [full_dres[r * length : r * length + size].astype(F32) for r in range(2)]

    grad_in, grad_out, grad_up, kept, halves_far, returned, dproj_sums = run_last(
        split, quarter, proj, proj_prefix, attended, full_dres, out_all, in_all, full1, prefix1, up_parts, lse
    )[:7]
    dnormed1 = [kept[r].astype(F32) + halves_far[r].astype(F32) for r in range(2)]
    at_g = lax.axis_index("g")
    for k in range(1, groups):
        dnormed1[0] += jnp.where(at_g + k < groups, returned[k - 1].astype(F32), 0.0)
    grad_in = grad_in.reshape(in_weight.shape)
    tokens_grad, sums1 = [], []
    for r in range(2):
        tokens_grad.append(
            (dres[r] + norm_back(dnormed1[r], scaled1[r], inverse1[r], first_gain)).astype(BF16)
        )
        sums1.append(jnp.stack([jnp.sum(dnormed1[r] * scaled1[r], 0), jnp.sum(dnormed1[r], 0)]))

    sums = dproj_sums.reshape(2, groups, 3, cols)
    grad_q_bias = sums[0, :, 0]
    grad_v_bias = sums[0, :, 2] + sums[1, :, 2]

    def to_owner(x):
        share = x.reshape(groups, -1)
        return functools.reduce(
            jnp.add,
            [share[0]] + [turn(share[g], split, (0, (-g) % groups)) for g in range(1, groups)],
        )

    def sum_over(x, axes):
        for axis in axes:
            x = sum_axis(x, axis)
        return x

    early = sum_over(sums2, ("c", "h", "g") + DP)
    grad_up_bias = sum_over(to_owner(grad_up_bias), DP)
    late = sum_over(sums1[0] + sums1[1], ("c", "h", "g") + DP)
    grad_in_bias = sum_over(jnp.stack([to_owner(grad_q_bias), to_owner(grad_v_bias)]), DP)
    return (
        unpick(*mixed),
        unpick(*tokens_grad),
        late[0],
        late[1],
        grad_in,
        grad_in_bias,
        grad_out,
        early[0],
        early[1],
        early[2],
        grad_up,
        grad_up_bias,
        grad_down,
        early[3],
    )


def solution(mesh):
    dp, tp = mesh.shape["dp"], mesh.shape["tp"]
    split = Mesh(mesh.devices.reshape(dp // 4, 2, 2, tp // 4, 2, 2), DP + TP)
    in_specs = (
        P(DP, TP, None),
        P(DP, None),
        P(),
        P(),
        P(DP, None, TP),
        P(None, TP),
        P(TP, DP),
        P(),
        P(),
        P(),
        P(DP, TP),
        P(TP),
        P(TP, DP),
        P(),
        P(DP, TP, None),
    )
    out_specs = (
        P(DP, TP, None),
        P(DP, TP, None),
        P(),
        P(),
        P(DP, None, TP),
        P(None, TP),
        P(TP, DP),
        P(),
        P(),
        P(),
        P(DP, TP),
        P(TP),
        P(TP, DP),
        P(),
    )
    return jax.shard_map(local, mesh=split, in_specs=in_specs, out_specs=out_specs, check_vma=False)
```

```python
import functools

import jax
import jax.numpy as jnp
from jax import lax
from jax.experimental import pallas as pl
from jax.experimental.pallas import tpu as pltpu
from jax.sharding import Mesh, PartitionSpec as P

HDIM = 128
EPSILON = 1e-05
MASKED = -1e30
LOG2E = 1.4426950408889634
F32 = jnp.float32
BF16 = jnp.bfloat16
VMEM_LIMIT = 48 * 1024 * 1024
KERNEL_VMEM = 63 * 1024 * 1024
DP = ("e", "b", "a")
TP = ("g", "h", "c")
SLOTS = (0, 2, 1, 3)


def dot(x, y, contract=((1,), (0,))):
    return lax.dot_general(x, y, (contract, ((), ())), preferred_element_type=F32)


def stats(rows):
    mean = jnp.mean(rows, axis=-1, keepdims=True)
    center = rows - mean
    inverse = lax.rsqrt(jnp.mean(center * center, axis=-1, keepdims=True) + EPSILON)
    return center * inverse, inverse


def norm_back(grad_normed, scaled, inverse, gain):
    weighted = grad_normed * gain
    return inverse * (
        weighted
        - jnp.mean(weighted, axis=-1, keepdims=True)
        - scaled * jnp.mean(weighted * scaled, axis=-1, keepdims=True)
    )


def row_blocks(place, count, size):
    found = []
    for j in range(count):
        other = jnp.bitwise_xor(place, j)
        slot = (other >> 1) + 2 * (other & 1)
        found.append(pl.multiple_of(slot * size, size))
    return found


def causal(size):
    keys = lax.broadcasted_iota(jnp.int32, (size, size), 0)
    queries = lax.broadcasted_iota(jnp.int32, (size, size), 1)
    return keys <= queries


def first_key(block, size, segment):
    return 0 if segment is None else block * size // segment * segment


class Remote:
    def __init__(self, copies, number, source, target, device):
        self.copies, self.number, self.source, self.target = copies, number, source, target
        self.device = device

    def _copy(self):
        return pltpu.make_async_remote_copy(
            src_ref=self.source,
            dst_ref=self.target,
            send_sem=self.copies.send.at[self.number],
            recv_sem=self.copies.recv.at[self.number],
            device_id=self.device,
            device_id_type=pl.DeviceIdType.MESH,
        )

    def start(self):
        self._copy().start()

    def wait_send(self):
        self._copy().wait_send()

    def wait_recv(self):
        self._copy().wait_recv()


class Copies:
    def __init__(self, send, recv, near):
        self.send, self.recv, self.near = send, recv, near
        self.remotes, self.locals = 0, 0
        self.open_sends, self.open_locals = [], []

    def remote(self, source, target, device, tracked=True):
        copy = Remote(self, self.remotes, source, target, device)
        self.remotes += 1
        if tracked:
            copy.start()
            self.open_sends.append(copy)
        return copy

    def local(self, source, target, tracked=True):
        copy = pltpu.make_async_copy(source, target, self.near.at[self.locals])
        self.locals += 1
        copy.start()
        if tracked:
            self.open_locals.append(copy)
        return copy

    def sent(self, copy):
        copy.wait_send()
        self.open_sends = [c for c in self.open_sends if c is not copy]

    def finish(self):
        for copy in self.open_sends:
            copy.wait_send()
        for copy in self.open_locals:
            copy.wait()


class Places:
    def __init__(self, extra, groups):
        self.extra, self.groups = extra, groups
        self.e, self.b, self.a, self.g, self.h, self.c = (lax.axis_index(n) for n in DP + TP)
        self.to_a, self.to_b = {"a": 1 - self.a}, {"b": 1 - self.b}
        self.to_h, self.to_c = {"h": 1 - self.h}, {"c": 1 - self.c}
        self.offsets = [(e, g) for g in range(groups) for e in range(extra)]

    def further(self, offset):
        return {
            "e": lax.rem(self.e + offset[0] + self.extra, self.extra),
            "g": lax.rem(self.g + offset[1] + self.groups, self.groups),
        }

    def share(self, offset, i, j):
        e = lax.rem(self.e - offset[0] + self.extra, self.extra)
        b = self.b if i == 0 else 1 - self.b
        a = self.a if j == 0 else 1 - self.a
        return e * 4 + b * 2 + a

    def barrier(self):
        semaphore = pltpu.get_barrier_semaphore()
        partners = [self.to_a, self.to_b, self.to_h, self.to_c]
        partners += [self.further(o) for o in self.offsets[1:]]
        for partner in partners:
            pl.semaphore_signal(
                semaphore, inc=1, device_id=partner, device_id_type=pl.DeviceIdType.MESH
            )
        pl.semaphore_wait(semaphore, len(partners))


class WeightGather:
    def __init__(self, copies, places, shard, full, at):
        self.copies, self.places, self.shard, self.full, self.at = copies, places, shard, full, at
        self.rows = shard.shape[0]
        self.steps = {}

    def piece(self, n, i, j, low=0, count=None):
        place = self.at(n, self.places.share(self.places.offsets[n], i, j))
        return self.full.at[
            pl.ds(place[0] + low, self.rows if count is None else count), place[1]
        ]

    def own(self):
        self.here = self.copies.local(self.shard, self.piece(0, 0, 0), tracked=False)
        self._first(0, self.shard)

    def turn(self):
        for n, offset in enumerate(self.places.offsets):
            if n:
                e, g = offset
                share = self.places.share((0, 0), 0, 0)
                place = self.at(n, share)
                target = self.full.at[pl.ds(place[0], self.rows), place[1]]
                self.steps["t", n] = self.copies.remote(
                    self.shard, target, self.places.further(offset)
                )

    def _first(self, n, source):
        piece = self.piece(n, 0, 0)
        self.steps["a", n] = self.copies.remote(source, piece, self.places.to_a)
        self.steps["b", n] = self.copies.remote(source, piece, self.places.to_b)

    def turned(self):
        for n in range(1, len(self.places.offsets)):
            self.steps["t", n].wait_recv()
            self._first(n, self.piece(n, 0, 0))

    def second(self, far):
        half = self.rows // 2
        for n in range(1, len(self.places.offsets)) if far else (0,):
            self.steps["a", n].wait_recv()
            top = self.piece(n, 0, 1, 0, half)
            self.steps["ab", n] = self.copies.remote(top, top, self.places.to_b)
            self.steps["b", n].wait_recv()
            low = self.piece(n, 1, 0, half, half)
            self.steps["ba", n] = self.copies.remote(low, low, self.places.to_a)

    def finish(self, far):
        if not far:
            self.here.wait()
        for n in range(1, len(self.places.offsets)) if far else (0,):
            self.steps["ab", n].wait_recv()
            self.steps["ba", n].wait_recv()


def in_tiles(rows, size, body):
    lax.fori_loop(0, rows // size, lambda n, _: (body(pl.multiple_of(n * size, size)), 0)[1], 0)


def layer_forward(extra, groups, quarter, *refs):
    (
        rows_ref, in_ref, out_ref, up_ref, down_ref, wide_ref, bias_ref,
        in_all, out_all, up_all, down_all, bias_all, full1, prefix1, proj_out, prefix_out, att_out,
        lse_out, resid_out, full2,
        in_here, out_here, norm_here, prefix_here, proj, prefix_proj, att, lse, c_send, c_recv, h_send,
        h_recv, resid, normed2, k_own, v_own, send_sem, recv_sem, near_sem,
    ) = refs
    size, width = rows_ref.shape[1:]
    length = 4 * size
    cols = in_ref.shape[1] // 3
    hidden, depth = up_ref.shape[1], up_ref.shape[0]
    heads = groups * cols // HDIM
    per = cols // HDIM
    scale = HDIM**-0.5 * LOG2E
    places = Places(extra, groups)
    copies = Copies(send_sem, recv_sem, near_sem)
    bias_here = bias_all
    place = 2 * places.h + places.c
    at = row_blocks(place, 4, size)
    chunk = min(64, size)

    def in_at(wide):
        return lambda n, share: (share * depth, pl.ds((n // extra) * wide, wide))

    def column_at(rows):
        def where(n, share):
            return (n // extra) * rows, pl.ds(pl.multiple_of(share * depth, depth), depth)

        return where

    w_in = WeightGather(copies, places, in_ref, in_here, in_at(3 * cols))
    w_out = WeightGather(copies, places, out_ref, out_here, column_at(cols))
    w_up = WeightGather(copies, places, up_ref, up_all, in_at(hidden))
    w_down = WeightGather(copies, places, down_ref, down_all, column_at(hidden))

    def spread_to(source, full, row):
        return Spread(copies, places, source, full, row, size)

    def normalized(values, gain, shift):
        mean = jnp.mean(values, axis=-1, keepdims=True)
        center = values - mean
        inverse = lax.rsqrt(jnp.mean(center * center, axis=-1, keepdims=True) + EPSILON)
        return (center * inverse * wide_ref[gain : gain + 1] + wide_ref[shift : shift + 1]).astype(BF16)

    def first_norm(r):
        def body(at_row):
            values = rows_ref[r, pl.ds(at_row, chunk), :].astype(F32)
            norm_here[pl.ds(r * length + at_row, chunk), :] = normalized(values, 0, 1)

        in_tiles(size, chunk, body)

    def project(source, row, target, row_to, kind):
        wide = (3 - kind) * cols

        def body(n, _):
            g, m = n // 4, lax.rem(n, 4)
            x = source[pl.ds(pl.multiple_of(row + m * size, size), size), :]
            w = in_here[:, pl.ds(pl.multiple_of((g * 3 + kind) * cols, HDIM), wide)]
            bias = bias_here[g, :1, kind * cols : 3 * cols]
            to = pl.ds(pl.multiple_of(g * wide, HDIM), wide)
            target[pl.ds(pl.multiple_of(row_to + m * size, size), size), to] = (dot(x, w) + bias).astype(BF16)
            return 0

        lax.fori_loop(0, 4 * groups, body, 0)

    def attention(r, segment):
        def head(n, _):
            g, i = n // per, lax.rem(n, per)
            base = g * 3 * cols + i * HDIM
            q_at, k_at, v_at = (pl.ds(pl.multiple_of(base + m * cols, HDIM), HDIM) for m in range(3))
            pre = g * 2 * cols + i * HDIM
            kp_at, vp_at = (pl.ds(pl.multiple_of(pre + m * cols, HDIM), HDIM) for m in range(2))
            out_at = pl.ds(pl.multiple_of(n * HDIM, HDIM), HDIM)
            for j in range(4):
                there = pl.ds(r * length + at[j], size)
                k_own[j * size : (j + 1) * size] = proj[there, k_at]
                v_own[j * size : (j + 1) * size] = proj[there, v_at]

            def run(before):
                for j in range(4):
                    there = pl.ds(r * length + at[j], size)
                    q = proj[there, q_at]
                    start, end = first_key(j, size, segment), j * size
                    parts = [
                        (
                            prefix_proj[m * length : (m + 1) * length, kp_at],
                            prefix_proj[m * length : (m + 1) * length, vp_at],
                            None,
                        )
                        for m in range(before)
                    ]
                    if end > start:
                        parts.append((k_own[start:end], v_own[start:end], None))
                    parts.append((k_own[end : end + size], v_own[end : end + size], causal(size)))
                    scores = []
                    for k, _, mask in parts:
                        s = dot(k, q, ((1,), (1,)))
                        scores.append(s if mask is None else jnp.where(mask, s, MASKED))
                    top = functools.reduce(
                        jnp.maximum, [jnp.max(s, axis=0, keepdims=True) for s in scores]
                    )
                    total = jnp.zeros((1, size), F32)
                    out = jnp.zeros((HDIM, size), F32)
                    for s, (_, v, _) in zip(scores, parts):
                        p = jnp.exp2((s - top) * scale)
                        total = total + jnp.sum(p, axis=0, keepdims=True)
                        out = out + dot(v, p.astype(BF16), ((0,), (0,)))
                    att[there, out_at] = (out / total).T.astype(BF16)
                    lse[r * heads + n, :, j * size : (j + 1) * size] = top * scale + jnp.log(total) * LOG2E

            if segment is not None:
                run(0)
            else:
                for m in range(groups):
                    pl.when(places.g == m)(functools.partial(run, m))
            return 0

        lax.fori_loop(0, heads, head, 0)

    to_core, to_far = [None, None], [None, None]

    def out_product(r):
        def away(t):
            c_send[r, pl.ds(t, size), :] = dot(
                att[pl.ds(r * length + 2 * size + t, size), :], out_here[...]
            ).astype(BF16)

        in_tiles(2 * size, size, away)
        to_core[r] = copies.remote(c_send.at[r], c_recv.at[r], places.to_c)

    def out_sum(r):
        to_core[r].wait_recv()

        def far(t):
            h_send[r, pl.ds(t, size), :] = (
                dot(att[pl.ds(r * length + size + t, size), :], out_here[...])
                + c_recv[r, pl.ds(size + t, size), :].astype(F32)
            ).astype(BF16)

        in_tiles(size, size, far)
        to_far[r] = copies.remote(h_send.at[r], h_recv.at[r], places.to_h)

        def own(t):
            resid[r, pl.ds(t, size), :] = (
                dot(att[pl.ds(r * length + t, size), :], out_here[...])
                + c_recv[r, pl.ds(t, size), :].astype(F32)
                + rows_ref[r, pl.ds(t, size), :].astype(F32)
                + wide_ref[2:3]
            )

        in_tiles(size, size, own)

    def second_norm(r):
        to_far[r].wait_recv()

        def body(t):
            values = resid[r, pl.ds(t, chunk), :] + h_recv[r, pl.ds(t, chunk), :].astype(F32)
            resid[r, pl.ds(t, chunk), :] = values
            normed2[r, pl.ds(t, chunk), :] = normalized(values, 3, 4)

        in_tiles(size, chunk, body)
        copies.local(resid.at[r], resid_out.at[r])
        copies.local(normed2.at[r], full2.at[pl.ds(r * length, size), :])
        return spread_to(normed2.at[r], full2, r * length)

    def clear(t):
        prefix_here[pl.ds(t, size), :] = jnp.zeros((size, width), BF16)

    places.barrier()
    w_in.own()
    w_in.turn()
    bias_steps = [
        copies.remote(bias_ref, bias_here.at[n // extra], places.further(o))
        for n, o in enumerate(places.offsets)
        if n and o[0] == 0
    ]
    bias_here[0] = bias_ref[...]
    first_norm(1)
    spread = [None, spread_to(norm_here.at[pl.ds(length, size), :], norm_here, length)]
    first_norm(0)
    w_in.second(False)
    w_out.own()
    w_in.turned()
    w_out.turn()

    before, later = [], []
    for k in range(1, groups):
        row = (k - 1) * length
        slot = [prefix_here.at[pl.ds(row + n * size, size), :] for n in range(4)]
        copy = copies.remote(
            norm_here.at[pl.ds(0, size), :], slot[0], places.further((0, k)), tracked=False
        )
        pl.when(places.g + k < groups)(copy.start)
        before.append(copy)
        far = copies.remote(slot[0], slot[1], places.to_h, tracked=False)
        core = copies.remote(slot[0], slot[2], places.to_c, tracked=False)
        last = copies.remote(slot[1], slot[3], places.to_c, tracked=False)
        later.append((far, core, last))

    def for_prefix(action):
        for k in range(1, groups):
            pl.when(places.g >= k)(functools.partial(action, k - 1))

    def prefix_came(k):
        before[k].wait_recv()
        later[k][0].start()
        later[k][1].start()

    def prefix_forward(k):
        later[k][0].wait_recv()
        later[k][2].start()

    def prefix_finish(k):
        later[k][1].wait_recv()
        later[k][2].wait_recv()

    for k in range(1, groups):

        @pl.when(places.g < k)
        def _():
            in_tiles(length, size, lambda t: clear((k - 1) * length + t))

    w_out.second(False)
    spread[1].forward()
    spread[0] = spread_to(norm_here.at[pl.ds(0, size), :], norm_here, 0)
    w_in.second(True)
    w_in.finish(False)
    w_in.finish(True)
    w_up.own()
    copies.local(in_here, in_all)
    for copy in bias_steps:
        copy.wait_recv()
    spread[1].finish()
    project(norm_here, length, proj, length, 0)
    w_out.turned()
    spread[0].forward()
    attention(1, quarter)
    w_out.second(True)
    w_up.second(False)
    spread[0].finish()
    copies.local(norm_here, full1)
    project(norm_here, 0, proj, 0, 0)
    copies.local(proj, proj_out)
    for_prefix(prefix_came)
    w_up.turn()
    w_out.finish(False)
    w_out.finish(True)
    copies.local(out_here, out_all)
    w_down.own()
    out_product(1)
    out_sum(1)
    for_prefix(prefix_forward)
    w_down.second(False)
    for_prefix(prefix_finish)
    for k in range(1, groups):
        project(prefix_here, (k - 1) * length, prefix_proj, (k - 1) * length, 1)
    copies.local(prefix_here, prefix1)
    copies.local(prefix_proj, prefix_out)
    w_down.turn()
    spread2 = [None, second_norm(1)]
    attention(0, None)
    w_up.turned()
    copies.local(att, att_out)
    copies.local(lse, lse_out)
    out_product(0)
    out_sum(0)
    spread2[1].forward()
    w_up.second(True)
    spread2[0] = second_norm(0)
    w_down.turned()
    spread2[0].forward()
    w_up.finish(False)
    w_up.finish(True)
    w_down.second(True)
    w_down.finish(False)
    spread2[1].finish()
    spread2[0].finish()
    w_down.finish(True)

    for k in range(1, groups):
        far, core, last = later[k - 1]
        pl.when(places.g + k < groups)(before[k - 1].wait_send)

        @pl.when(places.g >= k)
        def _():
            far.wait_send()
            core.wait_send()
            last.wait_send()

    copies.finish()


def run_forward(split, quarter, rows, in_w, out_w, up_w, down_w, wide, bias):
    extra, groups = split
    size, width = rows.shape[1:]
    length = 4 * size
    cols, hidden = in_w.shape[1] // 3, up_w.shape[1]
    all_cols = groups * cols
    heads = all_cols // HDIM
    shape = jax.ShapeDtypeStruct
    anywhere = pl.BlockSpec(memory_space=pl.ANY)
    inside = pl.BlockSpec(memory_space=pltpu.VMEM)
    count = extra * groups * 20 + 4 * groups + 24
    out_shape = [
        shape((width, 3 * all_cols), BF16),
        shape((all_cols, width), BF16),
        shape((width, groups * hidden), BF16),
        shape((groups * hidden, width), BF16),
        shape((groups,) + bias.shape, F32),
        shape((2 * length, width), BF16),
        shape(((groups - 1) * length, width), BF16),
        shape((2 * length, 3 * all_cols), BF16),
        shape(((groups - 1) * length, 2 * all_cols), BF16),
        shape((2 * length, all_cols), BF16),
        shape((2 * heads, 1, length), F32),
        shape((2, size, width), F32),
        shape((2 * length, width), BF16),
    ]
    return pl.pallas_call(
        functools.partial(layer_forward, extra, groups, quarter),
        in_specs=[inside] + [anywhere] * 4 + [inside] * 2,
        out_specs=[inside if n == 4 else anywhere for n in range(len(out_shape))],
        out_shape=out_shape,
        scratch_shapes=[
            pltpu.VMEM((width, 3 * all_cols), BF16),
            pltpu.VMEM((all_cols, width), BF16),
            pltpu.VMEM((2 * length, width), BF16),
            pltpu.VMEM(((groups - 1) * length, width), BF16),
            pltpu.VMEM((2 * length, 3 * all_cols), BF16),
            pltpu.VMEM(((groups - 1) * length, 2 * all_cols), BF16),
            pltpu.VMEM((2 * length, all_cols), BF16),
            pltpu.VMEM((2 * heads, 1, length), F32),
            pltpu.VMEM((2, 2 * size, width), BF16),
            pltpu.VMEM((2, 2 * size, width), BF16),
            pltpu.VMEM((2, size, width), BF16),
            pltpu.VMEM((2, size, width), BF16),
            pltpu.VMEM((2, size, width), F32),
            pltpu.VMEM((2, size, width), BF16),
            pltpu.VMEM((length, HDIM), BF16),
            pltpu.VMEM((length, HDIM), BF16),
            pltpu.SemaphoreType.DMA((count,)),
            pltpu.SemaphoreType.DMA((count,)),
            pltpu.SemaphoreType.DMA((24,)),
        ],
        compiler_params=kernel_params(0),
        cost_estimate=pl.CostEstimate(flops=10**11, bytes_accessed=10**8, transcendentals=10**7),
    )(rows, in_w, out_w, up_w, down_w, wide, bias)


class GradScatter:
    def __init__(self, copies, places, parts, land, turned, work, own, fetched, out):
        self.copies, self.places, self.parts = copies, places, parts
        self.land, self.turned, self.work, self.own = land, turned, work, own
        self.fetched, self.out = fetched, out
        self.half, self.cols = land.shape[2:]
        self.steps = {}
        numbers = range(len(places.offsets))
        self.land_at = {(n, k): land.at[n, k] for n in numbers for k in range(6)}
        self.work_at = {(n, k): work.at[n, k] for n in numbers for k in range(2)}

    def piece(self, n, i, j, part):
        places = self.places
        offset = places.offsets[n]
        index = offset[1] * places.extra * 4 + places.share(offset, i, j)
        return self.parts.at[index, pl.ds(part * self.half, self.half), :]

    def _send(self, n, key, source, partner):
        self.steps[n, key] = self.copies.remote(source, self.land_at[n, key], partner)

    ORDER = ((1, 1), (0, 1), (1, 0), (0, 0))

    def index(self, n, i, j):
        places = self.places
        return places.offsets[n][1] * places.extra * 4 + places.share(places.offsets[n], i, j)

    def send(self, n, i, j):
        to_a, to_b = self.places.to_a, self.places.to_b
        if (i, j) == (1, 1):
            self._send(n, 0, self.piece(n, 1, 1, 0), to_a)
            self._send(n, 1, self.piece(n, 1, 1, 1), to_b)
        elif (i, j) == (0, 1):
            self._send(n, 2, self.piece(n, 0, 1, 0), to_a)
        elif (i, j) == (1, 0):
            self._send(n, 3, self.piece(n, 1, 0, 1), to_b)

    def start(self, n):
        for i, j in self.ORDER:
            self.send(n, i, j)

    def _run(self, jobs):
        before = None
        for m, (waits, sources, finish) in enumerate(jobs):
            for copy in waits:
                copy.wait_recv()
            slots = [
                self.fetched.at[m % 2, k, : self.half, : self.cols] for k in range(len(sources))
            ]
            loads = [self.copies.local(s, t, tracked=False) for s, t in zip(sources, slots)]
            if before is not None:
                before()

            def after(loads=loads, slots=slots, finish=finish):
                for load in loads:
                    load.wait()
                finish(functools.reduce(jnp.add, [t[...].astype(F32) for t in slots]))

            before = after
        if before is not None:
            before()

    def middle(self, *numbers):
        jobs = []
        for n in numbers:
            for key, target, partner, arrived, piece in (
                (5, 0, self.places.to_b, 0, self.piece(n, 1, 0, 0)),
                (4, 1, self.places.to_a, 1, self.piece(n, 0, 1, 1)),
            ):

                def finish(summed, n=n, key=key, target=target, partner=partner):
                    self.work[n, target] = summed.astype(BF16)
                    self._send(n, key, self.work_at[n, target], partner)

                jobs.append(([self.steps[n, arrived]], [self.land.at[n, arrived], piece], finish))
        self._run(jobs)

    def last(self, *numbers):
        jobs = []
        for n in numbers:
            for part, keys in ((0, (2, 5)), (1, (3, 4))):

                def finish(summed, n=n, part=part):
                    rows = slice(part * self.half, (part + 1) * self.half)
                    if n == 0:
                        self.out[rows, :] = summed
                        return
                    self.own[n - 1, rows, :] = summed.astype(BF16)
                    if part == 1:
                        e, g = self.places.offsets[n]
                        self.steps[n, "t"] = self.copies.remote(
                            self.own.at[n - 1],
                            self.turned.at[n - 1],
                            self.places.further((-e, -g)),
                        )

                jobs.append(
                    (
                        [self.steps[n, k] for k in keys],
                        [self.piece(n, 0, 0, part)] + [self.land.at[n, k] for k in keys],
                        finish,
                    )
                )
        self._run(jobs)

    def total(self):
        jobs = []
        for n in range(1, len(self.places.offsets)):
            for part in range(2):

                def finish(summed, part=part):
                    self.out[part * self.half : (part + 1) * self.half, :] += summed

                jobs.append(
                    (
                        [] if part else [self.steps[n, "t"]],
                        [self.turned.at[n - 1, pl.ds(part * self.half, self.half), :]],
                        finish,
                    )
                )
        self._run(jobs)

    @staticmethod
    def landing(sources, rows, cols):
        return [
            jax.ShapeDtypeStruct((sources, 6, rows // 2, cols), BF16),
            jax.ShapeDtypeStruct((max(sources - 1, 1), rows, cols), BF16),
        ]

    @staticmethod
    def working(sources, rows, cols):
        return [
            pltpu.VMEM((sources, 2, rows // 2, cols), BF16),
            pltpu.VMEM((max(sources - 1, 1), rows, cols), BF16),
        ]


class Fold:
    def __init__(self, copies, places, c_send, c_recv, h_send, free, size):
        self.copies, self.places, self.size = copies, places, size
        self.c_send, self.c_recv, self.h_send, self.free = c_send, c_recv, h_send, free
        self.core, self.count, self.far = None, 0, {}

    def away(self, block):
        if self.core is not None:
            self.copies.sent(self.core)
        for t in range(2):
            self.c_send[t * self.size : (t + 1) * self.size, :] = block(2 + t).astype(BF16)
        if self.core is not None:
            pl.semaphore_wait(self.free, 1)
        self.core = self.copies.remote(self.c_send, self.c_recv, self.places.to_c)

    def kept(self, block, target, more, h_recv=None, far_out=None):
        size, turn = self.size, self.count % len(self.h_send)
        self.count += 1
        h_send = self.h_send[turn]
        if turn in self.far:
            self.far.pop(turn)()
        h_send[...] = block(1).astype(BF16)
        target[...] = block(0).astype(BF16)
        self.core.wait_recv()
        h_send[...] = (h_send[...].astype(F32) + self.c_recv[size:, :].astype(F32)).astype(BF16)
        if far_out is None:
            copy = self.copies.remote(h_send, h_recv, self.places.to_h)
            self.far[turn] = functools.partial(self.copies.sent, copy)
        else:
            copy = self.copies.local(h_send, far_out, tracked=False)
            self.far[turn] = copy.wait
        target[...] = (target[...].astype(F32) + self.c_recv[:size, :].astype(F32)).astype(BF16)
        if more:
            pl.semaphore_signal(
                self.free, inc=1, device_id=self.places.to_c, device_id_type=pl.DeviceIdType.MESH
            )
        return copy

    def finish(self):
        for wait in self.far.values():
            wait()
        self.copies.sent(self.core)


class Stream:
    def __init__(self, copies, slots, blocks, ready=None):
        self.copies, self.slots, self.blocks = copies, slots, blocks
        self.ready = ready
        self.loads = {}
        self._load(0)

    def _load(self, n):
        if n < len(self.blocks):
            targets = [s[n % 2] for s in self.slots]
            if self.ready is not None:
                self.ready(n)
            self.loads[n] = [
                self.copies.local(s, t, tracked=False) for s, t in zip(self.blocks[n], targets)
            ]

    def take(self, n):
        for load in self.loads[n]:
            load.wait()
        self._load(n + 1)
        return n % 2


class Spread:
    def __init__(self, copies, places, source, full, row, size):
        self.copies, self.places, self.full, self.row, self.size = copies, places, full, row, size
        self.far = copies.remote(source, self.slot(1), places.to_h)
        self.core = copies.remote(source, self.slot(2), places.to_c)

    def slot(self, n):
        return self.full.at[pl.ds(self.row + n * self.size, self.size), :]

    def forward(self):
        self.far.wait_recv()
        self.last = self.copies.remote(self.slot(1), self.slot(3), self.places.to_c)

    def finish(self):
        self.core.wait_recv()
        self.last.wait_recv()


def middle_kernel(extra, groups, *refs):
    (
        full2, own_cots, up_all, down_all, resid, wide, bias_up,
        mixed, full_dres, grad_down, up_parts, sums, up_sums, mixed_far, full_cot, act, dup, down_parts,
        land, turned,
        big, down, narrow, tiles, cots, c_send, c_recv, h_send, h_recv, low, stage_down, work, own,
        fetched, send_sem, recv_sem, near_sem, free,
    ) = refs
    size, width = mixed.shape[1:]
    length = 4 * size
    hidden, depth = grad_down.shape
    shares = extra * 4
    chunk = min(64, size)
    strip = min(512, hidden)
    places = Places(extra, groups)
    copies = Copies(send_sem, recv_sem, near_sem)
    sources = len(places.offsets)
    scatter = GradScatter(
        copies, places, down_parts, land, turned, work, own, fetched, grad_down
    )
    fold = Fold(copies, places, c_send, c_recv, [h_send.at[0], h_send.at[1]], free, size)
    folded = {}

    def load(source, target):
        return copies.local(source, target, tracked=False)

    def load_big(source):
        return load(source, big.at[: source.shape[0]])

    loading = [load_big(up_all), load(down_all, down)]
    tile_slots = [tiles.at[0], tiles.at[1]]
    cot_slots = [cots.at[0], cots.at[1]]
    narrow_slots = [narrow.at[0], narrow.at[1]]
    order = [(r, slot) for slot in (0, 2, 1, 3) for r in range(2)]
    where = [pl.ds(r * length + s * size, size) for r, s in order]
    places.barrier()
    spread_cot = []
    for r in range(2):
        copies.local(own_cots.at[r], full_cot.at[pl.ds(r * length, size), :], tracked=False).wait()
        spread_cot.append(Spread(copies, places, own_cots.at[r], full_cot, r * length, size))

    def cot_ready(n):
        r, slot = order[n]
        if slot == 1:
            spread_cot[r].forward()
        elif slot == 2:
            spread_cot[r].core.wait_recv()
        elif slot == 3:
            spread_cot[r].last.wait_recv()

    stream = Stream(
        copies,
        [tile_slots, cot_slots],
        [[full2.at[w, :], full_cot.at[w, :]] for w in where],
        cot_ready,
    )
    sums[...] = jnp.zeros_like(sums)
    up_sums[...] = jnp.zeros_like(up_sums)
    for copy in loading:
        copy.wait()

    stored = {}
    for n, (r, slot) in enumerate(order):
        at = stream.take(n)
        if n >= 2:
            for copy in stored.pop(n - 2):
                copy.wait()
        act_at, dup_at = c_send.at[pl.ds(at * size, size), :], low.at[at]

        def body(g, _):
            columns = pl.ds(pl.multiple_of(g * strip, HDIM), strip)
            value = dot(tiles[at], big[:width, columns]) + bias_up[:1, columns]
            square = value * value
            tanh = jnp.tanh(0.7978845608028654 * value * (1.0 + 0.044715 * square))
            half = 0.5 * (1.0 + tanh)
            act_at[:, columns] = (value * half).astype(BF16)
            slope = half + 0.5 * value * (1.0 - tanh * tanh) * 0.7978845608028654 * (
                1.0 + 3 * 0.044715 * square
            )
            back = (dot(cots[at], down[columns, :], ((1,), (1,))) * slope).astype(BF16)
            dup_at[:, columns] = back
            up_sums[:, columns] += jnp.sum(back.astype(F32), axis=0, keepdims=True)
            return 0

        lax.fori_loop(0, groups * hidden // strip, body, 0)
        stored[n] = [
            load(act_at, act.at[where[n], :]),
            load(dup_at, dup.at[where[n], :]),
        ]
    for n in list(stored):
        for copy in stored.pop(n):
            copy.wait()

    here_cots = [load(own_cots.at[r], cots.at[r]) for r in range(2)]
    dup_order = [(r, slot) for r in range(2) for slot in (2, 3, 1, 0)]
    stream_dup = Stream(
        copies,
        [tile_slots],
        [[dup.at[pl.ds(r * length + s * size, size), :]] for r, s in dup_order],
    )

    def dup_block(r):
        def block(slot):
            at = stream_dup.take(dup_order.index((r, slot)))
            return dot(tiles[at], big[:width], ((1,), (1,)))

        return block

    for r in range(2):
        fold.away(dup_block(r))
        folded[r] = fold.kept(dup_block(r), low.at[r], True, h_recv.at[r])

    def norm_back_rows(r):
        folded[r].wait_recv()

        def body(t):
            rows = pl.ds(t, chunk)
            grad = low[r, rows, :].astype(F32) + h_recv[r, rows, :].astype(F32)
            scaled, inverse = stats(resid[r, rows, :])
            cot = cots[r, rows, :].astype(F32)
            value = cot + norm_back(grad, scaled, inverse, wide[3:4])
            low[r, rows, :] = value.astype(BF16)
            for n, term in enumerate((value, grad * scaled, grad, cot)):
                sums[n : n + 1, :] += jnp.sum(term, axis=0, keepdims=True)

        in_tiles(size, chunk, body)
        copies.local(low.at[r], full_dres.at[pl.ds(r * length, size), :])
        return Spread(copies, places, low.at[r], full_dres, r * length, size)

    def columns_of(source):
        return [
            [source.at[:, pl.ds(d * depth, depth)]] for g in range(groups) for d in range(shares)
        ]

    turn_order = list(range(groups))[::-1]

    def of_group(g):
        return [n for n in range(sources) if places.offsets[n][1] == g][::-1]

    wanted = [(n, i, j) for g in turn_order for n in of_group(g) for i, j in GradScatter.ORDER]

    def wanted_columns(source):
        found = []
        for n, i, j in wanted:
            share = places.share(places.offsets[n], i, j)
            found.append([source.at[:, pl.ds(pl.multiple_of(share * depth, depth), depth)]])
        return found

    loading = load_big(act)
    stream_cot = Stream(copies, [narrow_slots], wanted_columns(full_cot))
    loading.wait()
    for copy in here_cots:
        copy.wait()
    put = {}
    spread = [None, None]

    def settle(number):
        if number in put:
            put.pop(number).wait()
            scatter.send(*wanted[number])

    for number, (n, i, j) in enumerate(wanted):
        at = stream_cot.take(number)
        slot = number % 2
        first = places.offsets[n][1] * hidden

        def body(t):
            left = big[: 2 * length, pl.ds(pl.multiple_of(first + t, HDIM), hidden // 2)]
            stage_down[slot, pl.ds(t, hidden // 2), :] = dot(
                left, narrow[at], ((0,), (0,))
            ).astype(BF16)

        in_tiles(hidden, hidden // 2, body)
        put[number] = load(stage_down.at[slot], down_parts.at[scatter.index(n, i, j)])
        settle(number - 1)
        if number == 4 * extra - 1:
            settle(number)
            spread[0] = norm_back_rows(0)
            scatter.middle(*of_group(turn_order[0]))
    settle(len(wanted) - 1)
    spread[1] = norm_back_rows(1)
    scatter.last(*[n for n in of_group(turn_order[0]) if n])

    def act_block(r):
        def block(slot):
            return dot(big[r * length + slot * size : r * length + (slot + 1) * size, :], down[...])

        return block

    for r in range(2):
        fold.away(act_block(r))
        fold.kept(act_block(r), mixed.at[r], r == 0, far_out=mixed_far.at[r])
        spread[r].forward()
        if r == 0:
            scatter.middle(*[n for g in turn_order[1:] for n in of_group(g)])

    loading = load_big(dup)
    stream_two = Stream(copies, [narrow_slots], columns_of(full2))
    stage_up = [down.at[pl.ds(n * depth, depth), pl.ds(0, hidden)] for n in range(2)]
    loading.wait()
    put_up = {}
    done = 0
    for g in turn_order:
        for d in range(shares):
            at = stream_two.take(done)
            if done >= 2:
                put_up.pop(done - 2).wait()
            stage_up[done % 2][...] = dot(
                narrow[at], big[: 2 * length, g * hidden : (g + 1) * hidden], ((0,), (0,))
            ).astype(BF16)
            put_up[done] = load(stage_up[done % 2], up_parts.at[g * shares + d])
            done += 1
    for copy in put_up.values():
        copy.wait()
    spread[0].finish()
    spread[1].finish()
    scatter.last(*[n for g in turn_order for n in of_group(g) if (n, "t") not in scatter.steps])
    scatter.total()
    fold.finish()
    copies.finish()


def attention_back_rows(places, row, length, size, heads, per, segment, refs, column, pump=None):
    (
        proj, prefix_proj, att, datt, lse, dproj, dprefix,
        k_own, v_own, dk_own, dv_own, dk_pre, dv_pre,
    ) = refs
    scale = HDIM**-0.5 * LOG2E
    factor = HDIM**-0.5
    at = row_blocks(2 * places.h + places.c, 4, size)
    base = row * length

    def head(n, _):
        q_at, k_at, v_at = (pl.ds(column(n, 3, m), HDIM) for m in range(3))
        kp_at, vp_at = (pl.ds(column(n, 2, m), HDIM) for m in range(2))
        out_at = pl.ds(pl.multiple_of(n * HDIM, HDIM), HDIM)
        for j in range(4):
            there = pl.ds(base + at[j], size)
            k_own[j * size : (j + 1) * size] = proj[there, k_at]
            v_own[j * size : (j + 1) * size] = proj[there, v_at]
        dk_own[...] = jnp.zeros_like(dk_own)
        dv_own[...] = jnp.zeros_like(dv_own)
        if segment is None:
            dk_pre[...] = jnp.zeros_like(dk_pre)
            dv_pre[...] = jnp.zeros_like(dv_pre)

        def run(before):
            for j in range(4):
                there = pl.ds(base + at[j], size)
                q = proj[there, q_at]
                do = datt[there, out_at]
                product = do.astype(F32) * att[there, out_at].astype(F32)
                delta = lax.dot_general(
                    jnp.ones((8, HDIM), F32),
                    product,
                    (((1,), (1,)), ((), ())),
                    precision=lax.Precision.HIGHEST,
                    preferred_element_type=F32,
                )[:1]
                log_total = lse[row * heads + n, :, j * size : (j + 1) * size]
                start, end = first_key(j, size, segment), j * size
                parts = []
                step = min(512, length)
                for m in range(0, before * length, step):
                    rows = slice(m, m + step)
                    parts.append(
                        (prefix_proj[rows, kp_at], prefix_proj[rows, vp_at], dk_pre, dv_pre, rows, None)
                    )
                if end > start:
                    rows = slice(start, end)
                    parts.append((k_own[rows], v_own[rows], dk_own, dv_own, rows, None))
                rows = slice(end, end + size)
                parts.append((k_own[rows], v_own[rows], dk_own, dv_own, rows, causal(size)))
                dq = jnp.zeros((HDIM, size), F32)
                for k, v, dk, dv, rows, mask in parts:
                    s = dot(k, q, ((1,), (1,))) * scale - log_total
                    p = jnp.exp2(s if mask is None else jnp.where(mask, s, MASKED))
                    dscores = (p * (dot(v, do, ((1,), (1,))) - delta)).astype(BF16)
                    dv[rows] += dot(p.astype(BF16), do)
                    dk[rows] += dot(dscores, q)
                    dq = dq + dot(k, dscores, ((0,), (0,)))
                dproj[there, q_at] = (dq * factor).T.astype(BF16)

        if segment is not None:
            run(0)
        else:
            for m in range(places.groups):
                pl.when(places.g == m)(functools.partial(run, m))
            dprefix[:, q_at] = jnp.zeros_like(dk_pre, dtype=BF16)
            dprefix[:, k_at] = (dk_pre[...] * factor).astype(BF16)
            dprefix[:, v_at] = dv_pre[...].astype(BF16)
        for j in range(4):
            rows = slice(j * size, (j + 1) * size)
            there = pl.ds(base + at[j], size)
            dproj[there, k_at] = (dk_own[rows] * factor).astype(BF16)
            dproj[there, v_at] = dv_own[rows].astype(BF16)
        if pump is not None:
            pl.when(n == heads // 2 - 1)(pump)
        return 0

    lax.fori_loop(0, heads, head, 0)


def last_kernel(extra, groups, quarter, *refs):
    (
        proj_in, prefix_in, att_in, full_dres, out_all, in_all, full1, prefix1, up_parts, mixed_far, rows_in,
        lse, wide_ref, sums2, up_sums,
        grad_in, grad_out, grad_up, dnormed1, all_sums, bias_sums, mixed_recv,
        in_parts, out_parts, land_in, turned_in, land_out, turned_out, land_up, turned_up,
        proj, prefix_proj, att, datt, dprefix, w_in, w_out, spare,
        k_own, v_own, dk_own, dv_own, dk_pre, dv_pre,
        c_send, c_recv, h_send, h_recv, back, returned, dproj_sums, sum_send, sum_recv, bias_send, bias_recv,
        bias_out, bias_turn, stage_in, stage_out,
        work_in, own_in, work_out, own_out, work_up, own_up, fetched, send_sem, recv_sem, near_sem, free,
    ) = refs
    size, width = dnormed1.shape[1:]
    length = 4 * size
    cols = grad_in.shape[1] // 3
    depth = grad_in.shape[0]
    wide = 3 * cols
    heads = groups * cols // HDIM
    per = cols // HDIM
    shares = extra * 4
    places = Places(extra, groups)
    copies = Copies(send_sem, recv_sem, near_sem)
    sources = len(places.offsets)
    far_first = list(range(sources))[::-1]
    up = GradScatter(
        copies, places, up_parts, land_up, turned_up, work_up, own_up, fetched, grad_up
    )
    out = GradScatter(
        copies, places, out_parts, land_out, turned_out, work_out, own_out, fetched, grad_out
    )
    into = GradScatter(
        copies, places, in_parts, land_in, turned_in, work_in, own_in, fetched, grad_in
    )
    dproj = proj
    folds = Fold(copies, places, c_send, c_recv, [h_send.at[0], h_send.at[1]], free, size)
    folded = {}

    def column(n, parts, m):
        return pl.multiple_of((n // per * parts + m) * cols + lax.rem(n, per) * HDIM, HDIM)

    here = [
        copies.local(s, t, tracked=False)
        for s, t in (
            (out_all, w_out), (proj_in, proj), (prefix_in, prefix_proj), (att_in, att), (in_all, w_in),
        )
    ]
    order = [(r, slot) for r in range(2) for slot in range(4)]
    tiles = [c_send.at[pl.ds(n * size, size), :] for n in range(2)]
    stream = Stream(
        copies, [tiles], [[full_dres.at[pl.ds(r * length + s * size, size), :]] for r, s in order]
    )
    places.barrier()
    for n in far_first:
        up.start(n)
    mixed_steps = [
        copies.remote(mixed_far.at[r], mixed_recv.at[r], places.to_h) for r in range(2)
    ]
    for copy in here:
        copy.wait()

    def attended_grad(r):
        for slot in range(4):
            at = stream.take(r * 4 + slot)
            datt[r * length + slot * size : r * length + (slot + 1) * size, :] = dot(
                tiles[at][...], w_out[...], ((1,), (1,))
            ).astype(BF16)

    def attention_back(r, segment, pump=None):
        attention_back_rows(
            places, r, length, size, heads, per, segment,
            (
                proj, prefix_proj, att, datt, lse, dproj, dprefix,
                k_own, v_own, dk_own, dv_own, dk_pre, dv_pre,
            ),
            column,
            pump,
        )

    def block_of(source, row):
        def block(slot):
            rows = source[row + slot * size : row + (slot + 1) * size, :]
            return dot(rows, w_in[...], ((1,), (1,)))

        return block

    def fold(number, source, row, target, more=True):
        folds.away(block_of(source, row))
        folded[number] = folds.kept(block_of(source, row), target, more, h_recv.at[number])

    attended_grad(0)
    attended_grad(1)
    attention_back(0, None, lambda: up.middle(*far_first))
    up.last(*far_first[:-1])
    for k in range(1, groups):
        fold(1 + k, dprefix, (k - 1) * length, back.at[k - 1])
    attention_back(1, quarter)

    home = []
    for k in range(1, groups):
        folded[1 + k].wait_recv()
        back[k - 1] = (back[k - 1].astype(F32) + h_recv[1 + k].astype(F32)).astype(BF16)
        copy = copies.remote(
            back.at[k - 1], returned.at[k - 1], places.further((0, -k)), tracked=False
        )
        pl.when(places.g >= k)(copy.start)
        home.append(copy)

    slots = [datt.at[:, pl.ds(0, depth)], spare]
    prefix_rows = prefix1.shape[0]
    slots_pre = [prefix_proj.at[:, pl.ds(n * depth, depth)] for n in range(2)]

    def share_of(n, i, j):
        return places.share(places.offsets[n], i, j)

    class Columns:
        def __init__(self, pairs, shares_at):
            self.pairs, self.shares_at, self.loads = pairs, shares_at, {}
            self._load(0)

        def _load(self, n):
            if n < len(self.shares_at):
                at = pl.ds(pl.multiple_of(self.shares_at[n] * depth, depth), depth)
                self.loads[n] = [
                    copies.local(s.at[:, at], slot[n % 2], tracked=False) for s, slot in self.pairs
                ]

        def take(self, n):
            for load in self.loads[n]:
                load.wait()
            self._load(n + 1)
            return n % 2

    groups_first = [
        n for g in range(groups)[::-1] for n in far_first if places.offsets[n][1] == g
    ]
    wanted = [(n, i, j) for n in groups_first for i, j in GradScatter.ORDER]
    stream_in = Columns([(full1, slots), (prefix1, slots_pre)], [share_of(*w) for w in wanted])
    put = {}

    def settle(scatter, todo, number):
        if number in put:
            put.pop(number).wait()
            scatter.send(*todo[number])

    def in_pieces(numbers):
        for number in numbers:
            n, i, j = wanted[number]
            at = stream_in.take(number)
            which = pl.ds(places.offsets[n][1] * wide, wide)
            value = dot(slots[at][...], dproj[:, which], ((0,), (0,)))
            if prefix_rows:
                value = value + dot(slots_pre[at][...], dprefix[:, which], ((0,), (0,)))
            stage_in[number % 2] = value.astype(BF16)
            put[number] = copies.local(
                stage_in.at[number % 2], in_parts.at[into.index(n, i, j)], tracked=False
            )
            settle(into, wanted, number - 1)
        settle(into, wanted, numbers[-1])

    hidden = up_parts.shape[2]
    far_ones = [n for n in far_first if places.offsets[n][1] == groups - 1]
    near_ones = [n for n in far_first if places.offsets[n][1] != groups - 1]
    in_pieces(range(4 * len(far_ones)))
    fold(0, dproj, 0, dnormed1.at[0])
    into.middle(*far_ones)
    if near_ones:
        in_pieces(range(4 * len(far_ones), len(wanted)))
    into.last(*[n for n in far_ones if n])
    fold(1, dproj, length, dnormed1.at[1], False)
    todo = [(n, i, j) for i, j in GradScatter.ORDER for n in groups_first]
    stream_out = Columns([(full_dres, slots)], [share_of(*w) for w in todo])
    put.clear()
    for number, (n, i, j) in enumerate(todo):
        at = stream_out.take(number)
        first = places.offsets[n][1] * cols
        stage_out[number % 2] = dot(
            att[:, first : first + cols], slots[at][...], ((0,), (0,))
        ).astype(BF16)
        put[number] = copies.local(
            stage_out.at[number % 2], out_parts.at[out.index(n, i, j)], tracked=False
        )
        settle(out, todo, number - 1)
    settle(out, todo, len(todo) - 1)
    folds.finish()
    here = [
        copies.local(rows_in, c_send, tracked=False),
        copies.local(
            full_dres.at[pl.ds(0, size), :], c_recv.at[pl.ds(0, size), :], tracked=False
        ),
        copies.local(
            full_dres.at[pl.ds(length, size), :], c_recv.at[pl.ds(size, size), :], tracked=False
        ),
    ]
    into.middle(*near_ones)
    into.last(*[n for n in near_ones if n])
    dproj_sums[...] = jnp.zeros_like(dproj_sums)

    def add_rows(t):
        dproj_sums[0:1, :] += jnp.sum(dproj[pl.ds(t, size), :].astype(F32), axis=0, keepdims=True)

    in_tiles(2 * length, size, add_rows)

    def add_prefix(t):
        dproj_sums[1:2, :] += jnp.sum(dprefix[pl.ds(t, size), :].astype(F32), axis=0, keepdims=True)

    in_tiles(prefix_rows, size, add_prefix)
    bias_send[...] = jnp.zeros_like(bias_send)
    for g in range(groups):
        base = g * wide
        bias_send[g, 0:1, :cols] = dproj_sums[0:1, base : base + cols]
        bias_send[g, 0:1, cols : 2 * cols] = (
            dproj_sums[0:1, base + 2 * cols : base + wide] + dproj_sums[1:2, base + 2 * cols : base + wide]
        )
        bias_send[g, 0:1, 2 * cols :] = up_sums[0:1, g * hidden : (g + 1) * hidden]
    bias_steps = [
        copies.remote(bias_send.at[g], bias_turn.at[g - 1], places.further((0, -g)))
        for g in range(1, groups)
    ]
    out.middle(*far_first)
    up.last(0)

    all_sums[...] = jnp.zeros_like(all_sums)
    all_sums[0:4, :] = sums2[...]
    chunk = min(64, size)
    for copy in here:
        copy.wait()
    for r in (1, 0):
        if r == 0:
            out.last(*far_first[:-1])
            for k in range(1, groups):

                @pl.when(places.g + k < groups)
                def _():
                    home[k - 1].wait_recv()
                    dnormed1[0] = (
                        dnormed1[0].astype(F32) + returned[k - 1].astype(F32)
                    ).astype(BF16)

                pl.when(places.g >= k)(home[k - 1].wait_send)
        folded[r].wait_recv()

        def norm_rows(t):
            at = pl.ds(t, chunk)
            grad = dnormed1[r, at, :].astype(F32) + h_recv[r, at, :].astype(F32)
            scaled, inverse = stats(c_send[pl.ds(r * size + t, chunk), :].astype(F32))
            value = c_recv[pl.ds(r * size + t, chunk), :].astype(F32) + norm_back(
                grad, scaled, inverse, wide_ref[0:1]
            )
            dnormed1[r, at, :] = value.astype(BF16)
            all_sums[4:5, :] += jnp.sum(grad * scaled, axis=0, keepdims=True)
            all_sums[5:6, :] += jnp.sum(grad, axis=0, keepdims=True)

        in_tiles(size, chunk, norm_rows)

    for copy in bias_steps:
        copy.wait_recv()
    bias_sums[...] = functools.reduce(
        jnp.add, [bias_send[0]] + [bias_turn[g - 1] for g in range(1, groups)]
    )
    waiting = [up.total, lambda: into.last(0), lambda: out.last(0)]
    stages = [("c", 2), ("h", 2), ("g", groups), ("b", 2), ("a", 2), ("e", extra)]
    for number, (axis, count) in enumerate(stages):
        if count == 1:
            continue
        pairs = [(all_sums, sum_send.at[number], sum_recv.at[number])]
        if axis in DP:
            pairs.append((bias_sums, bias_out.at[number], bias_recv.at[number]))
        me = lax.axis_index(axis)
        steps = []
        for values, sending, coming in pairs:
            sending[...] = values[...]
            for k in range(1, count):
                partner = {axis: lax.rem(me + k, count)}
                steps.append(copies.remote(sending, coming.at[k - 1], partner))
        if waiting:
            waiting.pop(0)()
        for copy in steps:
            copy.wait_recv()
        for values, sending, coming in pairs:
            if count == 2:
                values[...] = sending[...] + coming[0]
            else:
                total = jnp.zeros(values.shape, F32)
                for device in range(count):
                    back_by = lax.rem(me - device + count, count)
                    other = coming[jnp.maximum(back_by - 1, 0)]
                    total = total + jnp.where(back_by == 0, sending[...], other)
                values[...] = total
    for job in waiting:
        job()
    for copy in mixed_steps:
        copy.wait_recv()
    out.total()
    into.total()
    copies.finish()


def kernel_params(number):
    return pltpu.CompilerParams(
        collective_id=number, has_side_effects=True, vmem_limit_bytes=KERNEL_VMEM
    )


def run_middle(split, full2, cots, up_all, down_all, resid, wide, bias_up, hidden, depth):
    extra, groups = split
    sources = extra * groups
    size, width = resid.shape[1:]
    length = 4 * size
    all_hidden = groups * hidden
    shape = jax.ShapeDtypeStruct
    anywhere = pl.BlockSpec(memory_space=pl.ANY)
    inside = pl.BlockSpec(memory_space=pltpu.VMEM)
    shares = sources * 4
    return pl.pallas_call(
        functools.partial(middle_kernel, extra, groups),
        in_specs=[anywhere] * 4 + [inside] * 3,
        out_specs=[inside, anywhere, inside, anywhere, inside, inside] + [anywhere] * 7,
        out_shape=[
            shape((2, size, width), BF16),
            shape((2 * length, width), BF16),
            shape((hidden, depth), F32),
            shape((shares, depth, hidden), BF16),
            shape((4, width), F32),
            shape((1, all_hidden), F32),
            shape((2, size, width), BF16),
            shape((2 * length, width), BF16),
            shape((2 * length, all_hidden), BF16),
            shape((2 * length, all_hidden), BF16),
            shape((shares, hidden, depth), BF16),
        ]
        + GradScatter.landing(sources, hidden, depth),
        scratch_shapes=[
            pltpu.VMEM((max(width, 2 * length), all_hidden), BF16),
            pltpu.VMEM((all_hidden, width), BF16),
            pltpu.VMEM((2, 2 * length, depth), BF16),
            pltpu.VMEM((2, size, width), BF16),
            pltpu.VMEM((2, size, width), BF16),
            pltpu.VMEM((2 * size, width), BF16),
            pltpu.VMEM((2 * size, width), BF16),
            pltpu.VMEM((2, size, width), BF16),
            pltpu.VMEM((2, size, width), BF16),
            pltpu.VMEM((2, size, width), BF16),
            pltpu.VMEM((2, hidden, depth), BF16),
        ]
        + GradScatter.working(sources, hidden, depth)
        + [
            pltpu.VMEM((2, 3, hidden // 2, depth), BF16),
            pltpu.SemaphoreType.DMA((sources * 8 + 16,)),
            pltpu.SemaphoreType.DMA((sources * 8 + 16,)),
            pltpu.SemaphoreType.DMA((sources * 16 + 6 * shares + 80,)),
            pltpu.SemaphoreType.REGULAR,
        ],
        compiler_params=kernel_params(1),
        cost_estimate=pl.CostEstimate(flops=10**11, bytes_accessed=10**8, transcendentals=10**6),
    )(full2, cots, up_all, down_all, resid, wide, bias_up)


def run_last(split, quarter, proj, prefix_proj, att, full_dres, out_all, in_all, full1, prefix1, up_parts, mixed_far, rows, lse, norms, sums2, up_sums):
    extra, groups = split
    sources = extra * groups
    shares = sources * 4
    length, width = full1.shape[0] // 2, full1.shape[1]
    size = length // 4
    cols = att.shape[1] // groups
    depth, hidden = up_parts.shape[1:]
    wide, all_wide = 3 * cols, 3 * cols * groups
    prefix_rows = prefix1.shape[0]
    most = max(extra, groups, 2) - 1
    shape = jax.ShapeDtypeStruct
    anywhere = pl.BlockSpec(memory_space=pl.ANY)
    inside = pl.BlockSpec(memory_space=pltpu.VMEM)
    heads_rows = [pltpu.VMEM((length, HDIM), BF16)] * 2 + [pltpu.VMEM((length, HDIM), F32)] * 2
    return pl.pallas_call(
        functools.partial(last_kernel, extra, groups, quarter),
        in_specs=[anywhere] * 11 + [inside] * 4,
        out_specs=[inside] * 6 + [anywhere] * 9,
        out_shape=[
            shape((depth, wide), F32),
            shape((cols, depth), F32),
            shape((depth, hidden), F32),
            shape((2, size, width), BF16),
            shape((8, width), F32),
            shape((8, 2 * cols + hidden), F32),
            shape((2, size, width), BF16),
            shape((shares, depth, wide), BF16),
            shape((shares, cols, depth), BF16),
        ]
        + GradScatter.landing(sources, depth, wide)
        + GradScatter.landing(sources, cols, depth)
        + GradScatter.landing(sources, depth, hidden),
        scratch_shapes=[
            pltpu.VMEM(proj.shape, BF16),
            pltpu.VMEM(prefix_proj.shape, BF16),
            pltpu.VMEM(att.shape, BF16),
            pltpu.VMEM(att.shape, BF16),
            pltpu.VMEM((prefix_rows, all_wide), BF16),
            pltpu.VMEM(in_all.shape, BF16),
            pltpu.VMEM(out_all.shape, BF16),
            pltpu.VMEM((2 * length, depth), BF16),
        ]
        + heads_rows
        + [pltpu.VMEM((prefix_rows, HDIM), F32)] * 2
        + [
            pltpu.VMEM((2 * size, width), BF16),
            pltpu.VMEM((2 * size, width), BF16),
            pltpu.VMEM((2, size, width), BF16),
            pltpu.VMEM((1 + groups, size, width), BF16),
            pltpu.VMEM((max(groups - 1, 1), size, width), BF16),
            pltpu.VMEM((max(groups - 1, 1), size, width), BF16),
            pltpu.VMEM((2, all_wide), F32),
            pltpu.VMEM((6, 8, width), F32),
            pltpu.VMEM((6, most, 8, width), F32),
            pltpu.VMEM((groups, 8, 2 * cols + hidden), F32),
            pltpu.VMEM((6, most, 8, 2 * cols + hidden), F32),
            pltpu.VMEM((6, 8, 2 * cols + hidden), F32),
            pltpu.VMEM((max(groups - 1, 1), 8, 2 * cols + hidden), F32),
            pltpu.VMEM((2, depth, wide), BF16),
            pltpu.VMEM((2, cols, depth), BF16),
        ]
        + GradScatter.working(sources, depth, wide)
        + GradScatter.working(sources, cols, depth)
        + GradScatter.working(sources, depth, hidden)
        + [
            pltpu.VMEM((2, 3, depth // 2, max(wide, hidden, depth)), BF16),
            pltpu.SemaphoreType.DMA((sources * 24 + 12 * groups + 48,)),
            pltpu.SemaphoreType.DMA((sources * 24 + 12 * groups + 48,)),
            pltpu.SemaphoreType.DMA((sources * 48 + 10 * shares + 32,)),
            pltpu.SemaphoreType.REGULAR,
        ],
        compiler_params=kernel_params(2),
        cost_estimate=pl.CostEstimate(flops=10**11, bytes_accessed=10**8, transcendentals=10**7),
    )(proj, prefix_proj, att, full_dres, out_all, in_all, full1, prefix1, up_parts, mixed_far, rows, lse, norms, sums2, up_sums)


def local(
    tokens,
    segments,
    first_gain,
    first_shift,
    in_weight,
    in_bias,
    out_weight,
    out_bias,
    second_gain,
    second_shift,
    up_weight,
    up_bias,
    down_weight,
    down_bias,
    cotangent,
):
    extra, groups = lax.axis_size("e"), lax.axis_size("g")
    split = (extra, groups)
    size, width = tokens.shape[1:]
    cols, hidden, depth = in_weight.shape[2], up_weight.shape[1], in_weight.shape[0]
    quarter = segments.shape[1] // 4

    single = jnp.where(segments[0, -1] == 0, 0, 1)
    order = (single, 1 - single)

    def pick(x):
        return [lax.dynamic_index_in_dim(x, r, 0, keepdims=False) for r in order]

    def unpick(first, second):
        return jnp.where(single == 0, jnp.stack([first, second]), jnp.stack([second, first]))

    picked = jnp.stack(pick(tokens))
    cots = pick(cotangent)

    no_bias = jnp.zeros_like(in_bias[0])
    biases = jnp.concatenate([in_bias[0], no_bias, in_bias[1], up_bias])
    biases = jnp.broadcast_to(biases, (8, biases.shape[0]))
    wide = jnp.stack([first_gain, first_shift, out_bias, second_gain, second_shift, down_bias])
    (
        in_all, out_all, up_all, down_all, biases, full1, prefix1, proj, proj_prefix, attended, lse,
        resid, full2,
    ) = run_forward(
        split,
        quarter,
        picked,
        in_weight.reshape(depth, 3 * cols),
        out_weight,
        up_weight,
        down_weight,
        wide,
        biases,
    )
    bias_up = biases[:, 0, 3 * cols :].reshape(1, -1)
    length = 4 * size

    mixed, full_dres, grad_down, up_parts, sums2, up_sums, mixed_far = run_middle(
        split, full2, jnp.stack(cots), up_all, down_all, resid, wide, bias_up, hidden, depth
    )[:7]
    grad_in, grad_out, grad_up, tokens_grad, all_sums, bias_sums, mixed_recv = run_last(
        split, quarter, proj, proj_prefix, attended, full_dres, out_all, in_all, full1, prefix1, up_parts,
        mixed_far, picked.reshape(2 * size, width), lse, wide, sums2, up_sums,
    )[:7]
    mixed = (resid + mixed.astype(F32) + mixed_recv.astype(F32) + down_bias).astype(BF16)
    return (
        unpick(*mixed),
        unpick(*tokens_grad),
        all_sums[4],
        all_sums[5],
        grad_in.reshape(in_weight.shape),
        bias_sums[0, : 2 * cols].reshape(2, cols),
        grad_out,
        all_sums[0],
        all_sums[1],
        all_sums[2],
        grad_up,
        bias_sums[0, 2 * cols :],
        grad_down,
        all_sums[3],
    )


def solution(mesh):
    dp, tp = mesh.shape["dp"], mesh.shape["tp"]
    split = Mesh(mesh.devices.reshape(dp // 4, 2, 2, tp // 4, 2, 2), DP + TP)
    in_specs = (
        P(DP, TP, None),
        P(DP, None),
        P(),
        P(),
        P(DP, None, TP),
        P(None, TP),
        P(TP, DP),
        P(),
        P(),
        P(),
        P(DP, TP),
        P(TP),
        P(TP, DP),
        P(),
        P(DP, TP, None),
    )
    out_specs = (
        P(DP, TP, None),
        P(DP, TP, None),
        P(),
        P(),
        P(DP, None, TP),
        P(None, TP),
        P(TP, DP),
        P(),
        P(),
        P(),
        P(DP, TP),
        P(TP),
        P(TP, DP),
        P(),
    )
    return jax.shard_map(local, mesh=split, in_specs=in_specs, out_specs=out_specs, check_vma=False)
```

```python
import functools

import jax
import jax.numpy as jnp
from jax import lax
from jax.experimental import pallas as pl
from jax.experimental.pallas import tpu as pltpu
from jax.sharding import Mesh, PartitionSpec as P

HDIM = 128
EPSILON = 1e-05
MASKED = -1e30
LOG2E = 1.4426950408889634
F32 = jnp.float32
BF16 = jnp.bfloat16
VMEM_LIMIT = 48 * 1024 * 1024
KERNEL_VMEM = 63 * 1024 * 1024
DP = ("e", "b", "a")
TP = ("g", "h", "c")
SLOTS = (0, 2, 1, 3)


def dot(x, y, contract=((1,), (0,))):
    return lax.dot_general(x, y, (contract, ((), ())), preferred_element_type=F32)


def stats(rows):
    mean = jnp.mean(rows, axis=-1, keepdims=True)
    center = rows - mean
    inverse = lax.rsqrt(jnp.mean(center * center, axis=-1, keepdims=True) + EPSILON)
    return center * inverse, inverse


def norm_back(grad_normed, scaled, inverse, gain):
    weighted = grad_normed * gain
    return inverse * (
        weighted
        - jnp.mean(weighted, axis=-1, keepdims=True)
        - scaled * jnp.mean(weighted * scaled, axis=-1, keepdims=True)
    )


def row_blocks(place, count, size):
    found = []
    for j in range(count):
        other = jnp.bitwise_xor(place, j)
        slot = (other >> 1) + 2 * (other & 1)
        found.append(pl.multiple_of(slot * size, size))
    return found


def causal(size):
    keys = lax.broadcasted_iota(jnp.int32, (size, size), 0)
    queries = lax.broadcasted_iota(jnp.int32, (size, size), 1)
    return keys <= queries


def first_key(block, size, segment):
    return 0 if segment is None else block * size // segment * segment


class Remote:
    def __init__(self, copies, number, source, target, device):
        self.copies, self.number, self.source, self.target = copies, number, source, target
        self.device = device

    def _copy(self):
        return pltpu.make_async_remote_copy(
            src_ref=self.source,
            dst_ref=self.target,
            send_sem=self.copies.send.at[self.number],
            recv_sem=self.copies.recv.at[self.number],
            device_id=self.device,
            device_id_type=pl.DeviceIdType.MESH,
        )

    def start(self):
        self._copy().start()

    def wait_send(self):
        self._copy().wait_send()

    def wait_recv(self):
        self._copy().wait_recv()


class Copies:
    def __init__(self, send, recv, near):
        self.send, self.recv, self.near = send, recv, near
        self.remotes, self.locals = 0, 0
        self.open_sends, self.open_locals = [], []

    def remote(self, source, target, device, tracked=True):
        copy = Remote(self, self.remotes, source, target, device)
        self.remotes += 1
        if tracked:
            copy.start()
            self.open_sends.append(copy)
        return copy

    def local(self, source, target, tracked=True):
        copy = pltpu.make_async_copy(source, target, self.near.at[self.locals])
        self.locals += 1
        copy.start()
        if tracked:
            self.open_locals.append(copy)
        return copy

    def sent(self, copy):
        copy.wait_send()
        self.open_sends = [c for c in self.open_sends if c is not copy]

    def finish(self):
        for copy in self.open_sends:
            copy.wait_send()
        for copy in self.open_locals:
            copy.wait()


class Places:
    def __init__(self, extra, groups):
        self.extra, self.groups = extra, groups
        self.e, self.b, self.a, self.g, self.h, self.c = (lax.axis_index(n) for n in DP + TP)
        self.to_a, self.to_b = {"a": 1 - self.a}, {"b": 1 - self.b}
        self.to_h, self.to_c = {"h": 1 - self.h}, {"c": 1 - self.c}
        self.offsets = [(e, g) for g in range(groups) for e in range(extra)]

    def further(self, offset):
        return {
            "e": lax.rem(self.e + offset[0] + self.extra, self.extra),
            "g": lax.rem(self.g + offset[1] + self.groups, self.groups),
        }

    def share(self, offset, i, j):
        e = lax.rem(self.e - offset[0] + self.extra, self.extra)
        b = self.b if i == 0 else 1 - self.b
        a = self.a if j == 0 else 1 - self.a
        return e * 4 + b * 2 + a

    def barrier(self):
        semaphore = pltpu.get_barrier_semaphore()
        partners = [self.to_a, self.to_b, self.to_h, self.to_c]
        partners += [self.further(o) for o in self.offsets[1:]]
        for partner in partners:
            pl.semaphore_signal(
                semaphore, inc=1, device_id=partner, device_id_type=pl.DeviceIdType.MESH
            )
        pl.semaphore_wait(semaphore, len(partners))


class WeightGather:
    def __init__(self, copies, places, shard, full, at):
        self.copies, self.places, self.shard, self.full, self.at = copies, places, shard, full, at
        self.rows = shard.shape[0]
        self.steps = {}

    def piece(self, n, i, j, low=0, count=None):
        place = self.at(n, self.places.share(self.places.offsets[n], i, j))
        return self.full.at[
            pl.ds(place[0] + low, self.rows if count is None else count), place[1]
        ]

    def own(self):
        self.here = self.copies.local(self.shard, self.piece(0, 0, 0), tracked=False)
        self._first(0, self.shard)

    def turn(self):
        for n, offset in enumerate(self.places.offsets):
            if n:
                e, g = offset
                share = self.places.share((0, 0), 0, 0)
                place = self.at(n, share)
                target = self.full.at[pl.ds(place[0], self.rows), place[1]]
                self.steps["t", n] = self.copies.remote(
                    self.shard, target, self.places.further(offset)
                )

    def _first(self, n, source):
        piece = self.piece(n, 0, 0)
        self.steps["a", n] = self.copies.remote(source, piece, self.places.to_a)
        self.steps["b", n] = self.copies.remote(source, piece, self.places.to_b)

    def turned(self):
        for n in range(1, len(self.places.offsets)):
            self.steps["t", n].wait_recv()
            self._first(n, self.piece(n, 0, 0))

    def second(self, far):
        half = self.rows // 2
        for n in range(1, len(self.places.offsets)) if far else (0,):
            self.steps["a", n].wait_recv()
            top = self.piece(n, 0, 1, 0, half)
            self.steps["ab", n] = self.copies.remote(top, top, self.places.to_b)
            self.steps["b", n].wait_recv()
            low = self.piece(n, 1, 0, half, half)
            self.steps["ba", n] = self.copies.remote(low, low, self.places.to_a)

    def finish(self, far):
        if not far:
            self.here.wait()
        for n in range(1, len(self.places.offsets)) if far else (0,):
            self.steps["ab", n].wait_recv()
            self.steps["ba", n].wait_recv()


def in_tiles(rows, size, body):
    lax.fori_loop(0, rows // size, lambda n, _: (body(pl.multiple_of(n * size, size)), 0)[1], 0)


def layer_forward(extra, groups, quarter, *refs):
    (
        rows_ref, in_ref, out_ref, up_ref, down_ref, wide_ref, bias_ref,
        in_all, out_all, up_all, down_all, bias_all, full1, prefix1, proj_out, prefix_out, att_out,
        lse_out, resid_out, full2,
        in_here, out_here, norm_here, prefix_here, proj, prefix_proj, att, lse, c_send, c_recv, h_send,
        h_recv, resid, normed2, k_own, v_own, send_sem, recv_sem, near_sem,
    ) = refs
    size, width = rows_ref.shape[1:]
    length = 4 * size
    cols = in_ref.shape[1] // 3
    hidden, depth = up_ref.shape[1], up_ref.shape[0]
    heads = groups * cols // HDIM
    per = cols // HDIM
    scale = HDIM**-0.5 * LOG2E
    places = Places(extra, groups)
    copies = Copies(send_sem, recv_sem, near_sem)
    bias_here = bias_all
    place = 2 * places.h + places.c
    at = row_blocks(place, 4, size)
    chunk = min(64, size)

    def in_at(wide):
        return lambda n, share: (share * depth, pl.ds((n // extra) * wide, wide))

    def column_at(rows):
        def where(n, share):
            return (n // extra) * rows, pl.ds(pl.multiple_of(share * depth, depth), depth)

        return where

    w_in = WeightGather(copies, places, in_ref, in_here, in_at(3 * cols))
    w_out = WeightGather(copies, places, out_ref, out_here, column_at(cols))
    w_up = WeightGather(copies, places, up_ref, up_all, in_at(hidden))
    w_down = WeightGather(copies, places, down_ref, down_all, column_at(hidden))

    def spread_to(source, full, row):
        return Spread(copies, places, source, full, row, size)

    def normalized(values, gain, shift):
        mean = jnp.mean(values, axis=-1, keepdims=True)
        center = values - mean
        inverse = lax.rsqrt(jnp.mean(center * center, axis=-1, keepdims=True) + EPSILON)
        return (center * inverse * wide_ref[gain : gain + 1] + wide_ref[shift : shift + 1]).astype(BF16)

    def first_norm(r):
        def body(at_row):
            values = rows_ref[r, pl.ds(at_row, chunk), :].astype(F32)
            norm_here[pl.ds(r * length + at_row, chunk), :] = normalized(values, 0, 1)

        in_tiles(size, chunk, body)

    def project(source, row, target, row_to, kind):
        wide = (3 - kind) * cols

        def body(n, _):
            g, m = n // 4, lax.rem(n, 4)
            x = source[pl.ds(pl.multiple_of(row + m * size, size), size), :]
            w = in_here[:, pl.ds(pl.multiple_of((g * 3 + kind) * cols, HDIM), wide)]
            bias = bias_here[g, :1, kind * cols : 3 * cols]
            to = pl.ds(pl.multiple_of(g * wide, HDIM), wide)
            target[pl.ds(pl.multiple_of(row_to + m * size, size), size), to] = (dot(x, w) + bias).astype(BF16)
            return 0

        lax.fori_loop(0, 4 * groups, body, 0)

    def attention(r, segment):
        def head(n, _):
            g, i = n // per, lax.rem(n, per)
            base = g * 3 * cols + i * HDIM
            q_at, k_at, v_at = (pl.ds(pl.multiple_of(base + m * cols, HDIM), HDIM) for m in range(3))
            pre = g * 2 * cols + i * HDIM
            kp_at, vp_at = (pl.ds(pl.multiple_of(pre + m * cols, HDIM), HDIM) for m in range(2))
            out_at = pl.ds(pl.multiple_of(n * HDIM, HDIM), HDIM)
            for j in range(4):
                there = pl.ds(r * length + at[j], size)
                k_own[j * size : (j + 1) * size] = proj[there, k_at]
                v_own[j * size : (j + 1) * size] = proj[there, v_at]

            def run(before):
                for j in range(4):
                    there = pl.ds(r * length + at[j], size)
                    q = proj[there, q_at]
                    start, end = first_key(j, size, segment), j * size
                    parts = [
                        (
                            prefix_proj[m * length : (m + 1) * length, kp_at],
                            prefix_proj[m * length : (m + 1) * length, vp_at],
                            None,
                        )
                        for m in range(before)
                    ]
                    if end > start:
                        parts.append((k_own[start:end], v_own[start:end], None))
                    parts.append((k_own[end : end + size], v_own[end : end + size], causal(size)))
                    scores = []
                    for k, _, mask in parts:
                        s = dot(k, q, ((1,), (1,)))
                        scores.append(s if mask is None else jnp.where(mask, s, MASKED))
                    top = functools.reduce(
                        jnp.maximum, [jnp.max(s, axis=0, keepdims=True) for s in scores]
                    )
                    total = jnp.zeros((1, size), F32)
                    out = jnp.zeros((HDIM, size), F32)
                    for s, (_, v, _) in zip(scores, parts):
                        p = jnp.exp2((s - top) * scale)
                        total = total + jnp.sum(p, axis=0, keepdims=True)
                        out = out + dot(v, p.astype(BF16), ((0,), (0,)))
                    att[there, out_at] = (out / total).T.astype(BF16)
                    lse[r * heads + n, :, j * size : (j + 1) * size] = top * scale + jnp.log(total) * LOG2E

            if segment is not None:
                run(0)
            else:
                for m in range(groups):
                    pl.when(places.g == m)(functools.partial(run, m))
            return 0

        lax.fori_loop(0, heads, head, 0)

    to_core, to_far = [None, None], [None, None]

    def out_product(r):
        def away(t):
            c_send[r, pl.ds(t, size), :] = dot(
                att[pl.ds(r * length + 2 * size + t, size), :], out_here[...]
            ).astype(BF16)

        in_tiles(2 * size, size, away)
        to_core[r] = copies.remote(c_send.at[r], c_recv.at[r], places.to_c)

    def out_sum(r):
        to_core[r].wait_recv()

        def far(t):
            h_send[r, pl.ds(t, size), :] = (
                dot(att[pl.ds(r * length + size + t, size), :], out_here[...])
                + c_recv[r, pl.ds(size + t, size), :].astype(F32)
            ).astype(BF16)

        in_tiles(size, size, far)
        to_far[r] = copies.remote(h_send.at[r], h_recv.at[r], places.to_h)

        def own(t):
            resid[r, pl.ds(t, size), :] = (
                dot(att[pl.ds(r * length + t, size), :], out_here[...])
                + c_recv[r, pl.ds(t, size), :].astype(F32)
                + rows_ref[r, pl.ds(t, size), :].astype(F32)
                + wide_ref[2:3]
            )

        in_tiles(size, size, own)

    def second_norm(r):
        to_far[r].wait_recv()

        def body(t):
            values = resid[r, pl.ds(t, chunk), :] + h_recv[r, pl.ds(t, chunk), :].astype(F32)
            resid[r, pl.ds(t, chunk), :] = values
            normed2[r, pl.ds(t, chunk), :] = normalized(values, 3, 4)

        in_tiles(size, chunk, body)
        copies.local(resid.at[r], resid_out.at[r])
        copies.local(normed2.at[r], full2.at[pl.ds(r * length, size), :])
        return spread_to(normed2.at[r], full2, r * length)

    def clear(t):
        prefix_here[pl.ds(t, size), :] = jnp.zeros((size, width), BF16)

    places.barrier()
    w_in.own()
    w_in.turn()
    bias_steps = [
        copies.remote(bias_ref, bias_here.at[n // extra], places.further(o))
        for n, o in enumerate(places.offsets)
        if n and o[0] == 0
    ]
    bias_here[0] = bias_ref[...]
    first_norm(1)
    spread = [None, spread_to(norm_here.at[pl.ds(length, size), :], norm_here, length)]
    first_norm(0)
    w_in.second(False)
    w_out.own()
    w_in.turned()
    w_out.turn()

    before, later = [], []
    for k in range(1, groups):
        row = (k - 1) * length
        slot = [prefix_here.at[pl.ds(row + n * size, size), :] for n in range(4)]
        copy = copies.remote(
            norm_here.at[pl.ds(0, size), :], slot[0], places.further((0, k)), tracked=False
        )
        pl.when(places.g + k < groups)(copy.start)
        before.append(copy)
        far = copies.remote(slot[0], slot[1], places.to_h, tracked=False)
        core = copies.remote(slot[0], slot[2], places.to_c, tracked=False)
        last = copies.remote(slot[1], slot[3], places.to_c, tracked=False)
        later.append((far, core, last))

    def for_prefix(action):
        for k in range(1, groups):
            pl.when(places.g >= k)(functools.partial(action, k - 1))

    def prefix_came(k):
        before[k].wait_recv()
        later[k][0].start()
        later[k][1].start()

    def prefix_forward(k):
        later[k][0].wait_recv()
        later[k][2].start()

    def prefix_finish(k):
        later[k][1].wait_recv()
        later[k][2].wait_recv()

    for k in range(1, groups):

        @pl.when(places.g < k)
        def _():
            in_tiles(length, size, lambda t: clear((k - 1) * length + t))

    w_out.second(False)
    spread[1].forward()
    spread[0] = spread_to(norm_here.at[pl.ds(0, size), :], norm_here, 0)
    w_in.second(True)
    w_in.finish(False)
    w_in.finish(True)
    w_up.own()
    copies.local(in_here, in_all)
    for copy in bias_steps:
        copy.wait_recv()
    spread[1].finish()
    project(norm_here, length, proj, length, 0)
    w_out.turned()
    spread[0].forward()
    attention(1, quarter)
    w_out.second(True)
    w_up.second(False)
    spread[0].finish()
    copies.local(norm_here, full1)
    project(norm_here, 0, proj, 0, 0)
    copies.local(proj, proj_out)
    for_prefix(prefix_came)
    w_up.turn()
    w_out.finish(False)
    w_out.finish(True)
    copies.local(out_here, out_all)
    w_down.own()
    out_product(1)
    out_sum(1)
    for_prefix(prefix_forward)
    w_down.second(False)
    for_prefix(prefix_finish)
    for k in range(1, groups):
        project(prefix_here, (k - 1) * length, prefix_proj, (k - 1) * length, 1)
    copies.local(prefix_here, prefix1)
    copies.local(prefix_proj, prefix_out)
    w_down.turn()
    spread2 = [None, second_norm(1)]
    attention(0, None)
    w_up.turned()
    copies.local(att, att_out)
    copies.local(lse, lse_out)
    out_product(0)
    out_sum(0)
    spread2[1].forward()
    w_up.second(True)
    spread2[0] = second_norm(0)
    w_down.turned()
    spread2[0].forward()
    w_up.finish(False)
    w_up.finish(True)
    w_down.second(True)
    w_down.finish(False)
    spread2[1].finish()
    spread2[0].finish()
    w_down.finish(True)

    for k in range(1, groups):
        far, core, last = later[k - 1]
        pl.when(places.g + k < groups)(before[k - 1].wait_send)

        @pl.when(places.g >= k)
        def _():
            far.wait_send()
            core.wait_send()
            last.wait_send()

    copies.finish()


def run_forward(split, quarter, rows, in_w, out_w, up_w, down_w, wide, bias):
    extra, groups = split
    size, width = rows.shape[1:]
    length = 4 * size
    cols, hidden = in_w.shape[1] // 3, up_w.shape[1]
    all_cols = groups * cols
    heads = all_cols // HDIM
    shape = jax.ShapeDtypeStruct
    anywhere = pl.BlockSpec(memory_space=pl.ANY)
    inside = pl.BlockSpec(memory_space=pltpu.VMEM)
    count = extra * groups * 20 + 4 * groups + 24
    out_shape = [
        shape((width, 3 * all_cols), BF16),
        shape((all_cols, width), BF16),
        shape((width, groups * hidden), BF16),
        shape((groups * hidden, width), BF16),
        shape((groups,) + bias.shape, F32),
        shape((2 * length, width), BF16),
        shape(((groups - 1) * length, width), BF16),
        shape((2 * length, 3 * all_cols), BF16),
        shape(((groups - 1) * length, 2 * all_cols), BF16),
        shape((2 * length, all_cols), BF16),
        shape((2 * heads, 1, length), F32),
        shape((2, size, width), F32),
        shape((2 * length, width), BF16),
    ]
    return pl.pallas_call(
        functools.partial(layer_forward, extra, groups, quarter),
        in_specs=[inside] + [anywhere] * 4 + [inside] * 2,
        out_specs=[inside if n == 4 else anywhere for n in range(len(out_shape))],
        out_shape=out_shape,
        scratch_shapes=[
            pltpu.VMEM((width, 3 * all_cols), BF16),
            pltpu.VMEM((all_cols, width), BF16),
            pltpu.VMEM((2 * length, width), BF16),
            pltpu.VMEM(((groups - 1) * length, width), BF16),
            pltpu.VMEM((2 * length, 3 * all_cols), BF16),
            pltpu.VMEM(((groups - 1) * length, 2 * all_cols), BF16),
            pltpu.VMEM((2 * length, all_cols), BF16),
            pltpu.VMEM((2 * heads, 1, length), F32),
            pltpu.VMEM((2, 2 * size, width), BF16),
            pltpu.VMEM((2, 2 * size, width), BF16),
            pltpu.VMEM((2, size, width), BF16),
            pltpu.VMEM((2, size, width), BF16),
            pltpu.VMEM((2, size, width), F32),
            pltpu.VMEM((2, size, width), BF16),
            pltpu.VMEM((length, HDIM), BF16),
            pltpu.VMEM((length, HDIM), BF16),
            pltpu.SemaphoreType.DMA((count,)),
            pltpu.SemaphoreType.DMA((count,)),
            pltpu.SemaphoreType.DMA((24,)),
        ],
        compiler_params=kernel_params(0),
        cost_estimate=pl.CostEstimate(flops=10**11, bytes_accessed=10**8, transcendentals=10**7),
    )(rows, in_w, out_w, up_w, down_w, wide, bias)


class GradScatter:
    def __init__(self, copies, places, parts, land, turned, work, own, fetched, out):
        self.copies, self.places, self.parts = copies, places, parts
        self.land, self.turned, self.work, self.own = land, turned, work, own
        self.fetched, self.out = fetched, out
        self.half, self.cols = land.shape[2:]
        self.steps = {}
        numbers = range(len(places.offsets))
        self.land_at = {(n, k): land.at[n, k] for n in numbers for k in range(6)}
        self.work_at = {(n, k): work.at[n, k] for n in numbers for k in range(2)}

    def piece(self, n, i, j, part):
        places = self.places
        offset = places.offsets[n]
        index = offset[1] * places.extra * 4 + places.share(offset, i, j)
        return self.parts.at[index, pl.ds(part * self.half, self.half), :]

    def _send(self, n, key, source, partner):
        self.steps[n, key] = self.copies.remote(source, self.land_at[n, key], partner)

    ORDER = ((1, 1), (0, 1), (1, 0), (0, 0))

    def index(self, n, i, j):
        places = self.places
        return places.offsets[n][1] * places.extra * 4 + places.share(places.offsets[n], i, j)

    def send(self, n, i, j):
        to_a, to_b = self.places.to_a, self.places.to_b
        if (i, j) == (1, 1):
            self._send(n, 0, self.piece(n, 1, 1, 0), to_a)
            self._send(n, 1, self.piece(n, 1, 1, 1), to_b)
        elif (i, j) == (0, 1):
            self._send(n, 2, self.piece(n, 0, 1, 0), to_a)
        elif (i, j) == (1, 0):
            self._send(n, 3, self.piece(n, 1, 0, 1), to_b)

    def start(self, n):
        for i, j in self.ORDER:
            self.send(n, i, j)

    def _run(self, jobs):
        before = None
        for m, (waits, sources, finish) in enumerate(jobs):
            for copy in waits:
                copy.wait_recv()
            slots = [
                self.fetched.at[m % 2, k, : self.half, : self.cols] for k in range(len(sources))
            ]
            loads = [self.copies.local(s, t, tracked=False) for s, t in zip(sources, slots)]
            if before is not None:
                before()

            def after(loads=loads, slots=slots, finish=finish):
                for load in loads:
                    load.wait()
                finish(functools.reduce(jnp.add, [t[...].astype(F32) for t in slots]))

            before = after
        if before is not None:
            before()

    def middle(self, *numbers):
        jobs = []
        for n in numbers:
            for key, target, partner, arrived, piece in (
                (5, 0, self.places.to_b, 0, self.piece(n, 1, 0, 0)),
                (4, 1, self.places.to_a, 1, self.piece(n, 0, 1, 1)),
            ):

                def finish(summed, n=n, key=key, target=target, partner=partner):
                    self.work[n, target] = summed.astype(BF16)
                    self._send(n, key, self.work_at[n, target], partner)

                jobs.append(([self.steps[n, arrived]], [self.land.at[n, arrived], piece], finish))
        self._run(jobs)

    def last(self, *numbers):
        jobs = []
        for n in numbers:
            for part, keys in ((0, (2, 5)), (1, (3, 4))):

                def finish(summed, n=n, part=part):
                    rows = slice(part * self.half, (part + 1) * self.half)
                    if n == 0:
                        self.out[rows, :] = summed
                        return
                    self.own[n - 1, rows, :] = summed.astype(BF16)
                    if part == 1:
                        e, g = self.places.offsets[n]
                        self.steps[n, "t"] = self.copies.remote(
                            self.own.at[n - 1],
                            self.turned.at[n - 1],
                            self.places.further((-e, -g)),
                        )

                jobs.append(
                    (
                        [self.steps[n, k] for k in keys],
                        [self.piece(n, 0, 0, part)] + [self.land.at[n, k] for k in keys],
                        finish,
                    )
                )
        self._run(jobs)

    def total(self):
        jobs = []
        for n in range(1, len(self.places.offsets)):
            for part in range(2):

                def finish(summed, part=part):
                    self.out[part * self.half : (part + 1) * self.half, :] += summed

                jobs.append(
                    (
                        [] if part else [self.steps[n, "t"]],
                        [self.turned.at[n - 1, pl.ds(part * self.half, self.half), :]],
                        finish,
                    )
                )
        self._run(jobs)

    @staticmethod
    def landing(sources, rows, cols):
        return [
            jax.ShapeDtypeStruct((sources, 6, rows // 2, cols), BF16),
            jax.ShapeDtypeStruct((max(sources - 1, 1), rows, cols), BF16),
        ]

    @staticmethod
    def working(sources, rows, cols):
        return [
            pltpu.VMEM((sources, 2, rows // 2, cols), BF16),
            pltpu.VMEM((max(sources - 1, 1), rows, cols), BF16),
        ]


class Fold:
    def __init__(self, copies, places, c_send, c_recv, h_send, free, size):
        self.copies, self.places, self.size = copies, places, size
        self.c_send, self.c_recv, self.h_send, self.free = c_send, c_recv, h_send, free
        self.core, self.count, self.far = None, 0, {}

    def away(self, block):
        if self.core is not None:
            self.copies.sent(self.core)
        for t in range(2):
            self.c_send[t * self.size : (t + 1) * self.size, :] = block(2 + t).astype(BF16)
        if self.core is not None:
            pl.semaphore_wait(self.free, 1)
        self.core = self.copies.remote(self.c_send, self.c_recv, self.places.to_c)

    def kept(self, block, target, more, h_recv=None, far_out=None):
        size, turn = self.size, self.count % len(self.h_send)
        self.count += 1
        h_send = self.h_send[turn]
        if turn in self.far:
            self.far.pop(turn)()
        h_send[...] = block(1).astype(BF16)
        target[...] = block(0).astype(BF16)
        self.core.wait_recv()
        h_send[...] = (h_send[...].astype(F32) + self.c_recv[size:, :].astype(F32)).astype(BF16)
        if far_out is None:
            copy = self.copies.remote(h_send, h_recv, self.places.to_h)
            self.far[turn] = functools.partial(self.copies.sent, copy)
        else:
            copy = self.copies.local(h_send, far_out, tracked=False)
            self.far[turn] = copy.wait
        target[...] = (target[...].astype(F32) + self.c_recv[:size, :].astype(F32)).astype(BF16)
        if more:
            pl.semaphore_signal(
                self.free, inc=1, device_id=self.places.to_c, device_id_type=pl.DeviceIdType.MESH
            )
        return copy

    def finish(self):
        for wait in self.far.values():
            wait()
        self.copies.sent(self.core)


class Stream:
    def __init__(self, copies, slots, blocks, ready=None):
        self.copies, self.slots, self.blocks = copies, slots, blocks
        self.ready = ready
        self.loads = {}
        self._load(0)

    def _load(self, n):
        if n < len(self.blocks):
            targets = [s[n % 2] for s in self.slots]
            if self.ready is not None:
                self.ready(n)
            self.loads[n] = [
                self.copies.local(s, t, tracked=False) for s, t in zip(self.blocks[n], targets)
            ]

    def take(self, n):
        for load in self.loads[n]:
            load.wait()
        self._load(n + 1)
        return n % 2


class Spread:
    def __init__(self, copies, places, source, full, row, size):
        self.copies, self.places, self.full, self.row, self.size = copies, places, full, row, size
        self.far = copies.remote(source, self.slot(1), places.to_h)
        self.core = copies.remote(source, self.slot(2), places.to_c)

    def slot(self, n):
        return self.full.at[pl.ds(self.row + n * self.size, self.size), :]

    def forward(self):
        self.far.wait_recv()
        self.last = self.copies.remote(self.slot(1), self.slot(3), self.places.to_c)

    def finish(self):
        self.core.wait_recv()
        self.last.wait_recv()


def middle_kernel(extra, groups, *refs):
    (
        full2, own_cots, up_all, down_all, resid, wide, bias_up,
        mixed, full_dres, grad_down, up_parts, sums, up_sums, mixed_far, full_cot, act, dup, down_parts,
        land, turned,
        big, down, narrow, tiles, cots, c_send, c_recv, h_send, h_recv, low, stage_down, work, own,
        fetched, send_sem, recv_sem, near_sem, free,
    ) = refs
    size, width = mixed.shape[1:]
    length = 4 * size
    hidden, depth = grad_down.shape
    shares = extra * 4
    chunk = min(64, size)
    strip = min(512, hidden)
    places = Places(extra, groups)
    copies = Copies(send_sem, recv_sem, near_sem)
    sources = len(places.offsets)
    scatter = GradScatter(
        copies, places, down_parts, land, turned, work, own, fetched, grad_down
    )
    fold = Fold(copies, places, c_send, c_recv, [h_send.at[0], h_send.at[1]], free, size)
    folded = {}

    def load(source, target):
        return copies.local(source, target, tracked=False)

    def load_big(source):
        return load(source, big.at[: source.shape[0]])

    loading = [load_big(up_all), load(down_all, down)]
    tile_slots = [tiles.at[0], tiles.at[1]]
    cot_slots = [cots.at[0], cots.at[1]]
    narrow_slots = [narrow.at[0], narrow.at[1]]
    order = [(r, slot) for slot in (0, 2, 1, 3) for r in range(2)]
    where = [pl.ds(r * length + s * size, size) for r, s in order]
    places.barrier()
    spread_cot = []
    placed = []
    for r in range(2):
        spread_cot.append(Spread(copies, places, own_cots.at[r], full_cot, r * length, size))
        placed.append(load(own_cots.at[r], full_cot.at[pl.ds(r * length, size), :]))
    for copy in placed:
        copy.wait()

    def cot_ready(n):
        r, slot = order[n]
        if slot == 1:
            spread_cot[r].forward()
        elif slot == 2:
            spread_cot[r].core.wait_recv()
        elif slot == 3:
            spread_cot[r].last.wait_recv()

    stream = Stream(
        copies,
        [tile_slots, cot_slots],
        [[full2.at[w, :], full_cot.at[w, :]] for w in where],
        cot_ready,
    )
    sums[...] = jnp.zeros_like(sums)
    up_sums[...] = jnp.zeros_like(up_sums)
    for copy in loading:
        copy.wait()

    stored = {}
    for n, (r, slot) in enumerate(order):
        at = stream.take(n)
        if n >= 2:
            for copy in stored.pop(n - 2):
                copy.wait()
        act_at, dup_at = c_send.at[pl.ds(at * size, size), :], low.at[at]

        def body(g, _):
            columns = pl.ds(pl.multiple_of(g * strip, HDIM), strip)
            value = dot(tiles[at], big[:width, columns]) + bias_up[:1, columns]
            square = value * value
            tanh = jnp.tanh(0.7978845608028654 * value * (1.0 + 0.044715 * square))
            half = 0.5 * (1.0 + tanh)
            act_at[:, columns] = (value * half).astype(BF16)
            slope = half + 0.5 * value * (1.0 - tanh * tanh) * 0.7978845608028654 * (
                1.0 + 3 * 0.044715 * square
            )
            back = (dot(cots[at], down[columns, :], ((1,), (1,))) * slope).astype(BF16)
            dup_at[:, columns] = back
            up_sums[:, columns] += jnp.sum(back.astype(F32), axis=0, keepdims=True)
            return 0

        lax.fori_loop(0, groups * hidden // strip, body, 0)
        stored[n] = [
            load(act_at, act.at[where[n], :]),
            load(dup_at, dup.at[where[n], :]),
        ]
    for n in list(stored):
        for copy in stored.pop(n):
            copy.wait()

    here_cots = [load(own_cots.at[r], cots.at[r]) for r in range(2)]
    dup_order = [(r, slot) for r in range(2) for slot in (2, 3, 1, 0)]
    stream_dup = Stream(
        copies,
        [tile_slots],
        [[dup.at[pl.ds(r * length + s * size, size), :]] for r, s in dup_order],
    )

    def dup_block(r):
        def block(slot):
            at = stream_dup.take(dup_order.index((r, slot)))
            return dot(tiles[at], big[:width], ((1,), (1,)))

        return block

    for r in range(2):
        fold.away(dup_block(r))
        folded[r] = fold.kept(dup_block(r), low.at[r], True, h_recv.at[r])

    def norm_back_rows(r):
        folded[r].wait_recv()

        def body(t):
            rows = pl.ds(t, chunk)
            grad = low[r, rows, :].astype(F32) + h_recv[r, rows, :].astype(F32)
            scaled, inverse = stats(resid[r, rows, :])
            cot = cots[r, rows, :].astype(F32)
            value = cot + norm_back(grad, scaled, inverse, wide[3:4])
            low[r, rows, :] = value.astype(BF16)
            for n, term in enumerate((value, grad * scaled, grad, cot)):
                sums[n : n + 1, :] += jnp.sum(term, axis=0, keepdims=True)

        in_tiles(size, chunk, body)
        copies.local(low.at[r], full_dres.at[pl.ds(r * length, size), :])
        return Spread(copies, places, low.at[r], full_dres, r * length, size)

    def columns_of(source):
        return [
            [source.at[:, pl.ds(d * depth, depth)]] for g in range(groups) for d in range(shares)
        ]

    turn_order = list(range(groups))[::-1]

    def of_group(g):
        return [n for n in range(sources) if places.offsets[n][1] == g][::-1]

    wanted = [(n, i, j) for g in turn_order for n in of_group(g) for i, j in GradScatter.ORDER]

    def wanted_columns(source):
        found = []
        for n, i, j in wanted:
            share = places.share(places.offsets[n], i, j)
            found.append([source.at[:, pl.ds(pl.multiple_of(share * depth, depth), depth)]])
        return found

    loading = load_big(act)
    stream_cot = Stream(copies, [narrow_slots], wanted_columns(full_cot))
    loading.wait()
    for copy in here_cots:
        copy.wait()
    put = {}
    spread = [None, None]

    def settle(number):
        if number in put:
            put.pop(number).wait()
            scatter.send(*wanted[number])

    for number, (n, i, j) in enumerate(wanted):
        at = stream_cot.take(number)
        slot = number % 2
        first = places.offsets[n][1] * hidden

        def body(t):
            left = big[: 2 * length, pl.ds(pl.multiple_of(first + t, HDIM), hidden // 2)]
            stage_down[slot, pl.ds(t, hidden // 2), :] = dot(
                left, narrow[at], ((0,), (0,))
            ).astype(BF16)

        in_tiles(hidden, hidden // 2, body)
        put[number] = load(stage_down.at[slot], down_parts.at[scatter.index(n, i, j)])
        settle(number - 1)
        if number == 4 * extra - 1:
            settle(number)
            spread[0] = norm_back_rows(0)
            scatter.middle(*of_group(turn_order[0]))
    settle(len(wanted) - 1)
    spread[1] = norm_back_rows(1)
    scatter.last(*[n for n in of_group(turn_order[0]) if n])

    def act_block(r):
        def block(slot):
            return dot(big[r * length + slot * size : r * length + (slot + 1) * size, :], down[...])

        return block

    for r in range(2):
        fold.away(act_block(r))
        fold.kept(act_block(r), mixed.at[r], r == 0, far_out=mixed_far.at[r])
        spread[r].forward()
        if r == 0:
            scatter.middle(*[n for g in turn_order[1:] for n in of_group(g)])

    loading = load_big(dup)
    stream_two = Stream(copies, [narrow_slots], columns_of(full2))
    stage_up = [down.at[pl.ds(n * depth, depth), pl.ds(0, hidden)] for n in range(2)]
    loading.wait()
    put_up = {}
    done = 0
    for g in turn_order:
        for d in range(shares):
            at = stream_two.take(done)
            if done >= 2:
                put_up.pop(done - 2).wait()
            stage_up[done % 2][...] = dot(
                narrow[at], big[: 2 * length, g * hidden : (g + 1) * hidden], ((0,), (0,))
            ).astype(BF16)
            put_up[done] = load(stage_up[done % 2], up_parts.at[g * shares + d])
            done += 1
    for copy in put_up.values():
        copy.wait()
    spread[0].finish()
    spread[1].finish()
    scatter.last(*[n for g in turn_order for n in of_group(g) if (n, "t") not in scatter.steps])
    scatter.total()
    fold.finish()
    copies.finish()


def attention_back_rows(places, row, length, size, heads, per, segment, refs, column, pump=None):
    (
        proj, prefix_proj, att, datt, lse, dproj, dprefix,
        k_own, v_own, dk_own, dv_own, dk_pre, dv_pre,
    ) = refs
    scale = HDIM**-0.5 * LOG2E
    factor = HDIM**-0.5
    at = row_blocks(2 * places.h + places.c, 4, size)
    base = row * length

    def head(n, _):
        q_at, k_at, v_at = (pl.ds(column(n, 3, m), HDIM) for m in range(3))
        kp_at, vp_at = (pl.ds(column(n, 2, m), HDIM) for m in range(2))
        out_at = pl.ds(pl.multiple_of(n * HDIM, HDIM), HDIM)
        for j in range(4):
            there = pl.ds(base + at[j], size)
            k_own[j * size : (j + 1) * size] = proj[there, k_at]
            v_own[j * size : (j + 1) * size] = proj[there, v_at]
        dk_own[...] = jnp.zeros_like(dk_own)
        dv_own[...] = jnp.zeros_like(dv_own)
        if segment is None:
            dk_pre[...] = jnp.zeros_like(dk_pre)
            dv_pre[...] = jnp.zeros_like(dv_pre)

        def run(before):
            for j in range(4):
                there = pl.ds(base + at[j], size)
                q = proj[there, q_at]
                do = datt[there, out_at]
                product = do.astype(F32) * att[there, out_at].astype(F32)
                delta = lax.dot_general(
                    jnp.ones((8, HDIM), F32),
                    product,
                    (((1,), (1,)), ((), ())),
                    precision=lax.Precision.HIGHEST,
                    preferred_element_type=F32,
                )[:1]
                log_total = lse[row * heads + n, :, j * size : (j + 1) * size]
                start, end = first_key(j, size, segment), j * size
                parts = []
                step = min(512, length)
                for m in range(0, before * length, step):
                    rows = slice(m, m + step)
                    parts.append(
                        (prefix_proj[rows, kp_at], prefix_proj[rows, vp_at], dk_pre, dv_pre, rows, None)
                    )
                if end > start:
                    rows = slice(start, end)
                    parts.append((k_own[rows], v_own[rows], dk_own, dv_own, rows, None))
                rows = slice(end, end + size)
                parts.append((k_own[rows], v_own[rows], dk_own, dv_own, rows, causal(size)))
                dq = jnp.zeros((HDIM, size), F32)
                for k, v, dk, dv, rows, mask in parts:
                    s = dot(k, q, ((1,), (1,))) * scale - log_total
                    p = jnp.exp2(s if mask is None else jnp.where(mask, s, MASKED))
                    dscores = (p * (dot(v, do, ((1,), (1,))) - delta)).astype(BF16)
                    dv[rows] += dot(p.astype(BF16), do)
                    dk[rows] += dot(dscores, q)
                    dq = dq + dot(k, dscores, ((0,), (0,)))
                dproj[there, q_at] = (dq * factor).T.astype(BF16)

        if segment is not None:
            run(0)
        else:
            for m in range(places.groups):
                pl.when(places.g == m)(functools.partial(run, m))
            dprefix[:, q_at] = jnp.zeros_like(dk_pre, dtype=BF16)
            dprefix[:, k_at] = (dk_pre[...] * factor).astype(BF16)
            dprefix[:, v_at] = dv_pre[...].astype(BF16)
        for j in range(4):
            rows = slice(j * size, (j + 1) * size)
            there = pl.ds(base + at[j], size)
            dproj[there, k_at] = (dk_own[rows] * factor).astype(BF16)
            dproj[there, v_at] = dv_own[rows].astype(BF16)
        if pump is not None:
            pl.when(n == heads // 2 - 1)(pump)
        return 0

    lax.fori_loop(0, heads, head, 0)


def last_kernel(extra, groups, quarter, *refs):
    (
        proj_in, prefix_in, att_in, full_dres, out_all, in_all, full1, prefix1, up_parts, mixed_far, rows_in,
        lse, wide_ref, sums2, up_sums,
        grad_in, grad_out, grad_up, dnormed1, all_sums, bias_sums, mixed_recv,
        in_parts, out_parts, land_in, turned_in, land_out, turned_out, land_up, turned_up,
        proj, prefix_proj, att, datt, dprefix, w_in, w_out, spare,
        k_own, v_own, dk_own, dv_own, dk_pre, dv_pre,
        c_send, c_recv, h_send, h_recv, back, returned, dproj_sums, sum_send, sum_recv, bias_send, bias_recv,
        bias_out, bias_turn, stage_in, stage_out,
        work_in, own_in, work_out, own_out, work_up, own_up, fetched, send_sem, recv_sem, near_sem, free,
    ) = refs
    size, width = dnormed1.shape[1:]
    length = 4 * size
    cols = grad_in.shape[1] // 3
    depth = grad_in.shape[0]
    wide = 3 * cols
    heads = groups * cols // HDIM
    per = cols // HDIM
    shares = extra * 4
    places = Places(extra, groups)
    copies = Copies(send_sem, recv_sem, near_sem)
    sources = len(places.offsets)
    far_first = list(range(sources))[::-1]
    up = GradScatter(
        copies, places, up_parts, land_up, turned_up, work_up, own_up, fetched, grad_up
    )
    out = GradScatter(
        copies, places, out_parts, land_out, turned_out, work_out, own_out, fetched, grad_out
    )
    into = GradScatter(
        copies, places, in_parts, land_in, turned_in, work_in, own_in, fetched, grad_in
    )
    dproj = proj
    folds = Fold(copies, places, c_send, c_recv, [h_send.at[0], h_send.at[1]], free, size)
    folded = {}

    def column(n, parts, m):
        return pl.multiple_of((n // per * parts + m) * cols + lax.rem(n, per) * HDIM, HDIM)

    here = [
        copies.local(s, t, tracked=False)
        for s, t in (
            (out_all, w_out), (proj_in, proj), (prefix_in, prefix_proj), (att_in, att), (in_all, w_in),
        )
    ]
    order = [(r, slot) for r in range(2) for slot in range(4)]
    tiles = [c_send.at[pl.ds(n * size, size), :] for n in range(2)]
    stream = Stream(
        copies, [tiles], [[full_dres.at[pl.ds(r * length + s * size, size), :]] for r, s in order]
    )
    places.barrier()
    for n in far_first:
        up.start(n)
    mixed_steps = [
        copies.remote(mixed_far.at[r], mixed_recv.at[r], places.to_h) for r in range(2)
    ]
    here[0].wait()

    def attended_grad(r):
        for slot in range(4):
            at = stream.take(r * 4 + slot)
            datt[r * length + slot * size : r * length + (slot + 1) * size, :] = dot(
                tiles[at][...], w_out[...], ((1,), (1,))
            ).astype(BF16)

    def attention_back(r, segment, pump=None):
        attention_back_rows(
            places, r, length, size, heads, per, segment,
            (
                proj, prefix_proj, att, datt, lse, dproj, dprefix,
                k_own, v_own, dk_own, dv_own, dk_pre, dv_pre,
            ),
            column,
            pump,
        )

    def block_of(source, row):
        def block(slot):
            rows = source[row + slot * size : row + (slot + 1) * size, :]
            return dot(rows, w_in[...], ((1,), (1,)))

        return block

    def fold(number, source, row, target, more=True):
        folds.away(block_of(source, row))
        folded[number] = folds.kept(block_of(source, row), target, more, h_recv.at[number])

    attended_grad(0)
    attended_grad(1)
    for copy in here[1:]:
        copy.wait()
    attention_back(0, None, lambda: up.middle(*far_first))
    up.last(*far_first[:-1])
    for k in range(1, groups):
        fold(1 + k, dprefix, (k - 1) * length, back.at[k - 1])
    attention_back(1, quarter)

    home = []
    for k in range(1, groups):
        folded[1 + k].wait_recv()
        back[k - 1] = (back[k - 1].astype(F32) + h_recv[1 + k].astype(F32)).astype(BF16)
        copy = copies.remote(
            back.at[k - 1], returned.at[k - 1], places.further((0, -k)), tracked=False
        )
        pl.when(places.g >= k)(copy.start)
        home.append(copy)

    slots = [datt.at[:, pl.ds(0, depth)], spare]
    prefix_rows = prefix1.shape[0]
    slots_pre = [prefix_proj.at[:, pl.ds(n * depth, depth)] for n in range(2)]

    def share_of(n, i, j):
        return places.share(places.offsets[n], i, j)

    class Columns:
        def __init__(self, pairs, shares_at):
            self.pairs, self.shares_at, self.loads = pairs, shares_at, {}
            self._load(0)

        def _load(self, n):
            if n < len(self.shares_at):
                at = pl.ds(pl.multiple_of(self.shares_at[n] * depth, depth), depth)
                self.loads[n] = [
                    copies.local(s.at[:, at], slot[n % 2], tracked=False) for s, slot in self.pairs
                ]

        def take(self, n):
            for load in self.loads[n]:
                load.wait()
            self._load(n + 1)
            return n % 2

    groups_first = [
        n for g in range(groups)[::-1] for n in far_first if places.offsets[n][1] == g
    ]
    wanted = [(n, i, j) for n in groups_first for i, j in GradScatter.ORDER]
    stream_in = Columns([(full1, slots), (prefix1, slots_pre)], [share_of(*w) for w in wanted])
    put = {}

    def settle(scatter, todo, number):
        if number in put:
            put.pop(number).wait()
            scatter.send(*todo[number])

    def in_pieces(numbers):
        for number in numbers:
            n, i, j = wanted[number]
            at = stream_in.take(number)
            which = pl.ds(places.offsets[n][1] * wide, wide)
            value = dot(slots[at][...], dproj[:, which], ((0,), (0,)))
            if prefix_rows:
                value = value + dot(slots_pre[at][...], dprefix[:, which], ((0,), (0,)))
            stage_in[number % 2] = value.astype(BF16)
            put[number] = copies.local(
                stage_in.at[number % 2], in_parts.at[into.index(n, i, j)], tracked=False
            )
            settle(into, wanted, number - 1)
        settle(into, wanted, numbers[-1])

    hidden = up_parts.shape[2]
    far_ones = [n for n in far_first if places.offsets[n][1] == groups - 1]
    near_ones = [n for n in far_first if places.offsets[n][1] != groups - 1]
    in_pieces(range(4 * len(far_ones)))
    fold(0, dproj, 0, dnormed1.at[0])
    into.middle(*far_ones)
    if near_ones:
        in_pieces(range(4 * len(far_ones), len(wanted)))
    into.last(*[n for n in far_ones if n])
    fold(1, dproj, length, dnormed1.at[1], False)
    todo = [(n, i, j) for i, j in GradScatter.ORDER for n in groups_first]
    stream_out = Columns([(full_dres, slots)], [share_of(*w) for w in todo])
    put.clear()
    for number, (n, i, j) in enumerate(todo):
        at = stream_out.take(number)
        first = places.offsets[n][1] * cols
        stage_out[number % 2] = dot(
            att[:, first : first + cols], slots[at][...], ((0,), (0,))
        ).astype(BF16)
        put[number] = copies.local(
            stage_out.at[number % 2], out_parts.at[out.index(n, i, j)], tracked=False
        )
        settle(out, todo, number - 1)
    settle(out, todo, len(todo) - 1)
    folds.finish()
    here = [
        copies.local(rows_in, c_send, tracked=False),
        copies.local(
            full_dres.at[pl.ds(0, size), :], c_recv.at[pl.ds(0, size), :], tracked=False
        ),
        copies.local(
            full_dres.at[pl.ds(length, size), :], c_recv.at[pl.ds(size, size), :], tracked=False
        ),
    ]
    into.middle(*near_ones)
    into.last(*[n for n in near_ones if n])
    dproj_sums[...] = jnp.zeros_like(dproj_sums)

    def add_rows(t):
        dproj_sums[0:1, :] += jnp.sum(dproj[pl.ds(t, size), :].astype(F32), axis=0, keepdims=True)

    in_tiles(2 * length, size, add_rows)

    def add_prefix(t):
        dproj_sums[1:2, :] += jnp.sum(dprefix[pl.ds(t, size), :].astype(F32), axis=0, keepdims=True)

    in_tiles(prefix_rows, size, add_prefix)
    bias_send[...] = jnp.zeros_like(bias_send)
    for g in range(groups):
        base = g * wide
        bias_send[g, 0:1, :cols] = dproj_sums[0:1, base : base + cols]
        bias_send[g, 0:1, cols : 2 * cols] = (
            dproj_sums[0:1, base + 2 * cols : base + wide] + dproj_sums[1:2, base + 2 * cols : base + wide]
        )
        bias_send[g, 0:1, 2 * cols :] = up_sums[0:1, g * hidden : (g + 1) * hidden]
    bias_steps = [
        copies.remote(bias_send.at[g], bias_turn.at[g - 1], places.further((0, -g)))
        for g in range(1, groups)
    ]
    out.middle(*far_first)
    up.last(0)

    all_sums[...] = jnp.zeros_like(all_sums)
    all_sums[0:4, :] = sums2[...]
    chunk = min(64, size)
    for copy in here:
        copy.wait()
    for r in (1, 0):
        if r == 0:
            out.last(*far_first[:-1])
            for k in range(1, groups):

                @pl.when(places.g + k < groups)
                def _():
                    home[k - 1].wait_recv()
                    dnormed1[0] = (
                        dnormed1[0].astype(F32) + returned[k - 1].astype(F32)
                    ).astype(BF16)

                pl.when(places.g >= k)(home[k - 1].wait_send)
        folded[r].wait_recv()

        def norm_rows(t):
            at = pl.ds(t, chunk)
            grad = dnormed1[r, at, :].astype(F32) + h_recv[r, at, :].astype(F32)
            scaled, inverse = stats(c_send[pl.ds(r * size + t, chunk), :].astype(F32))
            value = c_recv[pl.ds(r * size + t, chunk), :].astype(F32) + norm_back(
                grad, scaled, inverse, wide_ref[0:1]
            )
            dnormed1[r, at, :] = value.astype(BF16)
            all_sums[4:5, :] += jnp.sum(grad * scaled, axis=0, keepdims=True)
            all_sums[5:6, :] += jnp.sum(grad, axis=0, keepdims=True)

        in_tiles(size, chunk, norm_rows)

    for copy in bias_steps:
        copy.wait_recv()
    bias_sums[...] = functools.reduce(
        jnp.add, [bias_send[0]] + [bias_turn[g - 1] for g in range(1, groups)]
    )
    waiting = [up.total, lambda: into.last(0), lambda: out.last(0)]
    stages = [("c", 2), ("h", 2), ("g", groups), ("b", 2), ("a", 2), ("e", extra)]
    for number, (axis, count) in enumerate(stages):
        if count == 1:
            continue
        pairs = [(all_sums, sum_send.at[number], sum_recv.at[number])]
        if axis in DP:
            pairs.append((bias_sums, bias_out.at[number], bias_recv.at[number]))
        me = lax.axis_index(axis)
        steps = []
        for values, sending, coming in pairs:
            sending[...] = values[...]
            for k in range(1, count):
                partner = {axis: lax.rem(me + k, count)}
                steps.append(copies.remote(sending, coming.at[k - 1], partner))
        if waiting:
            waiting.pop(0)()
        for copy in steps:
            copy.wait_recv()
        for values, sending, coming in pairs:
            if count == 2:
                values[...] = sending[...] + coming[0]
            else:
                total = jnp.zeros(values.shape, F32)
                for device in range(count):
                    back_by = lax.rem(me - device + count, count)
                    other = coming[jnp.maximum(back_by - 1, 0)]
                    total = total + jnp.where(back_by == 0, sending[...], other)
                values[...] = total
    for job in waiting:
        job()
    for copy in mixed_steps:
        copy.wait_recv()
    out.total()
    into.total()
    copies.finish()


def kernel_params(number):
    return pltpu.CompilerParams(
        collective_id=number, has_side_effects=True, vmem_limit_bytes=KERNEL_VMEM
    )


def run_middle(split, full2, cots, up_all, down_all, resid, wide, bias_up, hidden, depth):
    extra, groups = split
    sources = extra * groups
    size, width = resid.shape[1:]
    length = 4 * size
    all_hidden = groups * hidden
    shape = jax.ShapeDtypeStruct
    anywhere = pl.BlockSpec(memory_space=pl.ANY)
    inside = pl.BlockSpec(memory_space=pltpu.VMEM)
    shares = sources * 4
    return pl.pallas_call(
        functools.partial(middle_kernel, extra, groups),
        in_specs=[anywhere] * 4 + [inside] * 3,
        out_specs=[inside, anywhere, inside, anywhere, inside, inside] + [anywhere] * 7,
        out_shape=[
            shape((2, size, width), BF16),
            shape((2 * length, width), BF16),
            shape((hidden, depth), F32),
            shape((shares, depth, hidden), BF16),
            shape((4, width), F32),
            shape((1, all_hidden), F32),
            shape((2, size, width), BF16),
            shape((2 * length, width), BF16),
            shape((2 * length, all_hidden), BF16),
            shape((2 * length, all_hidden), BF16),
            shape((shares, hidden, depth), BF16),
        ]
        + GradScatter.landing(sources, hidden, depth),
        scratch_shapes=[
            pltpu.VMEM((max(width, 2 * length), all_hidden), BF16),
            pltpu.VMEM((all_hidden, width), BF16),
            pltpu.VMEM((2, 2 * length, depth), BF16),
            pltpu.VMEM((2, size, width), BF16),
            pltpu.VMEM((2, size, width), BF16),
            pltpu.VMEM((2 * size, width), BF16),
            pltpu.VMEM((2 * size, width), BF16),
            pltpu.VMEM((2, size, width), BF16),
            pltpu.VMEM((2, size, width), BF16),
            pltpu.VMEM((2, size, width), BF16),
            pltpu.VMEM((2, hidden, depth), BF16),
        ]
        + GradScatter.working(sources, hidden, depth)
        + [
            pltpu.VMEM((2, 3, hidden // 2, depth), BF16),
            pltpu.SemaphoreType.DMA((sources * 8 + 16,)),
            pltpu.SemaphoreType.DMA((sources * 8 + 16,)),
            pltpu.SemaphoreType.DMA((sources * 16 + 6 * shares + 80,)),
            pltpu.SemaphoreType.REGULAR,
        ],
        compiler_params=kernel_params(1),
        cost_estimate=pl.CostEstimate(flops=10**11, bytes_accessed=10**8, transcendentals=10**6),
    )(full2, cots, up_all, down_all, resid, wide, bias_up)


def run_last(split, quarter, proj, prefix_proj, att, full_dres, out_all, in_all, full1, prefix1, up_parts, mixed_far, rows, lse, norms, sums2, up_sums):
    extra, groups = split
    sources = extra * groups
    shares = sources * 4
    length, width = full1.shape[0] // 2, full1.shape[1]
    size = length // 4
    cols = att.shape[1] // groups
    depth, hidden = up_parts.shape[1:]
    wide, all_wide = 3 * cols, 3 * cols * groups
    prefix_rows = prefix1.shape[0]
    most = max(extra, groups, 2) - 1
    shape = jax.ShapeDtypeStruct
    anywhere = pl.BlockSpec(memory_space=pl.ANY)
    inside = pl.BlockSpec(memory_space=pltpu.VMEM)
    heads_rows = [pltpu.VMEM((length, HDIM), BF16)] * 2 + [pltpu.VMEM((length, HDIM), F32)] * 2
    return pl.pallas_call(
        functools.partial(last_kernel, extra, groups, quarter),
        in_specs=[anywhere] * 11 + [inside] * 4,
        out_specs=[inside] * 6 + [anywhere] * 9,
        out_shape=[
            shape((depth, wide), F32),
            shape((cols, depth), F32),
            shape((depth, hidden), F32),
            shape((2, size, width), BF16),
            shape((8, width), F32),
            shape((8, 2 * cols + hidden), F32),
            shape((2, size, width), BF16),
            shape((shares, depth, wide), BF16),
            shape((shares, cols, depth), BF16),
        ]
        + GradScatter.landing(sources, depth, wide)
        + GradScatter.landing(sources, cols, depth)
        + GradScatter.landing(sources, depth, hidden),
        scratch_shapes=[
            pltpu.VMEM(proj.shape, BF16),
            pltpu.VMEM(prefix_proj.shape, BF16),
            pltpu.VMEM(att.shape, BF16),
            pltpu.VMEM(att.shape, BF16),
            pltpu.VMEM((prefix_rows, all_wide), BF16),
            pltpu.VMEM(in_all.shape, BF16),
            pltpu.VMEM(out_all.shape, BF16),
            pltpu.VMEM((2 * length, depth), BF16),
        ]
        + heads_rows
        + [pltpu.VMEM((prefix_rows, HDIM), F32)] * 2
        + [
            pltpu.VMEM((2 * size, width), BF16),
            pltpu.VMEM((2 * size, width), BF16),
            pltpu.VMEM((2, size, width), BF16),
            pltpu.VMEM((1 + groups, size, width), BF16),
            pltpu.VMEM((max(groups - 1, 1), size, width), BF16),
            pltpu.VMEM((max(groups - 1, 1), size, width), BF16),
            pltpu.VMEM((2, all_wide), F32),
            pltpu.VMEM((6, 8, width), F32),
            pltpu.VMEM((6, most, 8, width), F32),
            pltpu.VMEM((groups, 8, 2 * cols + hidden), F32),
            pltpu.VMEM((6, most, 8, 2 * cols + hidden), F32),
            pltpu.VMEM((6, 8, 2 * cols + hidden), F32),
            pltpu.VMEM((max(groups - 1, 1), 8, 2 * cols + hidden), F32),
            pltpu.VMEM((2, depth, wide), BF16),
            pltpu.VMEM((2, cols, depth), BF16),
        ]
        + GradScatter.working(sources, depth, wide)
        + GradScatter.working(sources, cols, depth)
        + GradScatter.working(sources, depth, hidden)
        + [
            pltpu.VMEM((2, 3, depth // 2, max(wide, hidden, depth)), BF16),
            pltpu.SemaphoreType.DMA((sources * 24 + 12 * groups + 48,)),
            pltpu.SemaphoreType.DMA((sources * 24 + 12 * groups + 48,)),
            pltpu.SemaphoreType.DMA((sources * 48 + 10 * shares + 32,)),
            pltpu.SemaphoreType.REGULAR,
        ],
        compiler_params=kernel_params(2),
        cost_estimate=pl.CostEstimate(flops=10**11, bytes_accessed=10**8, transcendentals=10**7),
    )(proj, prefix_proj, att, full_dres, out_all, in_all, full1, prefix1, up_parts, mixed_far, rows, lse, norms, sums2, up_sums)


def local(
    tokens,
    segments,
    first_gain,
    first_shift,
    in_weight,
    in_bias,
    out_weight,
    out_bias,
    second_gain,
    second_shift,
    up_weight,
    up_bias,
    down_weight,
    down_bias,
    cotangent,
):
    extra, groups = lax.axis_size("e"), lax.axis_size("g")
    split = (extra, groups)
    size, width = tokens.shape[1:]
    cols, hidden, depth = in_weight.shape[2], up_weight.shape[1], in_weight.shape[0]
    quarter = segments.shape[1] // 4

    single = jnp.where(segments[0, -1] == 0, 0, 1)
    order = (single, 1 - single)

    def pick(x):
        return [lax.dynamic_index_in_dim(x, r, 0, keepdims=False) for r in order]

    def unpick(first, second):
        return jnp.where(single == 0, jnp.stack([first, second]), jnp.stack([second, first]))

    picked = jnp.stack(pick(tokens))
    cots = pick(cotangent)

    no_bias = jnp.zeros_like(in_bias[0])
    biases = jnp.concatenate([in_bias[0], no_bias, in_bias[1], up_bias])
    biases = jnp.broadcast_to(biases, (8, biases.shape[0]))
    wide = jnp.stack([first_gain, first_shift, out_bias, second_gain, second_shift, down_bias])
    (
        in_all, out_all, up_all, down_all, biases, full1, prefix1, proj, proj_prefix, attended, lse,
        resid, full2,
    ) = run_forward(
        split,
        quarter,
        picked,
        in_weight.reshape(depth, 3 * cols),
        out_weight,
        up_weight,
        down_weight,
        wide,
        biases,
    )
    bias_up = biases[:, 0, 3 * cols :].reshape(1, -1)
    length = 4 * size

    mixed, full_dres, grad_down, up_parts, sums2, up_sums, mixed_far = run_middle(
        split, full2, jnp.stack(cots), up_all, down_all, resid, wide, bias_up, hidden, depth
    )[:7]
    grad_in, grad_out, grad_up, tokens_grad, all_sums, bias_sums, mixed_recv = run_last(
        split, quarter, proj, proj_prefix, attended, full_dres, out_all, in_all, full1, prefix1, up_parts,
        mixed_far, picked.reshape(2 * size, width), lse, wide, sums2, up_sums,
    )[:7]
    mixed = (resid + mixed.astype(F32) + mixed_recv.astype(F32) + down_bias).astype(BF16)
    return (
        unpick(*mixed),
        unpick(*tokens_grad),
        all_sums[4],
        all_sums[5],
        grad_in.reshape(in_weight.shape),
        bias_sums[0, : 2 * cols].reshape(2, cols),
        grad_out,
        all_sums[0],
        all_sums[1],
        all_sums[2],
        grad_up,
        bias_sums[0, 2 * cols :],
        grad_down,
        all_sums[3],
    )


def solution(mesh):
    dp, tp = mesh.shape["dp"], mesh.shape["tp"]
    split = Mesh(mesh.devices.reshape(dp // 4, 2, 2, tp // 4, 2, 2), DP + TP)
    in_specs = (
        P(DP, TP, None),
        P(DP, None),
        P(),
        P(),
        P(DP, None, TP),
        P(None, TP),
        P(TP, DP),
        P(),
        P(),
        P(),
        P(DP, TP),
        P(TP),
        P(TP, DP),
        P(),
        P(DP, TP, None),
    )
    out_specs = (
        P(DP, TP, None),
        P(DP, TP, None),
        P(),
        P(),
        P(DP, None, TP),
        P(None, TP),
        P(TP, DP),
        P(),
        P(),
        P(),
        P(DP, TP),
        P(TP),
        P(TP, DP),
        P(),
    )
    return jax.shard_map(local, mesh=split, in_specs=in_specs, out_specs=out_specs, check_vma=False)
```
